128 devices in a mesh: dp: 4 (over x_lo, core), tensor: 4 (over y), ctx: 8 (over x_hi, z).
Axes of the slice: x: 4 (x_hi: 2, x_lo: 2; x = x_hi * 2 + x_lo), y: 4, z: 4, core: 2. Of those that a mesh axis runs over, the one named last changes fastest.
Arguments:
- tokens: bfloat16 [4, 4096, 768], P('dp', 'ctx'), may hold values from -6 to 6
- norm_gain: bfloat16 [2, 768], P(None, ('dp', 'ctx')), may hold values from 0.099609375 to 1.8984375
- norm_bias: bfloat16 [2, 768], P(None, ('dp', 'ctx')), may hold values from -1.5 to 1.5
- qkv_weight: bfloat16 [768, 3, 768], P(('dp', 'ctx'), None, 'tensor'), may hold values from -0.21875 to 0.21875
- qkv_bias: bfloat16 [3, 12, 64], P(None, 'tensor', ('dp', 'ctx')), may hold values from -2.5 to 2.5
- dense_weight: bfloat16 [768, 768], P('tensor', ('dp', 'ctx')), may hold values from -3 to 3
- fc1_weight: bfloat16 [768, 3072], P(('dp', 'ctx'), 'tensor'), may hold values from -0.21875 to 0.21875
- fc1_bias: bfloat16 [48, 64], P('tensor', ('dp', 'ctx')), may hold values from -2.5 to 2.5
- fc2_weight: bfloat16 [3072, 768], P('tensor', ('dp', 'ctx')), may hold values from -0.109375 to 0.109375
- out_bias: bfloat16 [2, 768], P(None, ('dp', 'ctx')), may hold values from -1.5 to 1.5
- cotangent: bfloat16 [4, 4096, 768], P('dp', 'ctx', 'tensor'), may hold values from -6 to 6
Outputs:
- output: bfloat16 [4, 4096, 768], P('dp', 'ctx', 'tensor')
- input_grad: float32 [4, 4096, 768], P('dp', 'ctx', 'tensor')
- grad_norm_gain: float32 [2, 768], P(None, ('dp', 'ctx'))
- grad_norm_bias: float32 [2, 768], P(None, ('dp', 'ctx'))
- grad_qkv_weight: float32 [768, 3, 768], P(('dp', 'ctx'), None, 'tensor')
- grad_qkv_bias: float32 [3, 12, 64], P(None, 'tensor', ('dp', 'ctx'))
- grad_dense_weight: float32 [768, 768], P('tensor', ('dp', 'ctx'))
- grad_fc1_weight: float32 [768, 3072], P(('dp', 'ctx'), 'tensor')
- grad_fc1_bias: float32 [48, 64], P('tensor', ('dp', 'ctx'))
- grad_fc2_weight: float32 [3072, 768], P('tensor', ('dp', 'ctx'))
- grad_out_bias: float32 [2, 768], P(None, ('dp', 'ctx'))
The draws below stay inside these ranges and needn't reach their ends.
All inputs are finite; a program needn't handle non-finite values.
Results may differ from the reference program's by a relative error of at most 0.023.
Values may be sent and summed in bfloat16 or wider, within the bound.
A program may use at most 64 MiB of HBM per device.

```python
import jax
import jax.numpy as jnp
from jax import lax

D = 768
HEADS = 12
HD = 64
FF = 3072
ROT = 16
LENGTH = 4096
BATCH = 4


def block_scale(rng, extent, shards, least, largest):
    gain = 1.0
    for axis_at, parts in shards:
        heights = jax.random.uniform(jax.random.fold_in(jax.random.fold_in(rng, 6), axis_at), (parts,), jnp.float32, least / len(shards), largest / len(shards))
        gain = gain * jnp.repeat(jnp.exp(heights), extent[axis_at] // parts).reshape((-1,) + (1,) * (len(extent) - 1 - axis_at))
    return gain


def gaussian(own_key, shape, deviation, limit, cuts=(), held_as=jnp.bfloat16):
    values = deviation * jax.random.normal(own_key, shape, jnp.float32)
    if cuts:
        values = values * block_scale(own_key, shape, cuts, -0.22, 0.18)
    return jnp.clip(values, -limit, limit).astype(held_as)


def setup_inputs(seed: int = 0) -> dict:
    arg_keys = jax.random.split(jax.random.key(seed), 12)
    return {
        "tokens": gaussian(arg_keys[0], (BATCH, LENGTH, D), 1.0, 6.0, ((0, 4), (1, 8))),
        "norm_gain": jnp.clip(1.0 + 0.18 * jax.random.normal(arg_keys[1], (2, D), jnp.float32), 0.099609375, 1.8984375).astype(jnp.bfloat16),
        "norm_bias": gaussian(arg_keys[2], (2, D), 0.3, 1.5, ((1, 32),)),
        "qkv_weight": gaussian(arg_keys[3], (D, 3, D), D ** -0.5, 0.21875, ((0, 32), (2, 4))),
        "qkv_bias": gaussian(arg_keys[4], (3, HEADS, HD), 0.5, 2.5, ((1, 4), (2, 32))),
        "dense_weight": gaussian(arg_keys[5], (D, D), 4 ** -0.5, 3.0, ((0, 4), (1, 32))),
        "fc1_weight": gaussian(arg_keys[6], (D, FF), D ** -0.5, 0.21875, ((0, 32), (1, 4))),
        "fc1_bias": gaussian(arg_keys[7], (FF // 64, 64), 0.5, 2.5, ((0, 4), (1, 32))),
        "fc2_weight": gaussian(arg_keys[8], (FF, D), FF ** -0.5, 0.109375, ((0, 4), (1, 32))),
        "out_bias": gaussian(arg_keys[9], (2, D), 0.3, 1.5, ((1, 32),)),
        "cotangent": gaussian(arg_keys[10], (BATCH, LENGTH, D), 1.0, 6.0, ((0, 4), (1, 8), (2, 4))),
    }


@jax.custom_vjp
def low(v):
    return lax.optimization_barrier(v.astype(jnp.bfloat16)).astype(jnp.float32)

@jax.custom_vjp
def low_back(v):
    return v

def low_keep(v):
    return (low(v), None)

def low_pass(kept, grad):
    return (grad,)

def back_keep(v):
    return (v, None)

def back_low(kept, grad):
    return (low(grad),)
low.defvjp(low_keep, low_pass)
low_back.defvjp(back_keep, back_low)
EPSILON = 1e-05
PRECISE = lax.Precision.HIGHEST

def norm_rows(values_in, gain_row, shift_row):
    row_mean = lax.optimization_barrier(jnp.mean(values_in, axis=-1, keepdims=True))
    centred = values_in - row_mean
    variance = lax.optimization_barrier(jnp.mean(centred * centred, axis=-1, keepdims=True))
    return centred * lax.rsqrt(variance + EPSILON) * gain_row + shift_row

def angles(positions):
    frequency = 10000.0 ** (-2.0 * jnp.arange(ROT // 2, dtype=jnp.float32) / ROT)
    phases = positions.astype(jnp.float32)[:, None] * frequency[None, :]
    return (jnp.cos(phases)[:, None, :], jnp.sin(phases)[:, None, :])

def rotate(tensor_in, cosine, sine_table):
    half_rot = ROT // 2
    lower = tensor_in[..., :half_rot]
    upper = tensor_in[..., half_rot:ROT]
    return jnp.concatenate([lower * cosine - upper * sine_table, upper * cosine + lower * sine_table, tensor_in[..., ROT:]], axis=-1)

def one_sequence(seq_rows, norm_gain, norm_bias, qkv_weight, qkv_bias, dense_weight, fc1_weight, fc1_bias, fc2_weight, out_bias):
    length = seq_rows.shape[0]
    norm_one = low(norm_rows(seq_rows, norm_gain[0], norm_bias[0]))
    norm_two = low(norm_rows(seq_rows, norm_gain[1], norm_bias[1]))
    projected = jnp.einsum('td,dce->tce', norm_one, qkv_weight, precision=PRECISE) + qkv_bias.reshape(3, D)
    projected = low_back(projected)
    cosine, sine_table = angles(jnp.arange(length))
    queries = low(rotate(projected[:, 0].reshape(length, HEADS, HD), cosine, sine_table))
    key_rows = low(rotate(projected[:, 1].reshape(length, HEADS, HD), cosine, sine_table))
    value_rows = low(projected[:, 2].reshape(length, HEADS, HD))
    scores = jnp.einsum('qhe,khe->hqk', queries, key_rows, precision=PRECISE) * HD ** (-0.5)
    scores = low_back(scores)
    causal = jnp.arange(length)[:, None] >= jnp.arange(length)[None, :]
    scores = jnp.where(causal[None], scores, -1e+30)
    attn_probs = jax.nn.softmax(scores, axis=-1)
    probs_rounded = low(attn_probs)
    heads_out = jnp.einsum('hqk,khe->qhe', probs_rounded, value_rows, precision=PRECISE).reshape(length, D)
    heads_out = low(low_back(heads_out))
    attended = jnp.dot(heads_out, dense_weight, precision=PRECISE)
    hidden = low_back(jnp.dot(norm_two, fc1_weight, precision=PRECISE) + fc1_bias.reshape(FF))
    active = low(jax.nn.gelu(hidden, approximate=False))
    mlp_out = jnp.dot(active, fc2_weight, precision=PRECISE)
    return seq_rows + attended + mlp_out + out_bias[0] + out_bias[1]

def forward(tokens_in, norm_gain, norm_bias, qkv_weight, qkv_bias, dense_weight, fc1_weight, fc1_bias, fc2_weight, out_bias):

    def per_sequence(seq_rows):
        return one_sequence(seq_rows, norm_gain, norm_bias, qkv_weight, qkv_bias, dense_weight, fc1_weight, fc1_bias, fc2_weight, out_bias)
    return lax.map(jax.checkpoint(per_sequence), tokens_in)

def reference(tokens, norm_gain, norm_bias, qkv_weight, qkv_bias, dense_weight, fc1_weight, fc1_bias, fc2_weight, out_bias, cotangent):
    inputs = [tokens, norm_gain, norm_bias, qkv_weight, qkv_bias, dense_weight, fc1_weight, fc1_bias, fc2_weight, out_bias]
    inputs = [item.astype(jnp.float32) for item in inputs]
    result, pullback = jax.vjp(forward, *inputs)
    gradients = pullback(cotangent.astype(jnp.float32))
    return (result.astype(jnp.bfloat16), gradients[0], gradients[1], gradients[2], gradients[3], gradients[4], gradients[5], gradients[6], gradients[7], gradients[8], gradients[9])
```

```python
import jax
import jax.numpy as jnp
import numpy as np
from jax import lax
from jax.experimental import pallas as pl
from jax.experimental.pallas import tpu as pltpu
from jax.sharding import PartitionSpec as P

HD = 64
ROT = 16
EPSILON = 1e-05
ROWS = 512
WIDE = 768
HALF = 1280
PART = 192
TILE = 128
MESH = pl.DeviceIdType.MESH
VMEM_LIMIT = 60 << 20
F32 = jnp.float32
BF16 = jnp.bfloat16

QKV = slice(0, 640)
DENSE = slice(640, 896)
FC1 = slice(896, 1664)
FC2 = slice(1664, 2432)


def dot(a, b):
    return lax.dot_general(a, b, (((1,), (0,)), ((), ())), preferred_element_type=F32)


def dot_nt(a, b):
    return lax.dot_general(a, b, (((1,), (1,)), ((), ())), preferred_element_type=F32)


def dot_tn(a, b):
    return lax.dot_general(a, b, (((0,), (0,)), ((), ())), preferred_element_type=F32)


def place():
    dp = lax.axis_index("dp")
    cx = lax.axis_index("ctx")
    return dp // 2, dp % 2, cx // 4, cx % 4, lax.axis_index("tensor")


def device(x, y, z, core):
    return {"dp": (x % 2) * 2 + core, "ctx": (x // 2) * 4 + z, "tensor": y}


class Links:
    def __init__(self, send, recv):
        self.xlo, self.core, self.xhi, self.z, self.y = place()
        self.x = self.xhi * 2 + self.xlo
        self.send, self.recv, self.used = send, recv, 0

    def at_x(self, step):
        return device((self.x + step) % 4, self.y, self.z, self.core)

    def at_z(self, step):
        return device(self.x, self.y, (self.z + step) % 4, self.core)

    def at_y(self, step):
        return device(self.x, (self.y + step) % 4, self.z, self.core)

    def twin(self):
        return device(self.x, self.y, self.z, 1 - self.core)

    def greet(self):
        barrier = pltpu.get_barrier_semaphore()
        peers = [self.twin()]
        for step in (1, 2, 3):
            peers += [self.at_x(step), self.at_z(step), self.at_y(step)]
        for peer in peers:
            pl.semaphore_signal(barrier, inc=1, device_id=peer, device_id_type=MESH)
        pl.semaphore_wait(barrier, len(peers))

    def copy(self, source, target, peer):
        number = self.used
        self.used += 1
        return pltpu.make_async_remote_copy(
            src_ref=source,
            dst_ref=target,
            send_sem=self.send.at[number],
            recv_sem=self.recv.at[number],
            device_id=peer,
            device_id_type=MESH,
        )


def start(copies):
    for item in copies:
        item.start()


def wait(copies):
    for item in copies:
        item.wait()


def lanes(shape):
    return lax.broadcasted_iota(jnp.int32, shape, len(shape) - 1)


def low_half(tile):
    return jnp.where(lanes(tile.shape) < HD, tile, 0.0)


def high_half(tile):
    return jnp.where(lanes(tile.shape) >= HD, tile, 0.0)


def swap_halves(tile):
    return pltpu.roll(tile, HD, axis=1)


def turn(tile, cosine, sine_up, sine_down):
    return (
        tile * cosine
        + pltpu.roll(tile, ROT // 2, axis=1) * sine_up
        + pltpu.roll(tile, TILE - ROT // 2, axis=1) * sine_down
    )


def fold(block):
    rows, width = block.shape
    return jnp.sum(block.reshape(rows // 8, 8, width), axis=0)


def standardize(rows_in):
    values = rows_in.astype(F32)
    centred = values - jnp.mean(values, axis=-1, keepdims=True)
    scale = lax.rsqrt(jnp.mean(centred * centred, axis=-1, keepdims=True) + EPSILON)
    return centred * scale, scale


def norm_back(gradient, xhat, scale):
    return scale * (
        gradient
        - jnp.mean(gradient, axis=-1, keepdims=True)
        - xhat * jnp.mean(gradient * xhat, axis=-1, keepdims=True)
    )


def front_kernel(
    pack, cot, tok, cosine, sine_up, sine_down, perm,
    wq, qz, zd, kv, mlp, dx2, g12, srow, n1, cotb, small,
    slots, w2, n2, dhid, act, xhat, rstd, bias, send, recv,
):
    net = Links(send, recv)
    xlo, core, xhi, z, y = net.xlo, net.core, net.xhi, net.z, net.y
    own = ((xlo * 2 + core) * 2 + xhi) * 4 + z
    block = xhi * 4 + z
    net.greet()
    first_a = [
        net.copy(pack.at[:, 0:640], slots.at[own, :, 0:640], net.at_z(step)) for step in (1, 2, 3)
    ]
    first_b = [
        net.copy(pack.at[:, 640:HALF], slots.at[own, :, 640:HALF], net.at_x(step))
        for step in (1, 2, 3)
    ]
    gather_y = [net.copy(cot, cotb.at[y], net.at_y(step)) for step in (1, 2, 3)]
    start(first_a + first_b + gather_y)
    slots[own] = pack[...]
    cotb[y] = cot[...]

    @pl.loop(0, 4)
    def _(index):
        rows = pl.ds(pl.multiple_of(index * TILE, TILE), TILE)
        normed, scale = standardize(tok[rows, :])
        xhat[rows, :] = normed
        rstd[rows, :] = jnp.broadcast_to(scale, (TILE, TILE))

    wait(first_a)
    four = pl.ds(own - z, 4)
    second_a = [
        net.copy(slots.at[four, :, 0:640], slots.at[four, :, 0:640], net.at_x(step))
        for step in (1, 2, 3)
    ]
    start(second_a)
    wait(first_b)
    second_b = []
    for low in (0, 1):
        for high in (0, 1):
            slot = ((low * 2 + core) * 2 + high) * 4 + z
            piece = slots.at[slot, :, 640:HALF]
            second_b += [net.copy(piece, piece, net.at_z(step)) for step in (1, 2, 3)]
    start(second_b)
    wait(second_a)
    third_a, third_b = [], []
    for low in (0, 1):
        eight = pl.ds((low * 2 + core) * 8, 8)
        piece = slots.at[eight, :, 0:640]
        third_a.append(net.copy(piece, piece, net.twin()))
    start(third_a)
    wait(second_b)
    for low in (0, 1):
        eight = pl.ds((low * 2 + core) * 8, 8)
        piece = slots.at[eight, :, 640:HALF]
        third_b.append(net.copy(piece, piece, net.twin()))
    start(third_b)
    wait(third_a)

    def unpack(source, left, right):
        @pl.loop(0, 16)
        def _(pair):
            rows = pl.ds(pl.multiple_of(pair * 48, 16), 48)
            one = slots[2 * pair, :, source].astype(F32)
            two = slots[2 * pair + 1, :, source].astype(F32)
            width = right.stop - right.start
            w2[rows, left] = jnp.concatenate([one[0:24], two[0:24]], axis=0).astype(BF16)
            w2[rows, right] = jnp.concatenate(
                [one[24:48, 0:width], two[24:48, 0:width]], axis=0
            ).astype(BF16)

    unpack(slice(0, 640), slice(0, 640), slice(1280, 1920))
    turned = w2[:, 512:640].astype(F32).T
    small[...] = turned[64:80, :]
    spread = dot(turned[64:80, :].astype(BF16), perm[...])
    lane = lanes((1, 640))
    inner = lane % TILE
    bias[0:1, 0:640] = jnp.where(
        lane >= 384, spread[7:8, 0:640], jnp.where(inner < HD, spread[8:9, 0:640], spread[9:10, 0:640])
    )
    bias[1:2, :] = spread[6:7, 640:1408]

    @pl.loop(0, 4)
    def _(index):
        rows = pl.ds(pl.multiple_of(index * TILE, TILE), TILE)
        normed = xhat[rows, :]
        one = (normed * small[0:1, :] + small[2:3, :]).astype(BF16)
        n1[rows, :] = one
        n2[rows, :] = (normed * small[1:2, :] + small[3:4, :]).astype(BF16)
        projected = dot(one, w2[:, QKV]) + bias[0:1, 0:640]
        turning = (cosine[rows, :], sine_up[rows, :], sine_down[rows, :])
        for head in range(3):
            span = slice(head * TILE, head * TILE + TILE)
            kv[block, rows, span] = turn(projected[:, span], *turning).astype(BF16)
        pair, last = projected[:, 384:512], projected[:, 512:640]
        for head, tile in enumerate((pair, swap_halves(pair), last)):
            span = slice(head * TILE, head * TILE + TILE)
            qz[rows, span] = (low_half(turn(low_half(tile), *turning)) * 0.125).astype(BF16)

    mine = kv.at[block]
    across = net.copy(mine, mine, net.at_x(2))
    inside = [net.copy(mine, mine, net.at_z(step)) for step in (1, 2, 3)]
    prior = kv.at[z]
    before = [net.copy(prior, prior, net.at_z(step)) for step in (1, 2, 3)]

    @pl.when(xhi == 0)
    def _():
        across.start()

    for step in (1, 2, 3):
        pl.when(z + step <= 3)(inside[step - 1].start)

    wait(third_b)
    unpack(slice(640, HALF), slice(640, 1280), slice(1920, 2432))
    wq[...] = w2[:, 0:896]
    wait(gather_y)
    srow[...] = jnp.zeros_like(srow)

    @pl.when(xhi == 1)
    def _():
        across.wait_recv()
        start(before)

    @pl.loop(0, 4)
    def _(index):
        rows = pl.ds(pl.multiple_of(index * TILE, TILE), TILE)
        hidden = dot(n2[rows, :], w2[:, FC1]) + bias[1:2, :]
        spread_to = 0.5 + 0.5 * lax.erf(hidden * (0.5**0.5))
        active = (hidden * spread_to).astype(BF16)
        act[rows, :] = active
        slope = spread_to + hidden * jnp.exp(-0.5 * hidden * hidden) * 0.3989422804014327
        d_active = 0.0
        d_heads = 0.0
        for part in range(4):
            span = slice(part * PART, part * PART + PART)
            piece = cotb[part, rows, :]
            d_active = d_active + dot(piece, w2[span, FC2])
            d_heads = d_heads + dot(piece, w2[span, DENSE])
            mlp[part, rows, :] = dot_nt(active, w2[span, FC2])
        d_hidden = (slope * d_active).astype(BF16)
        dhid[rows, :] = d_hidden
        d_norm = dot_nt(d_hidden, w2[:, FC1])
        normed = xhat[rows, :]
        dx2[rows, :] = norm_back(small[1:2, :] * d_norm, normed, rstd[rows, 0:1])
        srow[0:8, :] += fold(d_norm * normed)
        srow[8:16, :] += fold(d_norm)
        srow[16:24, :] += fold(d_hidden.astype(F32))
        pair, last = d_heads[:, 0:TILE], d_heads[:, TILE : 2 * TILE]
        for head, tile in enumerate((swap_halves(pair), pair, swap_halves(last))):
            zd[rows, head * TILE : head * TILE + TILE] = high_half(tile).astype(BF16)

    for half in (0, 1):
        span = slice(half * 384, half * 384 + 384)
        g12[span, 0:WIDE] = dot_tn(n2[:, span], dhid[...]).astype(BF16)
    for part in range(4):
        span = slice(part * PART, part * PART + PART)
        g12[span, WIDE : 2 * WIDE] = dot_tn(cotb[part], act[...]).astype(BF16)

    @pl.when(xhi == 0)
    def _():
        across.wait_send()

    for step in (1, 2, 3):
        pl.when(z + step <= 3)(inside[step - 1].wait_send)
        pl.when(z - step >= 0)(inside[step - 1].wait_recv)

    @pl.when(xhi == 1)
    def _():
        wait(before)


def attention_kernel(
    qz, zd, kv, heads, dq, dkv, scores, weights, turned_kv, kept, d_query, limits, totals, summed
):
    block = lax.axis_index("ctx")

    @pl.loop(0, 3)
    def _(head):
        span = pl.ds(pl.multiple_of(head * TILE, TILE), TILE)
        query = qz[:, span]
        query_t = query.astype(F32).T.astype(BF16)

        def score(index, masked):
            tile = kv[index, :, span]
            value = dot(tile, query_t)
            if masked:
                key_at = lax.broadcasted_iota(jnp.int32, value.shape, 0)
                query_at = lax.broadcasted_iota(jnp.int32, value.shape, 1)
                value = jnp.where(key_at <= query_at, value, -1e30)
            scores[index] = value
            turned_kv[index] = tile.astype(F32).T.astype(BF16)
            limits[...] = jnp.maximum(
                limits[...], jnp.max(value.reshape(ROWS // 8, 8, ROWS), axis=0)
            )

        limits[...] = jnp.full_like(limits, -1e30)

        @pl.loop(0, block)
        def _(index):
            score(index, False)

        score(block, True)
        top = jnp.max(limits[...], axis=0, keepdims=True)
        totals[...] = jnp.zeros_like(totals)
        summed[...] = jnp.zeros_like(summed)

        @pl.loop(0, block + 1)
        def _(index):
            unnormed = jnp.exp(scores[index] - top)
            totals[...] += fold(unnormed)
            rounded = unnormed.astype(BF16)
            weights[index] = rounded
            summed[...] += dot(turned_kv[index], rounded)

        inverse = 1.0 / jnp.sum(totals[...], axis=0, keepdims=True)
        out_t = summed[...] * inverse
        kept[head] = out_t.T
        d_out_t = zd[:, span].astype(F32).T
        delta = jnp.sum(d_out_t * out_t, axis=0, keepdims=True) * inverse
        scaled = d_out_t * inverse
        d_out_t = scaled.astype(BF16)
        d_out = scaled.T.astype(BF16)
        d_query[...] = jnp.zeros_like(d_query)

        @pl.loop(0, block + 1)
        def _(index):
            weight = weights[index]
            d_weight = dot(kv[index, :, span], d_out_t)
            d_score = (weight.astype(F32) * (d_weight - delta)).astype(BF16)
            dkv[index, :, span] = (dot(d_score, query) + dot(weight, d_out)).astype(BF16)
            d_query[...] += dot(turned_kv[index], d_score)

        dq[:, span] = low_half((d_query[...] * 0.125).T)

    heads[:, 0:TILE] = jnp.where(
        lanes((ROWS, TILE)) < HD, swap_halves(kept[0]), kept[1]
    ).astype(BF16)
    heads[:, TILE : 2 * TILE] = low_half(swap_halves(kept[2])).astype(BF16)


def back_kernel(
    dkv, dq, heads, wq, mlp, cotb, n1, tok, tok_part, small, dx2, g12, srow, perm,
    cosine, sine_up, sine_down, cot,
    out, ingrad, final, final_y,
    from_z, from_prior, from_x, to_x, out_send, out_recv, dx_send, dx_recv, dqkv, gq, rowsum,
    slots, twin_recv, halves, recv_a, recv_b, sum_a, sum_b, last_a, last_b, y_send, y_recv,
    send, recv,
):
    net = Links(send, recv)
    xlo, core, xhi, z, y = net.xlo, net.core, net.xhi, net.z, net.y
    block = xhi * 4 + z
    net.greet()

    inside = [
        net.copy(dkv.at[xhi * 4 + (z - step) % 4], from_z.at[step - 1], net.at_z(4 - step))
        for step in (1, 2, 3)
    ]
    before = [
        net.copy(dkv.at[(z - step) % 4], from_prior.at[step - 1], net.at_z(4 - step))
        for step in (1, 2, 3)
    ]
    across = net.copy(to_x, from_x, net.at_x(2))

    @pl.when(xhi == 1)
    def _():
        start(before)

    for step in (1, 2, 3):
        pl.when(z - step >= 0)(inside[step - 1].start)

    for part in range(4):
        span = slice(part * PART, part * PART + PART)
        out_send[part] = (mlp[part] + dot_nt(heads[...], wq[span, DENSE])).astype(BF16)
    out_copies = [
        net.copy(out_send.at[(y + step) % 4], out_recv.at[step - 1], net.at_y(step))
        for step in (1, 2, 3)
    ]
    start(out_copies)
    ones = jnp.ones((ROWS, TILE), BF16)
    for part in range(4):
        span = slice(part * PART, part * PART + PART)
        gq[span, DENSE] = dot_tn(cotb[part], heads[...])
        gq[span, 896:1024] = dot_tn(cotb[part], ones)

    @pl.when(xhi == 1)
    def _():
        wait(before)

        @pl.loop(0, 4)
        def _(index):
            rows = pl.ds(pl.multiple_of(index * TILE, TILE), TILE)
            total = dkv[z, rows, :].astype(F32)
            for step in range(3):
                total = total + from_prior[step, rows, :].astype(F32)
            to_x[rows, :] = total.astype(BF16)

        across.start()

    for step in (1, 2, 3):
        pl.when(z - step >= 0)(inside[step - 1].wait_send)
        pl.when(z + step <= 3)(inside[step - 1].wait_recv)

        @pl.when(z + step > 3)
        def _():
            from_z[step - 1] = jnp.zeros((ROWS, 384), BF16)

    @pl.when(xhi == 0)
    def _():
        across.wait_recv()

    @pl.when(xhi == 1)
    def _():
        across.wait_send()
        from_x[...] = jnp.zeros_like(from_x)

    rowsum[...] = jnp.zeros_like(rowsum)

    @pl.loop(0, 4)
    def _(index):
        rows = pl.ds(pl.multiple_of(index * TILE, TILE), TILE)
        turning = (cosine[rows, :], -sine_up[rows, :], -sine_down[rows, :])
        total = dkv[block, rows, :].astype(F32) + from_x[rows, :].astype(F32)
        for step in range(3):
            total = total + from_z[step, rows, :].astype(F32)
        pieces = [
            turn(total[:, head * TILE : head * TILE + TILE], *turning) for head in range(3)
        ]
        query = [
            turn(dq[rows, head * TILE : head * TILE + TILE], *turning) for head in range(3)
        ]
        pieces.append(low_half(query[0]) + swap_halves(low_half(query[1])))
        pieces.append(low_half(query[2]))
        stacked = jnp.concatenate(pieces, axis=1).astype(BF16)
        dqkv[rows, :] = stacked
        d_norm = dot_nt(stacked, wq[:, QKV])
        normed, scale = standardize(tok[rows, :])
        d_input = dx2[rows, :] + norm_back(small[0:1, :] * d_norm, normed, scale)
        rowsum[0:8, :] += fold(d_norm * normed)
        rowsum[8:16, :] += fold(d_norm)
        rowsum[16:24, 0:640] += fold(stacked.astype(F32))
        dx_send[0, rows, :] = d_input[:, 0:PART].astype(BF16)
        for part in range(1, 4):
            moved = pltpu.roll(d_input, WIDE - part * PART, axis=1)
            dx_send[part, rows, :] = moved[:, 0:PART].astype(BF16)

    dx_copies = [
        net.copy(dx_send.at[(y + step) % 4], dx_recv.at[step - 1], net.at_y(step))
        for step in (1, 2, 3)
    ]
    start(dx_copies)
    for half in (0, 1):
        span = slice(half * 384, half * 384 + 384)
        gq[span, QKV] = dot_tn(n1[:, span], dqkv[...])

    def whole(ref, at):
        return jnp.sum(ref[at : at + 8, :], axis=0, keepdims=True)

    row_id = lax.broadcasted_iota(jnp.int32, (16, 640), 0)
    inner = lanes((16, 640)) % TILE
    query_lane = lanes((16, 640)) >= 384
    chosen = row_id == jnp.where(query_lane, 0, jnp.where(inner < HD, 1, 2))
    qkv_rows = jnp.where(chosen, whole(rowsum, 16)[:, 0:640], 0.0).astype(BF16)
    qkv_small = dot_nt(qkv_rows, perm[:, 0:640])
    fc1_rows = jnp.broadcast_to(whole(srow, 16), (16, WIDE)).astype(BF16)
    fc1_small = dot_nt(fc1_rows, perm[:, 640:1408])
    columns = jnp.concatenate(
        [
            jnp.zeros((64, WIDE), F32),
            whole(rowsum, 0),
            whole(srow, 0),
            whole(rowsum, 8),
            whole(srow, 8),
            jnp.zeros((2, WIDE), F32),
            fc1_small[0:1],
            qkv_small[0:3],
            jnp.zeros((54, WIDE), F32),
        ],
        axis=0,
    ).T
    lane = lanes((WIDE, TILE))
    columns = jnp.where((lane == 68) | (lane == 69), gq[:, 896:1024], columns)
    gq[:, 512:640] = jnp.where(lane < HD, gq[:, 512:640], columns)

    @pl.loop(0, 16)
    def _(pair):
        rows = pl.ds(pl.multiple_of(pair * 48, 16), 48)
        left = jnp.concatenate([gq[rows, 0:896], g12[rows, 0:384].astype(F32)], axis=1)
        right = jnp.concatenate(
            [g12[rows, 384:1536].astype(F32), jnp.zeros((48, TILE), F32)], axis=1
        )
        for index in (0, 1):
            part = slice(index * 24, index * 24 + 24)
            slots[2 * pair + index] = jnp.concatenate([left[part], right[part]], axis=0).astype(
                BF16
            )

    twins = [
        net.copy(
            slots.at[pl.ds((low * 2 + 1 - core) * 8, 8)], twin_recv.at[pl.ds(low * 8, 8)], net.twin()
        )
        for low in (0, 1)
    ]
    start(twins)
    wait(twins)

    @pl.loop(0, 16)
    def _(index):
        source = (index // 8 * 2 + core) * 8 + index % 8
        halves[index] = (slots[source].astype(F32) + twin_recv[index].astype(F32)).astype(BF16)

    def quad(position):
        return (position % 2) * 2 + position // 2

    stage_a = [
        net.copy(
            halves.at[pl.ds(quad((net.x + step) % 4) * 4, 4), :, 0:640],
            recv_a.at[step - 1],
            net.at_x(step),
        )
        for step in (1, 2, 3)
    ]
    stage_b = []
    for step in (1, 2, 3):
        for which in range(4):
            stage_b.append(
                net.copy(
                    halves.at[which * 4 + (z + step) % 4, :, 640:HALF],
                    recv_b.at[step - 1, which],
                    net.at_z(step),
                )
            )
    start(stage_a + stage_b)
    wait(stage_a)
    me = quad(net.x)

    @pl.loop(0, 4)
    def _(index):
        total = halves[me * 4 + index, :, 0:640].astype(F32)
        for step in range(3):
            total = total + recv_a[step, index].astype(F32)
        sum_a[index] = total.astype(BF16)

    end_a = [
        net.copy(sum_a.at[(z + step) % 4], last_a.at[step - 1], net.at_z(step))
        for step in (1, 2, 3)
    ]
    start(end_a)
    wait(stage_b)

    @pl.loop(0, 4)
    def _(index):
        total = halves[index * 4 + z, :, 640:HALF].astype(F32)
        for step in range(3):
            total = total + recv_b[step, index].astype(F32)
        sum_b[index] = total.astype(BF16)

    end_b = [
        net.copy(sum_b.at[quad((net.x + step) % 4)], last_b.at[step - 1], net.at_x(step))
        for step in (1, 2, 3)
    ]
    start(end_b)
    wait(end_a)
    total = sum_a[z].astype(F32)
    for step in range(3):
        total = total + last_a[step].astype(F32)
    final[:, 0:640] = total
    y_send[...] = total[:, 512:640]
    y_copies = [net.copy(y_send, y_recv.at[step - 1], net.at_y(step)) for step in (1, 2, 3)]
    start(y_copies)

    wait(out_copies + dx_copies)
    out_bias = small[4:5, :] + small[5:6, :]
    bias_part = jnp.where(y == 0, out_bias[:, 0:PART], 0.0)
    for part in range(1, 4):
        moved = pltpu.roll(jnp.broadcast_to(out_bias, (8, WIDE)), WIDE - part * PART, axis=1)
        bias_part = bias_part + jnp.where(y == part, moved[0:1, 0:PART], 0.0)

    @pl.loop(0, 4)
    def _(index):
        rows = pl.ds(pl.multiple_of(index * TILE, TILE), TILE)
        total = out_send[y, rows, :].astype(F32)
        grad = dx_send[y, rows, :].astype(F32)
        for step in range(3):
            total = total + out_recv[step, rows, :].astype(F32)
            grad = grad + dx_recv[step, rows, :].astype(F32)
        out[rows, :] = (total + tok_part[rows, :].astype(F32) + bias_part).astype(BF16)
        ingrad[rows, :] = grad + cot[rows, :].astype(F32)

    wait(end_b)
    total = sum_b[me].astype(F32)
    for step in range(3):
        total = total + last_b[step].astype(F32)
    final[:, 640:HALF] = total
    wait(y_copies)
    final_y[...] = y_send[...] + y_recv[0] + y_recv[1] + y_recv[2]


def permutation():
    table = np.zeros((WIDE, 1408), np.float32)
    for number in range(32):
        for row in range(12):
            for j in range(2):
                source = 24 * number + 2 * row + j
                table[source, 640 + 64 * row + 2 * number + j] = 1
                if row < 3:
                    at = 2 * number + j
                    table[source, 128 * row + at] = 1
                    table[source, 128 * row + 64 + at] = 1
                    table[source, 384 + 64 * row + at] = 1
    return table


def tables(first):
    frequency = 10000.0 ** (-2.0 * jnp.arange(ROT // 2, dtype=F32) / ROT)
    positions = (first + jnp.arange(ROWS)).astype(F32)
    phases = positions[:, None] * frequency[None, :]
    cosine, sine = jnp.cos(phases), jnp.sin(phases)
    blank = jnp.zeros_like(sine)
    pad = ((0, 0), (0, TILE - ROT))
    return (
        jnp.pad(jnp.concatenate([cosine, cosine], axis=1), pad, constant_values=1.0),
        jnp.pad(jnp.concatenate([blank, sine], axis=1), pad),
        jnp.pad(jnp.concatenate([-sine, blank], axis=1), pad),
    )


def call(kernel, name, shapes, scratch, collective, inputs):
    options = dict(vmem_limit_bytes=VMEM_LIMIT)
    if collective is not None:
        options.update(collective_id=collective, has_side_effects=True)
    return pl.pallas_call(
        kernel,
        name=name,
        out_shape=[jax.ShapeDtypeStruct(shape, kind) for shape, kind in shapes],
        in_specs=[pl.BlockSpec(memory_space=pltpu.VMEM)] * len(inputs),
        out_specs=[pl.BlockSpec(memory_space=pltpu.VMEM)] * len(shapes),
        scratch_shapes=scratch,
        compiler_params=pltpu.CompilerParams(**options),
    )(*inputs)


def shards(
    tokens,
    norm_gain,
    norm_bias,
    qkv_weight,
    qkv_bias,
    dense_weight,
    fc1_weight,
    fc1_bias,
    fc2_weight,
    out_bias,
    cotangent,
):
    tok = tokens[0]
    cot = cotangent[0]
    query, key, value = (qkv_weight[:, which].reshape(24, 3, HD) for which in range(3))
    key_value = jnp.concatenate([key, value], axis=2).reshape(24, 384)
    small_in = jnp.concatenate(
        [
            norm_gain.T,
            norm_bias.T,
            out_bias.T,
            fc1_bias.reshape(24, 1),
            jnp.pad(qkv_bias.reshape(3, 6).T, ((0, 18), (0, 0))),
            jnp.zeros((24, 54), BF16),
        ],
        axis=1,
    )
    blank = jnp.zeros((24, TILE), BF16)
    left = jnp.concatenate(
        [
            key_value,
            query.reshape(24, PART),
            small_in,
            dense_weight.T,
            blank[:, 0:64],
            fc1_weight[:, 0:384],
        ],
        axis=1,
    )
    right = jnp.concatenate([fc1_weight[:, 384:], fc2_weight.T, blank], axis=1)
    pack = jnp.concatenate([left, right], axis=0)
    turning = tables(lax.axis_index("ctx") * ROWS)
    perm = jnp.asarray(permutation(), BF16)
    vm = pltpu.VMEM
    dma = pltpu.SemaphoreType.DMA

    wq, qz, zd, kv, mlp, dx2, g12, srow, n1, cotb, small = call(
        front_kernel,
        "front",
        [
            ((WIDE, 896), BF16),
            ((ROWS, 384), BF16),
            ((ROWS, 384), BF16),
            ((8, ROWS, 384), BF16),
            ((4, ROWS, PART), F32),
            ((ROWS, WIDE), F32),
            ((WIDE, 2 * WIDE), BF16),
            ((24, WIDE), F32),
            ((ROWS, WIDE), BF16),
            ((4, ROWS, PART), BF16),
            ((16, WIDE), F32),
        ],
        [
            vm((32, 48, HALF), BF16),
            vm((WIDE, 2432), BF16),
            vm((ROWS, WIDE), BF16),
            vm((ROWS, WIDE), BF16),
            vm((ROWS, WIDE), BF16),
            vm((ROWS, WIDE), F32),
            vm((ROWS, TILE), F32),
            vm((8, WIDE), F32),
            dma((40,)),
            dma((40,)),
        ],
        0,
        [pack, cot, tok, *turning, perm],
    )
    heads, dq, dkv = call(
        attention_kernel,
        "attention",
        [((ROWS, 256), BF16), ((ROWS, 384), F32), ((8, ROWS, 384), BF16)],
        [
            vm((8, ROWS, ROWS), F32),
            vm((8, ROWS, ROWS), BF16),
            vm((8, TILE, ROWS), BF16),
            vm((3, ROWS, TILE), F32),
            vm((TILE, ROWS), F32),
            vm((8, ROWS), F32),
            vm((8, ROWS), F32),
            vm((TILE, ROWS), F32),
        ],
        None,
        [qz, zd, kv],
    )
    tok_part = lax.dynamic_slice_in_dim(tok, lax.axis_index("tensor") * PART, PART, 1)
    output, input_grad, final, final_y = call(
        back_kernel,
        "back",
        [
            ((ROWS, PART), BF16),
            ((ROWS, PART), F32),
            ((48, HALF), F32),
            ((48, TILE), F32),
        ],
        [
            vm((3, ROWS, 384), BF16),
            vm((3, ROWS, 384), BF16),
            vm((ROWS, 384), BF16),
            vm((ROWS, 384), BF16),
            vm((4, ROWS, PART), BF16),
            vm((3, ROWS, PART), BF16),
            vm((4, ROWS, PART), BF16),
            vm((3, ROWS, PART), BF16),
            vm((ROWS, 640), BF16),
            vm((WIDE, 1024), F32),
            vm((24, WIDE), F32),
            vm((32, 48, HALF), BF16),
            vm((16, 48, HALF), BF16),
            vm((16, 48, HALF), BF16),
            vm((3, 4, 48, 640), BF16),
            vm((3, 4, 48, 640), BF16),
            vm((4, 48, 640), BF16),
            vm((4, 48, 640), BF16),
            vm((3, 48, 640), BF16),
            vm((3, 48, 640), BF16),
            vm((48, TILE), F32),
            vm((3, 48, TILE), F32),
            dma((48,)),
            dma((48,)),
        ],
        1,
        [
            dkv, dq, heads, wq, mlp, cotb, n1, tok, tok_part, small, dx2, g12, srow, perm,
            *turning, cot,
        ],
    )
    grads = jnp.concatenate([final[0:24], final[24:48]], axis=1)
    summed = final_y[0:24, 64:68].T
    key_value = grads[:, 0:384].reshape(24, 3, 2, HD)
    grad_qkv = jnp.stack(
        [
            grads[:, 384:576],
            key_value[:, :, 0].reshape(24, PART),
            key_value[:, :, 1].reshape(24, PART),
        ],
        axis=1,
    )
    return (
        output[None],
        input_grad[None],
        summed[0:2],
        summed[2:4],
        grad_qkv,
        grads[0:6, 583:586].T.reshape(3, 3, 2),
        grads[:, 640:832].T,
        grads[:, 896:1664],
        grads[:, 582].reshape(12, 2),
        grads[:, 1664:2432].T,
        grads[:, 580:582].T,
    )


def solution(mesh):
    return jax.shard_map(
        shards,
        mesh=mesh,
        in_specs=(
            P("dp", "ctx", None),
            P(None, ("dp", "ctx")),
            P(None, ("dp", "ctx")),
            P(("dp", "ctx"), None, "tensor"),
            P(None, "tensor", ("dp", "ctx")),
            P("tensor", ("dp", "ctx")),
            P(("dp", "ctx"), "tensor"),
            P("tensor", ("dp", "ctx")),
            P("tensor", ("dp", "ctx")),
            P(None, ("dp", "ctx")),
            P("dp", "ctx", "tensor"),
        ),
        out_specs=(
            P("dp", "ctx", "tensor"),
            P("dp", "ctx", "tensor"),
            P(None, ("dp", "ctx")),
            P(None, ("dp", "ctx")),
            P(("dp", "ctx"), None, "tensor"),
            P(None, "tensor", ("dp", "ctx")),
            P("tensor", ("dp", "ctx")),
            P(("dp", "ctx"), "tensor"),
            P("tensor", ("dp", "ctx")),
            P("tensor", ("dp", "ctx")),
            P(None, ("dp", "ctx")),
        ),
        check_vma=False,
    )
```

```python
import jax
import jax.numpy as jnp
import numpy as np
from jax import lax
from jax.experimental import pallas as pl
from jax.experimental.pallas import tpu as pltpu
from jax.sharding import PartitionSpec as P

HD = 64
ROT = 16
EPSILON = 1e-05
ROWS = 512
WIDE = 768
HALF = 1280
PART = 192
TILE = 128
MESH = pl.DeviceIdType.MESH
VMEM_LIMIT = 61 << 20
F32 = jnp.float32
BF16 = jnp.bfloat16

QKV = slice(0, 640)
DENSE = slice(640, 896)
FC1 = slice(896, 1664)
FC2 = slice(1664, 2432)
EARLY = 512
SMALL = 64


def dot(a, b):
    return lax.dot_general(a, b, (((1,), (0,)), ((), ())), preferred_element_type=F32)


def dot_nt(a, b):
    return lax.dot_general(a, b, (((1,), (1,)), ((), ())), preferred_element_type=F32)


def dot_tn(a, b):
    return lax.dot_general(a, b, (((0,), (0,)), ((), ())), preferred_element_type=F32)


def device(x, y, z, core):
    return {"dp": (x % 2) * 2 + core, "ctx": (x // 2) * 4 + z, "tensor": y}


class Links:
    def __init__(self, send, recv):
        dp = lax.axis_index("dp")
        cx = lax.axis_index("ctx")
        self.xlo, self.core, self.xhi, self.z = dp // 2, dp % 2, cx // 4, cx % 4
        self.y = lax.axis_index("tensor")
        self.x = self.xhi * 2 + self.xlo
        self.send, self.recv, self.used = send, recv, 0

    def at_x(self, step):
        return device((self.x + step) % 4, self.y, self.z, self.core)

    def at_z(self, step):
        return device(self.x, self.y, (self.z + step) % 4, self.core)

    def at_y(self, step):
        return device(self.x, (self.y + step) % 4, self.z, self.core)

    def twin(self):
        return device(self.x, self.y, self.z, 1 - self.core)

    def pal(self):
        return device((self.x + 2) % 4, self.y, 3 - self.z, self.core)

    def knock(self):
        self.barrier = pltpu.get_barrier_semaphore()
        peers = [self.twin(), self.pal()]
        for step in (1, 2, 3):
            peers += [self.at_x(step), self.at_z(step), self.at_y(step)]
        for peer in peers:
            pl.semaphore_signal(self.barrier, inc=1, device_id=peer, device_id_type=MESH)
        self.expected = len(peers)

    def enter(self):
        pl.semaphore_wait(self.barrier, self.expected)

    def copy(self, source, target, peer):
        number = self.used
        self.used += 1
        return pltpu.make_async_remote_copy(
            src_ref=source,
            dst_ref=target,
            send_sem=self.send.at[number],
            recv_sem=self.recv.at[number],
            device_id=peer,
            device_id_type=MESH,
        )


def start(copies):
    for item in copies:
        item.start()


def wait(copies):
    for item in copies:
        item.wait()


def lanes(shape):
    return lax.broadcasted_iota(jnp.int32, shape, len(shape) - 1)


def low_half(tile):
    return jnp.where(lanes(tile.shape) < HD, tile, 0.0)


def high_half(tile):
    return jnp.where(lanes(tile.shape) >= HD, tile, 0.0)


def swap_halves(tile):
    return pltpu.roll(tile, HD, axis=1)


def turn(tile, cosine, sine_up, sine_down):
    return (
        tile * cosine
        + pltpu.roll(tile, ROT // 2, axis=1) * sine_up
        + pltpu.roll(tile, TILE - ROT // 2, axis=1) * sine_down
    )


def fold(block):
    rows, width = block.shape
    return jnp.sum(block.reshape(rows // 8, 8, width), axis=0)


def column_sum(block):
    return jnp.sum(block, axis=0, keepdims=True)


def standardize(rows_in):
    values = rows_in.astype(F32)
    centred = values - jnp.mean(values, axis=-1, keepdims=True)
    scale = lax.rsqrt(jnp.mean(centred * centred, axis=-1, keepdims=True) + EPSILON)
    return centred * scale, scale


def norm_back(gradient, xhat, scale):
    return scale * (
        gradient
        - jnp.mean(gradient, axis=-1, keepdims=True)
        - xhat * jnp.mean(gradient * xhat, axis=-1, keepdims=True)
    )


def tile_at(index):
    return pl.ds(pl.multiple_of(index * TILE, TILE), TILE)


def quad(position):
    return (position % 2) * 2 + position // 2


class Gather:
    def __init__(self, net, slots, own, low, middle, high):
        self.net, self.slots, self.own = net, slots, own
        self.first, self.second = slice(low, middle), slice(middle, high)

    def one(self):
        net = self.net
        a = self.slots.at[self.own, :, self.first]
        b = self.slots.at[self.own, :, self.second]
        self.a = [net.copy(a, a, net.at_z(step)) for step in (1, 2, 3)]
        self.b = [net.copy(b, b, net.at_x(step)) for step in (1, 2, 3)]
        start(self.a + self.b)

    def two(self):
        net = self.net
        wait(self.a)
        a = self.slots.at[pl.ds(self.own - net.z, 4), :, self.first]
        self.a = [net.copy(a, a, net.at_x(step)) for step in (1, 2, 3)]
        start(self.a)
        wait(self.b)
        self.b = []
        for low in (0, 1):
            for high in (0, 1):
                number = ((low * 2 + net.core) * 2 + high) * 4 + net.z
                b = self.slots.at[number, :, self.second]
                self.b += [net.copy(b, b, net.at_z(step)) for step in (1, 2, 3)]
        start(self.b)

    def three(self):
        net = self.net
        later = []
        for done, span in ((self.a, self.first), (self.b, self.second)):
            wait(done)
            for low in (0, 1):
                part = self.slots.at[pl.ds((low * 2 + net.core) * 8, 8), :, span]
                later.append(net.copy(part, part, net.twin()))
                later[-1].start()
        self.a = later

    def end(self):
        wait(self.a)


class Reduce:
    def __init__(self, net, slots, low, middle, high, twin_in, halves, in_a, in_b, sum_a, sum_b, end_a, end_b):
        self.net, self.slots = net, slots
        self.whole, self.first, self.second = slice(low, high), slice(low, middle), slice(middle, high)
        self.bufs = (twin_in, halves, in_a, in_b, sum_a, sum_b, end_a, end_b)

    def one(self):
        net = self.net
        self.twins = [
            net.copy(
                self.slots.at[pl.ds((low * 2 + 1 - net.core) * 8, 8), :, self.whole],
                self.bufs[0].at[pl.ds(low * 8, 8), :, self.whole],
                net.twin(),
            )
            for low in (0, 1)
        ]
        start(self.twins)

    def two(self):
        net = self.net
        twin_in, halves, in_a, in_b = self.bufs[:4]
        wait(self.twins)

        @pl.loop(0, 16)
        def _(index):
            source = (index // 8 * 2 + net.core) * 8 + index % 8
            halves[index, :, self.whole] = (
                self.slots[source, :, self.whole].astype(F32) + twin_in[index, :, self.whole].astype(F32)
            ).astype(BF16)

        self.a = [
            net.copy(
                halves.at[pl.ds(quad((net.x + step) % 4) * 4, 4), :, self.first],
                in_a.at[step - 1],
                net.at_x(step),
            )
            for step in (1, 2, 3)
        ]
        self.b = [
            net.copy(
                halves.at[which * 4 + (net.z + step) % 4, :, self.second],
                in_b.at[step - 1, which],
                net.at_z(step),
            )
            for step in (1, 2, 3)
            for which in range(4)
        ]
        start(self.a + self.b)

    def three(self):
        net = self.net
        halves, in_a, in_b, sum_a, sum_b, end_a, end_b = self.bufs[1:]
        me = quad(net.x)
        wait(self.a)
        for index in range(4):
            total = halves[me * 4 + index, :, self.first].astype(F32)
            for step in range(3):
                total = total + in_a[step, index].astype(F32)
            sum_a[index] = total.astype(BF16)
        self.a = [
            net.copy(sum_a.at[(net.z + step) % 4], end_a.at[step - 1], net.at_z(step))
            for step in (1, 2, 3)
        ]
        start(self.a)
        wait(self.b)
        for index in range(4):
            total = halves[index * 4 + net.z, :, self.second].astype(F32)
            for step in range(3):
                total = total + in_b[step, index].astype(F32)
            sum_b[index] = total.astype(BF16)
        self.b = [
            net.copy(sum_b.at[quad((net.x + step) % 4)], end_b.at[step - 1], net.at_x(step))
            for step in (1, 2, 3)
        ]
        start(self.b)

    def end(self, target):
        sum_a, sum_b, end_a, end_b = self.bufs[4:]
        for copies, own, arrived, span in (
            (self.a, sum_a.at[self.net.z], end_a, self.first),
            (self.b, sum_b.at[quad(self.net.x)], end_b, self.second),
        ):
            wait(copies)
            total = own[...].astype(F32)
            for step in range(3):
                total = total + arrived[step].astype(F32)
            target[:, span] = total


def layer_kernel(
    tok, gains, shifts, outs, qkv, qkv_small, dense, fc1, fc1_small, fc2, cot_own, perm, angle_rows, angle_block,
    out_t, grad_t, final,
    slots, w2, small, bias, small_rows, narrow, out_col, cosine, sine_up, sine_down, xhat, rstd, tok_t, n1, n2, dhid, act,
    cot_t, cot, mlp_t, dx2, srow, qd, qd_in, qdt, kv, dkv, kv_t, weights, tops, top, totals, summed,
    part_out, part_in, stat_out, stat_in, dq_out, dq_in, kept, gq,
    twin_in, halves, early_a, early_b, early_sa, early_sb, early_ea, early_eb,
    late_a, late_b, late_sa, late_sb, late_ea, late_eb,
    from_z, from_x, out_send, out_recv, dx_send, dx_recv, rowsum, y_send, y_recv,
    send, recv,
):
    net = Links(send, recv)
    xlo, core, xhi, z, y = net.xlo, net.core, net.xhi, net.z, net.y
    own = ((xlo * 2 + core) * 2 + xhi) * 4 + z
    block = xhi * 4 + z
    upper, lower = xhi == 1, xhi == 0
    both = jnp.logical_and
    either = jnp.logical_or
    helps = both(lower, z <= 2)
    helped = both(upper, z >= 1)
    heads = dhid.at[:, 0:256]
    dq_t = kept.at[:, 0:HD, :]
    to_x = act.at[:, 0:384]
    dqkv = n2.at[:, QKV]
    total_kv = gq.at[0:ROWS, 0:384]
    net.knock()

    narrow[...] = jnp.zeros_like(narrow)
    for which in range(3):
        narrow[which, :, 0:HD] = qkv[which, :, TILE:PART].astype(F32)
    narrow[3, :, 0:HD] = dense[:, TILE:PART].astype(F32)
    small_rows[...] = jnp.zeros_like(small_rows)
    small_rows[SMALL : SMALL + 2, 0:24] = gains[...].astype(F32)
    small_rows[SMALL + 2 : SMALL + 4, 0:24] = shifts[...].astype(F32)
    small_rows[SMALL + 4 : SMALL + 6, 0:24] = outs[...].astype(F32)
    small_rows[SMALL + 6 : SMALL + 8, 0:12] = fc1_small[...].astype(F32)
    for which in range(3):
        at = SMALL + 8 + 2 * which
        small_rows[at : at + 2, 0:3] = qkv_small[which].astype(F32)
    columns = small_rows[...].T[0:24]
    key = qkv[1, :, 0:TILE].astype(F32)
    value = qkv[2, :, 0:TILE].astype(F32)
    left = lanes((24, TILE)) < HD
    top_half = jnp.concatenate(
        [
            jnp.where(left, key, swap_halves(value)),
            jnp.where(left, swap_halves(key), value),
            narrow[1] + swap_halves(narrow[2]),
            dense[:, 0:TILE].astype(F32),
        ],
        axis=1,
    )
    bottom_half = jnp.concatenate(
        [qkv[0, :, 0:TILE].astype(F32), narrow[0] + columns, narrow[3], jnp.zeros((24, TILE), F32)], axis=1
    )
    slots[own, :, 0:EARLY] = jnp.concatenate([top_half, bottom_half], axis=0).astype(BF16)
    slots[own, :, EARLY:HALF] = jnp.concatenate([fc1[...].astype(F32), fc2[...].astype(F32)], axis=0).astype(BF16)
    net.enter()
    early = Gather(net, slots, own, 0, 256, EARLY)
    late = Gather(net, slots, own, EARLY, 896, HALF)
    early.one()

    row_cos, row_sin = angle_rows[0], angle_rows[1]
    block_cos, block_sin = angle_block[0, pl.ds(block, 1), :], angle_block[1, pl.ds(block, 1), :]
    cosine[...] = row_cos * block_cos - row_sin * block_sin
    sine = row_sin * block_cos + row_cos * block_sin
    upward = lanes((ROWS, TILE)) >= ROT // 2
    sine_up[...] = jnp.where(upward, sine, 0.0)
    sine_down[...] = jnp.where(upward, 0.0, -sine)

    @pl.loop(0, 4)
    def _(index):
        rows = tile_at(index)
        normed, scale = standardize(tok[rows, :])
        xhat[rows, :] = normed
        rstd[rows, :] = jnp.broadcast_to(scale, (TILE, TILE))

    early.two()
    late.one()
    mine_t = cot_t.at[pl.ds(pl.multiple_of(y * PART, 16), PART), :]
    gather_y = [net.copy(cot_own, mine_t, net.at_y(step)) for step in (1, 2, 3)]
    start(gather_y)
    mine_t[...] = cot_own[...]
    for index in range(4):
        rows = slice(index * TILE, index * TILE + TILE)
        tok_t[:, rows] = tok[rows, :].astype(F32).T.astype(BF16)
    dkv[...] = jnp.zeros_like(dkv)
    early.three()
    late.two()
    early.end()

    @pl.loop(0, 16)
    def _(pair):
        rows = pl.ds(pl.multiple_of(pair * 48, 16), 48)
        one = slots[2 * pair, :, 0:EARLY].astype(F32)
        two = slots[2 * pair + 1, :, 0:EARLY].astype(F32)
        upper_rows = jnp.concatenate([one[0:24], two[0:24]], axis=0).astype(BF16)
        lower_rows = jnp.concatenate([one[24:48], two[24:48]], axis=0).astype(BF16)
        w2[rows, 0:384] = upper_rows[:, 0:384]
        w2[rows, 640:768] = upper_rows[:, 384:512]
        w2[rows, 384:640] = lower_rows[:, 0:256]
        w2[rows, 768:896] = lower_rows[:, 256:384]

    column_form = w2[:, 512:640].astype(F32)
    out_col[...] = jnp.broadcast_to(
        column_form[:, SMALL + 4 : SMALL + 5] + column_form[:, SMALL + 5 : SMALL + 6], (WIDE, TILE)
    )
    turned = column_form.T[SMALL : SMALL + 16, :]
    small[...] = turned
    spread = dot(turned.astype(BF16), perm[...])
    lane = lanes((1, 640))
    inner = lane % TILE
    qkv_row = [
        spread[8 + 2 * which : 9 + 2 * which, 0:640]
        + pltpu.roll(jnp.broadcast_to(spread[9 + 2 * which : 10 + 2 * which, 0:640], (8, 640)), 1, axis=1)[0:1]
        for which in range(3)
    ]
    bias[0:1, 0:640] = jnp.where(lane >= 384, qkv_row[0], jnp.where(inner < HD, qkv_row[1], qkv_row[2]))
    bias[1:2, :] = (
        spread[6:7, 640:1408] + pltpu.roll(jnp.broadcast_to(spread[7:8, 640:1408], (8, WIDE)), 1, axis=1)[0:1]
    )

    @pl.loop(0, 4)
    def _(index):
        rows = tile_at(index)
        normed = xhat[rows, :]
        one = (normed * small[0:1, :] + small[2:3, :]).astype(BF16)
        n1[rows, :] = one
        n2[rows, :] = (normed * small[1:2, :] + small[3:4, :]).astype(BF16)
        projected = dot(one, w2[:, QKV]) + bias[0:1, 0:640]
        turning = (cosine[rows, :], sine_up[rows, :], sine_down[rows, :])
        for head in range(3):
            span = slice(head * TILE, head * TILE + TILE)
            kv[block, rows, span] = turn(projected[:, span], *turning).astype(BF16)
        pair, last = projected[:, 384:512], projected[:, 512:640]
        for head, tile in enumerate((pair, swap_halves(pair), last)):
            span = slice(head * TILE, head * TILE + TILE)
            qd[rows, span] = (low_half(turn(low_half(tile), *turning)) * 0.125).astype(BF16)

    spans = [slice(head * TILE, head * TILE + TILE) for head in range(3)]
    send_own, send_prior, receive, given = [], [], [], []
    for step in (1, 2, 3):
        behind = z + step <= 3
        send_own.append(either(behind, both(lower, both(z + step == 4, z <= 2))))
        send_prior.append(both(upper, z + step > 3))
        receive.append(either(upper, either(z - step >= 0, both(z == 0, step >= 2))))
        given.append((z - step + 4) % 4 + 4 * xhi * ((z - step + 4) // 4))
    across, along = [], []
    for head in range(3):
        mine = kv.at[block, :, spans[head]]
        across.append(net.copy(mine, mine, net.at_x(2)))
        along.append([])
        for step in (1, 2, 3):
            piece = kv.at[block - 4 * xhi * ((z + step) // 4), :, spans[head]]
            along[head].append(net.copy(piece, piece, net.at_z(step)))
    for head in range(3):
        pl.when(lower)(across[head].start)
        for step in range(3):
            pl.when(send_own[step])(along[head][step].start)
    late.three()

    wait(gather_y)
    for index in range(4):
        rows = slice(index * TILE, index * TILE + TILE)
        cot[rows, :] = cot_t[:, rows].astype(F32).T.astype(BF16)
    out_sums = jnp.sum(cot_t[...].astype(F32), axis=1, keepdims=True)

    @pl.loop(0, 4)
    def _(index):
        rows = tile_at(index)
        d_heads = dot(cot[rows, :], w2[:, DENSE])
        pair, last = d_heads[:, 0:TILE], d_heads[:, TILE : 2 * TILE]
        for head, tile in enumerate((swap_halves(pair), pair, swap_halves(last))):
            qd[rows, spans[head]] = (qd[rows, spans[head]].astype(F32) + high_half(tile)).astype(BF16)

    lend = net.copy(qd, qd_in, net.pal())
    pl.when(helped)(lend.start)
    for head in range(3):

        @pl.when(upper)
        def _():
            across[head].wait_recv()

        for step in range(3):
            pl.when(send_prior[step])(along[head][step].start)
    late.end()

    @pl.loop(0, 16)
    def _(pair):
        rows = pl.ds(pl.multiple_of(pair * 48, 16), 48)
        one = slots[2 * pair, :, EARLY:HALF].astype(F32)
        two = slots[2 * pair + 1, :, EARLY:HALF].astype(F32)
        w2[rows, FC1] = jnp.concatenate([one[0:24], two[0:24]], axis=0).astype(BF16)
        w2[rows, FC2] = jnp.concatenate([one[24:48], two[24:48]], axis=0).astype(BF16)

    srow[...] = jnp.zeros_like(srow)

    @pl.loop(0, 4)
    def _(index):
        rows = tile_at(index)
        hidden = dot(n2[rows, :], w2[:, FC1]) + bias[1:2, :]
        spread_to = 0.5 + 0.5 * lax.erf(hidden * (0.5**0.5))
        act[rows, :] = (hidden * spread_to).astype(BF16)
        slope = spread_to + hidden * jnp.exp(-0.5 * hidden * hidden) * 0.3989422804014327
        d_hidden = (slope * dot(cot[rows, :], w2[:, FC2])).astype(BF16)
        dhid[rows, :] = d_hidden
        d_norm = dot_nt(d_hidden, w2[:, FC1])
        normed = xhat[rows, :]
        dx2[rows, :] = norm_back(small[1:2, :] * d_norm, normed, rstd[rows, 0:1])
        srow[0:8, :] += fold(d_norm * normed)
        srow[8:16, :] += fold(d_norm)
        srow[16:24, :] += fold(d_hidden.astype(F32))

    for half in (0, 1):
        span = slice(half * 384, half * 384 + 384)
        mlp_t[span, :] = dot_nt(w2[span, FC2], act[...])
        gq[0:384, 0:WIDE] = dot_tn(n2[:, span], dhid[...])
        gq[384:768, 0:WIDE] = dot(cot_t[span, :], act[...])

        @pl.loop(0, 16)
        def _(index):
            first = pl.ds(pl.multiple_of(index * 24, 8), 24)
            second = pl.ds(pl.multiple_of(384 + index * 24, 8), 24)
            slots[half * 16 + index, :, EARLY:HALF] = jnp.concatenate(
                [gq[first, 0:WIDE], gq[second, 0:WIDE]], axis=0
            ).astype(BF16)

    fc_sum = Reduce(
        net, slots, EARLY, 896, HALF, twin_in, halves, late_a, late_b, late_sa, late_sb, late_ea, late_eb
    )
    fc_sum.one()

    row_is_low = lax.broadcasted_iota(jnp.int32, (TILE, ROWS), 0) < HD

    def absorb(head, slot, at, query_t, masked):
        tile = kv[at, :, spans[head]]
        tile_t = tile.astype(F32).T.astype(BF16)
        chunk = head * 5 + slot
        kv_t[chunk] = tile_t
        score = dot(tile, query_t)
        if masked:
            key_at = lax.broadcasted_iota(jnp.int32, score.shape, 0)
            query_at = lax.broadcasted_iota(jnp.int32, score.shape, 1)
            score = jnp.where(key_at <= query_at, score, -1e30)
        before = top[0:1, :]
        peak = jnp.maximum(before, jnp.max(score, axis=0, keepdims=True))
        weight = jnp.exp(score - peak)
        shrink = jnp.exp(before - peak)
        rounded = weight.astype(BF16)
        weights[chunk] = rounded
        tops[chunk] = jnp.broadcast_to(peak, (8, ROWS))
        top[...] = jnp.broadcast_to(peak, (8, ROWS))
        totals[...] = totals[...] * shrink + fold(weight)
        summed[...] = summed[...] * shrink + dot(tile_t, rounded)

    def fresh():
        top[...] = jnp.full_like(top, -1e30)
        totals[...] = jnp.zeros_like(totals)
        summed[...] = jnp.zeros_like(summed)

    first_own = 4 * xhi * 0 + z * xhi
    own_count = block - first_own
    stats = []
    partials = [net.copy(part_out.at[head], part_in.at[head], net.pal()) for head in range(3)]

    @pl.when(jnp.logical_not(helped))
    def _():
        part_in[...] = jnp.zeros_like(part_in)
        part_in[:, HD : HD + 8, :] = jnp.full((3, 8, ROWS), -1e30, F32)
        dq_in[...] = jnp.zeros_like(dq_in)

    @pl.when(helps)
    def _():
        lend.wait_recv()

    for head in range(3):
        pl.when(jnp.logical_and(lower, True))(across[head].wait_send)
        for step in range(3):
            pl.when(receive[step])(along[head][step].wait_recv)

        @pl.when(helps)
        def _():
            turned_in = qd_in[:, spans[head]].astype(F32).T
            qdt[3 + head] = turned_in.astype(BF16)
            query_t = jnp.where(row_is_low, turned_in, 0.0).astype(BF16)
            fresh()

            @pl.loop(0, 3 - z)
            def _(index):
                absorb(head, z + 1 + index, index, query_t, False)

            part_out[head, 0:HD, :] = summed[HD:TILE, :]
            part_out[head, HD : HD + 8, :] = top[...]
            part_out[head, HD + 8 : HD + 16, :] = jnp.broadcast_to(column_sum(totals[...]), (8, ROWS))
            partials[head].start()

        turned_own = qd[:, spans[head]].astype(F32).T
        qdt[head] = turned_own.astype(BF16)
        query_t = jnp.where(row_is_low, turned_own, 0.0).astype(BF16)
        fresh()

        @pl.loop(0, own_count)
        def _(index):
            absorb(head, index, first_own + index, query_t, False)

        absorb(head, own_count, block, query_t, True)
        kept[head, 0:HD, :] = summed[HD:TILE, :]
        kept[head, HD : HD + 8, :] = top[...]
        kept[head, HD + 8 : HD + 16, :] = jnp.broadcast_to(column_sum(totals[...]), (8, ROWS))
        if head == 0:
            fc_sum.two()

    stat_copies = [net.copy(stat_out.at[head], stat_in.at[head], net.pal()) for head in range(3)]
    for head in range(3):
        pl.when(helped)(partials[head].wait_recv)
        top_one, top_two = kept[head, HD : HD + 1, :], part_in[head, HD : HD + 1, :]
        peak = jnp.maximum(top_one, top_two)
        share_one, share_two = jnp.exp(top_one - peak), jnp.exp(top_two - peak)
        total = kept[head, HD + 8 : HD + 9, :] * share_one + part_in[head, HD + 8 : HD + 9, :] * share_two
        inverse = 1.0 / total
        result = (kept[head, 0:HD, :] * share_one + part_in[head, 0:HD, :] * share_two) * inverse
        delta = column_sum(qdt[head, HD:TILE, :].astype(F32) * result)
        kept[head, 0:HD, :] = result
        stat_out[head, 0:8, :] = jnp.broadcast_to(peak, (8, ROWS))
        stat_out[head, 8:16, :] = jnp.broadcast_to(inverse, (8, ROWS))
        stat_out[head, 16:24, :] = jnp.broadcast_to(delta, (8, ROWS))
        pl.when(helped)(stat_copies[head].start)
    heads[:, 0:TILE] = jnp.concatenate([kept[0, 0:HD, :], kept[1, 0:HD, :]], axis=0).T.astype(BF16)
    heads[:, TILE : 2 * TILE] = jnp.concatenate(
        [kept[2, 0:HD, :], jnp.zeros((HD, ROWS), F32)], axis=0
    ).T.astype(BF16)
    fc_sum.three()

    for half in (0, 1):
        span = slice(half * 384, half * 384 + 384)
        out_send[span, :] = (mlp_t[span, :] + dot_nt(w2[span, DENSE], heads[...])).astype(BF16)
        gq[span, DENSE] = dot(cot_t[span, :], heads[...])

    def part_of(number):
        return pl.ds(pl.multiple_of(number * PART, 16), PART)

    out_copies = [
        net.copy(out_send.at[part_of((y + step) % 4), :], out_recv.at[step - 1], net.at_y(step))
        for step in (1, 2, 3)
    ]
    start(out_copies)

    def revert(head, slot, at, stat, query, dout_t):
        chunk = head * 5 + slot
        factor = jnp.exp(tops[chunk, 0:1, :] - stat[head, 0:1, :]) * stat[head, 8:9, :]
        weight = weights[chunk]
        scaled = dout_t * factor
        d_weight = dot(kv[at, :, spans[head]], scaled.astype(BF16))
        d_score = (weight.astype(F32) * (d_weight - stat[head, 16:17, :] * factor)).astype(BF16)
        change = dot(d_score, query) + dot(weight, scaled.T.astype(BF16))
        dkv[at, :, spans[head]] = (dkv[at, :, spans[head]].astype(F32) + change).astype(BF16)
        summed[...] += dot(kv_t[chunk], d_score)

    dq_copies = [net.copy(dq_out.at[head], dq_in.at[head], net.pal()) for head in range(3)]
    returns, relays = [], []
    for head in range(3):
        returns.append(
            [
                net.copy(dkv.at[given[step - 1], :, spans[head]], from_z.at[step - 1, :, spans[head]], net.at_z(4 - step))
                for step in (1, 2, 3)
            ]
        )
        relays.append(net.copy(to_x.at[:, spans[head]], from_x.at[:, spans[head]], net.at_x(2)))

    def relay(head):
        for step in range(3):
            pl.when(either(send_own[step], send_prior[step]))(returns[head][step].wait_recv)

        @pl.when(upper)
        def _():
            total_kv[:, spans[head]] = dkv[z, :, spans[head]].astype(F32)
            for step in range(3):

                @pl.when(send_prior[step])
                def _():
                    total_kv[:, spans[head]] += from_z[step, :, spans[head]].astype(F32)

            to_x[:, spans[head]] = total_kv[:, spans[head]].astype(BF16)
            relays[head].start()

    for head in range(3):
        turned_own = qdt[head].astype(F32)
        dout_t = jnp.where(row_is_low, 0.0, turned_own)
        query = low_half(qd[:, spans[head]].astype(F32)).astype(BF16)
        summed[...] = jnp.zeros_like(summed)

        @pl.loop(0, own_count + 1)
        def _(index):
            revert(head, index, first_own + index, stat_out, query, dout_t)

        dq_t[head] = summed[0:HD, :]

        @pl.when(helps)
        def _():
            stat_copies[head].wait_recv()
            turned_in = qdt[3 + head].astype(F32)
            dout_in = jnp.where(row_is_low, 0.0, turned_in)
            query_in = low_half(qd_in[:, spans[head]].astype(F32)).astype(BF16)
            summed[...] = jnp.zeros_like(summed)

            @pl.loop(0, 3 - z)
            def _(index):
                revert(head, z + 1 + index, index, stat_in, query_in, dout_in)

            dq_out[head] = summed[0:HD, :].astype(BF16)
            dq_copies[head].start()

        for step in range(3):
            pl.when(receive[step])(returns[head][step].start)
        if head > 0:
            relay(head - 1)
        if head == 1:
            fc_sum.end(final)
    relay(2)

    for head in range(3):
        pl.when(helped)(dq_copies[head].wait_recv)
        pl.when(lower)(relays[head].wait_recv)
    total_kv[...] = dkv[block].astype(F32)
    for step in range(3):

        @pl.when(send_own[step])
        def _():
            total_kv[...] += from_z[step].astype(F32)

    @pl.when(lower)
    def _():
        total_kv[...] += from_x[...].astype(F32)

    rowsum[...] = jnp.zeros_like(rowsum)
    for index in range(4):
        rows = slice(index * TILE, index * TILE + TILE)
        turning = (cosine[rows, :], -sine_up[rows, :], -sine_down[rows, :])
        pieces = [turn(total_kv[rows, spans[head]], *turning) for head in range(3)]
        query = []
        for head in range(3):
            grad = (dq_t[head, :, rows] + dq_in[head, :, rows].astype(F32)) * 0.125
            grad = jnp.concatenate([grad, jnp.zeros((HD, TILE), F32)], axis=0).T
            query.append(turn(grad, *turning))
        pieces.append(low_half(query[0]) + swap_halves(low_half(query[1])))
        pieces.append(low_half(query[2]))
        stacked = jnp.concatenate(pieces, axis=1).astype(BF16)
        dqkv[rows, :] = stacked
        d_norm = dot_nt(stacked, w2[:, QKV])
        normed = xhat[rows, :]
        d_input = dx2[rows, :] + norm_back(small[0:1, :] * d_norm, normed, rstd[rows, 0:1])
        rowsum[0:8, :] += fold(d_norm * normed)
        rowsum[8:16, :] += fold(d_norm)
        rowsum[16:24, 0:640] += fold(stacked.astype(F32))
        dx_send[:, rows] = d_input.T.astype(BF16)

    dx_copies = [
        net.copy(dx_send.at[part_of((y + step) % 4), :], dx_recv.at[step - 1], net.at_y(step))
        for step in (1, 2, 3)
    ]

    def whole(ref, at):
        return column_sum(ref[at : at + 8, :])

    y_send[...] = jnp.concatenate(
        [whole(rowsum, 0), whole(srow, 0), whole(rowsum, 8), whole(srow, 8), jnp.zeros((4, WIDE), F32)], axis=0
    )
    y_copies = [net.copy(y_send, y_recv.at[step - 1], net.at_y(step)) for step in (1, 2, 3)]
    start(y_copies + dx_copies)
    for half in (0, 1):
        span = slice(half * 384, half * 384 + 384)
        gq[span, QKV] = dot_tn(n1[:, span], dqkv[...])
    row_id = lax.broadcasted_iota(jnp.int32, (8, 640), 0)
    lane = lanes((8, 640))
    target = jnp.where(lane >= 384, 0, jnp.where(lane % TILE < HD, 1, 2))
    qkv_rows = jnp.where(row_id == target, whole(rowsum, 16)[:, 0:640], 0.0)
    qkv_rows = jnp.concatenate([qkv_rows, pltpu.roll(qkv_rows, 640 - 1, axis=1)], axis=0)
    qkv_cols = dot_nt(qkv_rows.astype(BF16), perm[:, 0:640])
    fc1_rows = jnp.broadcast_to(whole(srow, 16), (8, WIDE))
    fc1_rows = jnp.concatenate([fc1_rows, pltpu.roll(fc1_rows, WIDE - 1, axis=1)], axis=0)
    fc1_cols = dot_nt(fc1_rows.astype(BF16), perm[:, 640:1408])
    wait(y_copies)
    shared = y_send[...] + y_recv[0] + y_recv[1] + y_recv[2]
    columns = jnp.concatenate(
        [
            jnp.zeros((SMALL, WIDE), F32),
            shared[0:4],
            jnp.zeros((2, WIDE), F32),
            fc1_cols[0:1],
            fc1_cols[8:9],
            qkv_cols[0:1],
            qkv_cols[8:9],
            qkv_cols[1:2],
            qkv_cols[9:10],
            qkv_cols[2:3],
            qkv_cols[10:11],
            jnp.zeros((50, WIDE), F32),
        ],
        axis=0,
    ).T
    lane = lanes((WIDE, TILE))
    columns = jnp.where((lane == SMALL + 4) | (lane == SMALL + 5), out_sums, columns)
    gq[:, 512:640] = jnp.where(lane < HD, gq[:, 512:640], columns)

    @pl.loop(0, 32)
    def _(index):
        rows = pl.ds(pl.multiple_of(index * 24, 8), 24)
        first = jnp.concatenate([gq[rows, 0:384], gq[rows, 640:768]], axis=1)
        second = jnp.concatenate([gq[rows, 384:640], gq[rows, 768:896], jnp.zeros((24, TILE), F32)], axis=1)
        slots[index, :, 0:EARLY] = jnp.concatenate([first, second], axis=0).astype(BF16)

    qkv_sum = Reduce(
        net, slots, 0, 256, EARLY, twin_in, halves, early_a, early_b, early_sa, early_sb, early_ea, early_eb
    )
    qkv_sum.one()
    qkv_sum.two()

    wait(out_copies + dx_copies)
    mine = part_of(y)
    total = out_send[mine, :].astype(F32) + tok_t[mine, :].astype(F32) + out_col[mine, 0:1]
    grad = dx_send[mine, :].astype(F32) + cot_own[...].astype(F32)
    for step in range(3):
        total = total + out_recv[step].astype(F32)
        grad = grad + dx_recv[step].astype(F32)
    out_t[...] = total.astype(BF16)
    grad_t[...] = grad
    qkv_sum.three()

    for head in range(3):
        pl.when(helps)(partials[head].wait_send)
        pl.when(helped)(stat_copies[head].wait_send)
        pl.when(helps)(dq_copies[head].wait_send)
        pl.when(upper)(relays[head].wait_send)
        for step in range(3):
            pl.when(either(send_own[step], send_prior[step]))(along[head][step].wait_send)
            pl.when(receive[step])(returns[head][step].wait_send)
    pl.when(helped)(lend.wait_send)
    qkv_sum.end(final)


def finish_kernel(
    out_in, grad_in, final, out_t, grad_t, gain, shift, qkv, qkv_small, dense, fc1, fc1_small, fc2, outs
):
    out_t[...] = out_in[...]
    grad_t[...] = grad_in[...]
    fc1[...] = final[0:24, EARLY:HALF]
    fc2[...] = final[24:48, EARLY:HALF]
    left = lanes((24, TILE)) < HD
    one, two, three = (final[0:24, head * TILE : head * TILE + TILE] for head in range(3))
    qkv[1, :, 0:TILE] = jnp.where(left, one, swap_halves(two))
    qkv[1, :, TILE:PART] = three[:, 0:HD]
    qkv[2, :, 0:TILE] = jnp.where(left, swap_halves(one), two)
    qkv[2, :, TILE:PART] = swap_halves(three)[:, 0:HD]
    qkv[0, :, 0:TILE] = final[24:48, 0:TILE]
    mixed = final[24:48, TILE : 2 * TILE]
    qkv[0, :, TILE:PART] = mixed[:, 0:HD]
    dense[:, 0:TILE] = final[0:24, 384:512]
    dense[:, TILE:PART] = final[24:48, 256 : 256 + HD]
    rows = jnp.concatenate([mixed, jnp.zeros((TILE - 24, TILE), F32)], axis=0).T
    gain[...] = rows[SMALL : SMALL + 2, 0:24]
    shift[...] = rows[SMALL + 2 : SMALL + 4, 0:24]
    outs[...] = rows[SMALL + 4 : SMALL + 6, 0:24]
    fc1_small[...] = rows[SMALL + 6 : SMALL + 8, 0:12]
    for which in range(3):
        at = SMALL + 8 + 2 * which
        qkv_small[which] = rows[at : at + 2, 0:3]


def permutation():
    table = np.zeros((WIDE, 1408), np.float32)
    for number in range(32):
        for row in range(12):
            source = 24 * number + row
            table[source, 640 + 64 * row + 2 * number] = 1
            if row < 3:
                table[source, 128 * row + 2 * number] = 1
                table[source, 128 * row + 64 + 2 * number] = 1
                table[source, 384 + 64 * row + 2 * number] = 1
    return table


def angle_tables():
    frequency = 10000.0 ** (-2.0 * np.arange(ROT // 2) / ROT)
    result = []
    for positions in (np.arange(ROWS), ROWS * np.arange(8)):
        phases = np.zeros((len(positions), TILE))
        phases[:, 0:ROT] = positions[:, None] * np.concatenate([frequency, frequency])[None, :]
        result.append(np.stack([np.cos(phases), np.sin(phases)]).astype(np.float32))
    return result


def call(kernel, name, shapes, scratch, collective, inputs):
    options = dict(vmem_limit_bytes=VMEM_LIMIT)
    if collective is not None:
        options.update(collective_id=collective, has_side_effects=True)
    return pl.pallas_call(
        kernel,
        name=name,
        out_shape=[jax.ShapeDtypeStruct(shape, kind) for shape, kind in shapes],
        in_specs=[pl.BlockSpec(memory_space=pltpu.VMEM)] * len(inputs),
        out_specs=[pl.BlockSpec(memory_space=pltpu.VMEM)] * len(shapes),
        scratch_shapes=scratch,
        compiler_params=pltpu.CompilerParams(**options),
    )(*inputs)


def shards(
    tokens,
    norm_gain,
    norm_bias,
    qkv_weight,
    qkv_bias,
    dense_weight,
    fc1_weight,
    fc1_bias,
    fc2_weight,
    out_bias,
    cotangent,
):
    vm = pltpu.VMEM
    dma = pltpu.SemaphoreType.DMA
    wide = (ROWS, WIDE)
    row_angles, block_angles = angle_tables()
    out_t, grad_t, final = call(
        layer_kernel,
        "layer",
        [((PART, ROWS), BF16), ((PART, ROWS), F32), ((48, HALF), F32)],
        [
            vm((32, 48, HALF), BF16),
            vm((WIDE, 2432), BF16),
            vm((16, WIDE), F32),
            vm((8, WIDE), F32),
            vm((TILE, TILE), F32),
            vm((4, 24, TILE), F32),
            vm((WIDE, TILE), F32),
            vm((ROWS, TILE), F32),
            vm((ROWS, TILE), F32),
            vm((ROWS, TILE), F32),
            vm(wide, F32),
            vm((ROWS, TILE), F32),
            vm((WIDE, ROWS), BF16),
            vm(wide, BF16),
            vm(wide, BF16),
            vm(wide, BF16),
            vm(wide, BF16),
            vm((WIDE, ROWS), BF16),
            vm(wide, BF16),
            vm((WIDE, ROWS), F32),
            vm(wide, F32),
            vm((24, WIDE), F32),
            vm((ROWS, 384), BF16),
            vm((ROWS, 384), BF16),
            vm((6, TILE, ROWS), BF16),
            vm((8, ROWS, 384), BF16),
            vm((8, ROWS, 384), BF16),
            vm((15, TILE, ROWS), BF16),
            vm((15, ROWS, ROWS), BF16),
            vm((15, 8, ROWS), F32),
            vm((8, ROWS), F32),
            vm((8, ROWS), F32),
            vm((TILE, ROWS), F32),
            vm((3, 80, ROWS), F32),
            vm((3, 80, ROWS), F32),
            vm((3, 24, ROWS), F32),
            vm((3, 24, ROWS), F32),
            vm((3, HD, ROWS), BF16),
            vm((3, HD, ROWS), BF16),
            vm((3, 80, ROWS), F32),
            vm((WIDE, 896), F32),
            vm((16, 48, HALF), BF16),
            vm((16, 48, HALF), BF16),
            vm((3, 4, 48, 256), BF16),
            vm((3, 4, 48, 256), BF16),
            vm((4, 48, 256), BF16),
            vm((4, 48, 256), BF16),
            vm((3, 48, 256), BF16),
            vm((3, 48, 256), BF16),
            vm((3, 4, 48, 384), BF16),
            vm((3, 4, 48, 384), BF16),
            vm((4, 48, 384), BF16),
            vm((4, 48, 384), BF16),
            vm((3, 48, 384), BF16),
            vm((3, 48, 384), BF16),
            vm((3, ROWS, 384), BF16),
            vm((ROWS, 384), BF16),
            vm((WIDE, ROWS), BF16),
            vm((3, PART, ROWS), BF16),
            vm((WIDE, ROWS), BF16),
            vm((3, PART, ROWS), BF16),
            vm((24, WIDE), F32),
            vm((8, WIDE), F32),
            vm((3, 8, WIDE), F32),
            dma((144,)),
            dma((144,)),
        ],
        0,
        [
            tokens[0],
            norm_gain,
            norm_bias,
            out_bias,
            jnp.transpose(qkv_weight, (1, 0, 2)),
            jnp.transpose(qkv_bias, (0, 2, 1)),
            dense_weight.T,
            fc1_weight,
            fc1_bias.T,
            fc2_weight.T,
            cotangent[0].T,
            jnp.asarray(permutation(), BF16),
            jnp.asarray(row_angles),
            jnp.asarray(block_angles),
        ],
    )
    out_t, grad_t, gain, shift, qkv, qkv_small, dense, fc1, fc1_small, fc2, outs = call(
        finish_kernel,
        "finish",
        [
            ((PART, ROWS), BF16),
            ((PART, ROWS), F32),
            ((2, 24), F32),
            ((2, 24), F32),
            ((3, 24, PART), F32),
            ((3, 2, 3), F32),
            ((24, PART), F32),
            ((24, WIDE), F32),
            ((2, 12), F32),
            ((24, WIDE), F32),
            ((2, 24), F32),
        ],
        [],
        None,
        [out_t, grad_t, final],
    )
    return (
        out_t.T[None],
        grad_t.T[None],
        gain,
        shift,
        jnp.transpose(qkv, (1, 0, 2)),
        jnp.transpose(qkv_small, (0, 2, 1)),
        dense.T,
        fc1,
        fc1_small.T,
        fc2.T,
        outs,
    )


def solution(mesh):
    return jax.shard_map(
        shards,
        mesh=mesh,
        in_specs=(
            P("dp", "ctx", None),
            P(None, ("dp", "ctx")),
            P(None, ("dp", "ctx")),
            P(("dp", "ctx"), None, "tensor"),
            P(None, "tensor", ("dp", "ctx")),
            P("tensor", ("dp", "ctx")),
            P(("dp", "ctx"), "tensor"),
            P("tensor", ("dp", "ctx")),
            P("tensor", ("dp", "ctx")),
            P(None, ("dp", "ctx")),
            P("dp", "ctx", "tensor"),
        ),
        out_specs=(
            P("dp", "ctx", "tensor"),
            P("dp", "ctx", "tensor"),
            P(None, ("dp", "ctx")),
            P(None, ("dp", "ctx")),
            P(("dp", "ctx"), None, "tensor"),
            P(None, "tensor", ("dp", "ctx")),
            P("tensor", ("dp", "ctx")),
            P(("dp", "ctx"), "tensor"),
            P("tensor", ("dp", "ctx")),
            P("tensor", ("dp", "ctx")),
            P(None, ("dp", "ctx")),
        ),
        check_vma=False,
    )
```

```python
import jax
import jax.numpy as jnp
import numpy as np
from jax import lax
from jax.experimental import pallas as pl
from jax.experimental.pallas import tpu as pltpu
from jax.sharding import PartitionSpec as P

HD = 64
ROT = 16
EPSILON = 1e-05
ROWS = 512
WIDE = 768
HALF = 1280
PART = 192
TILE = 128
MESH = pl.DeviceIdType.MESH
VMEM_LIMIT = 61 << 20
F32 = jnp.float32
BF16 = jnp.bfloat16

QKV = slice(0, 640)
DENSE = slice(640, 896)
FC1 = slice(896, 1664)
FC2 = slice(1664, 2432)
EARLY = 512
SMALL = 64


def dot(a, b):
    return lax.dot_general(a, b, (((1,), (0,)), ((), ())), preferred_element_type=F32)


def dot_nt(a, b):
    return lax.dot_general(a, b, (((1,), (1,)), ((), ())), preferred_element_type=F32)


def dot_tn(a, b):
    return lax.dot_general(a, b, (((0,), (0,)), ((), ())), preferred_element_type=F32)


def device(x, y, z, core):
    return {"dp": (x % 2) * 2 + core, "ctx": (x // 2) * 4 + z, "tensor": y}


class Links:
    def __init__(self, send, recv):
        dp = lax.axis_index("dp")
        cx = lax.axis_index("ctx")
        self.xlo, self.core, self.xhi, self.z = dp // 2, dp % 2, cx // 4, cx % 4
        self.y = lax.axis_index("tensor")
        self.x = self.xhi * 2 + self.xlo
        self.send, self.recv, self.used = send, recv, 0

    def at_x(self, step):
        return device((self.x + step) % 4, self.y, self.z, self.core)

    def at_z(self, step):
        return device(self.x, self.y, (self.z + step) % 4, self.core)

    def at_y(self, step):
        return device(self.x, (self.y + step) % 4, self.z, self.core)

    def twin(self):
        return device(self.x, self.y, self.z, 1 - self.core)

    def pal(self):
        return device((self.x + 2) % 4, self.y, 3 - self.z, self.core)

    def knock(self):
        self.barrier = pltpu.get_barrier_semaphore()
        peers = [self.twin(), self.pal()]
        for step in (1, 2, 3):
            peers += [self.at_x(step), self.at_z(step), self.at_y(step)]
        for peer in peers:
            pl.semaphore_signal(self.barrier, inc=1, device_id=peer, device_id_type=MESH)
        self.expected = len(peers)

    def enter(self):
        pl.semaphore_wait(self.barrier, self.expected)

    def take(self, count):
        self.used += count
        return self.used - count

    def copy(self, source, target, peer, number=None):
        if number is None:
            number = self.take(1)
        return pltpu.make_async_remote_copy(
            src_ref=source,
            dst_ref=target,
            send_sem=self.send.at[number],
            recv_sem=self.recv.at[number],
            device_id=peer,
            device_id_type=MESH,
        )


def start(copies):
    for item in copies:
        item.start()


def wait(copies):
    for item in copies:
        item.wait()


def lanes(shape):
    return lax.broadcasted_iota(jnp.int32, shape, len(shape) - 1)


def low_half(tile):
    return jnp.where(lanes(tile.shape) < HD, tile, 0.0)


def high_half(tile):
    return jnp.where(lanes(tile.shape) >= HD, tile, 0.0)


def swap_halves(tile):
    return pltpu.roll(tile, HD, axis=1)


def turn(tile, cosine, sine_up, sine_down):
    return (
        tile * cosine
        + pltpu.roll(tile, ROT // 2, axis=1) * sine_up
        + pltpu.roll(tile, TILE - ROT // 2, axis=1) * sine_down
    )


def fold(block):
    rows, width = block.shape
    return jnp.sum(block.reshape(rows // 8, 8, width), axis=0)


def column_sum(block):
    return jnp.sum(block, axis=0, keepdims=True)


def standardize(rows_in):
    values = rows_in.astype(F32)
    centred = values - jnp.mean(values, axis=-1, keepdims=True)
    scale = lax.rsqrt(jnp.mean(centred * centred, axis=-1, keepdims=True) + EPSILON)
    return centred * scale, scale


def norm_back(gradient, xhat, scale):
    return scale * (
        gradient
        - jnp.mean(gradient, axis=-1, keepdims=True)
        - xhat * jnp.mean(gradient * xhat, axis=-1, keepdims=True)
    )


def tile_at(index):
    return pl.ds(pl.multiple_of(index * TILE, TILE), TILE)


def quad(position):
    return (position % 2) * 2 + position // 2


class Gather:
    def __init__(self, net, slots, own, low, middle, high):
        first, second = slice(low, middle), slice(middle, high)
        mine_a, mine_b = slots.at[own, :, first], slots.at[own, :, second]
        four = slots.at[pl.ds(own - net.z, 4), :, first]
        steps = (1, 2, 3)
        self.a = [net.copy(mine_a, mine_a, net.at_z(step)) for step in steps]
        self.b = [net.copy(mine_b, mine_b, net.at_x(step)) for step in steps]
        self.mid_a = [net.copy(four, four, net.at_x(step)) for step in steps]
        self.mid_b, self.last_a, self.last_b = [], [], []
        for low in (0, 1):
            for high in (0, 1):
                piece = slots.at[((low * 2 + net.core) * 2 + high) * 4 + net.z, :, second]
                self.mid_b += [net.copy(piece, piece, net.at_z(step)) for step in steps]
            for span, copies in ((first, self.last_a), (second, self.last_b)):
                piece = slots.at[pl.ds((low * 2 + net.core) * 8, 8), :, span]
                copies.append(net.copy(piece, piece, net.twin()))

    def one(self):
        start(self.a + self.b)

    def two(self):
        wait(self.a)
        start(self.mid_a)
        wait(self.b)
        start(self.mid_b)

    def three(self):
        wait(self.mid_a)
        start(self.last_a)
        wait(self.mid_b)
        start(self.last_b)

    def end(self):
        wait(self.last_a + self.last_b)


class Reduce:
    def __init__(self, net, slots, low, middle, high, twin_in, halves, in_a, in_b, sum_a, sum_b, end_a, end_b):
        self.net, self.slots = net, slots
        self.whole, self.first, self.second = slice(low, high), slice(low, middle), slice(middle, high)
        self.bufs = (twin_in, halves, in_a, in_b, sum_a, sum_b, end_a, end_b)
        self.me = quad(net.x)
        self.twins = [
            net.copy(
                slots.at[pl.ds((low * 2 + 1 - net.core) * 8, 8), :, self.whole],
                twin_in.at[pl.ds(low * 8, 8), :, self.whole],
                net.twin(),
            )
            for low in (0, 1)
        ]
        self.mid_a, self.mid_b, self.last_a, self.last_b = [], [], [], []
        for step in (1, 2, 3):
            there = quad((net.x + step) % 4)
            self.mid_a.append(
                net.copy(halves.at[pl.ds(there * 4, 4), :, self.first], in_a.at[step - 1], net.at_x(step))
            )
            for which in range(4):
                self.mid_b.append(
                    net.copy(
                        halves.at[which * 4 + (net.z + step) % 4, :, self.second],
                        in_b.at[step - 1, which],
                        net.at_z(step),
                    )
                )
            self.last_a.append(net.copy(sum_a.at[(net.z + step) % 4], end_a.at[step - 1], net.at_z(step)))
            self.last_b.append(net.copy(sum_b.at[there], end_b.at[step - 1], net.at_x(step)))

    def one(self):
        start(self.twins)

    def two(self):
        twin_in, halves = self.bufs[:2]
        wait(self.twins)

        @pl.loop(0, 16)
        def _(index):
            source = (index // 8 * 2 + self.net.core) * 8 + index % 8
            halves[index, :, self.whole] = (
                self.slots[source, :, self.whole].astype(F32) + twin_in[index, :, self.whole].astype(F32)
            ).astype(BF16)

        start(self.mid_a + self.mid_b)

    def three(self):
        halves, in_a, in_b, sum_a, sum_b = self.bufs[1:6]
        wait(self.mid_a)

        @pl.loop(0, 4)
        def _(index):
            total = halves[self.me * 4 + index, :, self.first].astype(F32)
            for step in range(3):
                total = total + in_a[step, index].astype(F32)
            sum_a[index] = total.astype(BF16)

        start(self.last_a)
        wait(self.mid_b)

        @pl.loop(0, 4)
        def _(index):
            total = halves[index * 4 + self.net.z, :, self.second].astype(F32)
            for step in range(3):
                total = total + in_b[step, index].astype(F32)
            sum_b[index] = total.astype(BF16)

        start(self.last_b)

    def end(self, target):
        sum_a, sum_b, end_a, end_b = self.bufs[4:]
        for copies, own, arrived, span in (
            (self.last_a, sum_a.at[self.net.z], end_a, self.first),
            (self.last_b, sum_b.at[self.me], end_b, self.second),
        ):
            wait(copies)
            total = own[...].astype(F32)
            for step in range(3):
                total = total + arrived[step].astype(F32)
            target[:, span] = total


def layer_kernel(
    tok_in, gains, shifts, outs, qkv_in, qkv_small, dense_in, fc1_in, fc1_small, fc2_in, cot_in, angle_in, angle_block,
    out_t, grad_t, final,
    tok, qkv, dense, fc1, fc2, cot_own, angle_rows, loads,
    slots, w2, small, bias, small_rows, narrow, bias_rows, out_col, cosine, sine_up, sine_down, xhat, rstd, tok_t, n1, n2, dhid, act,
    cot_t, cot, mlp_t, dx2, srow, qd, qd_in, qdt, kv, dkv, kv_t, weights, tops, top, totals, summed, query_t, query_n,
    part_out, part_in, stat, dq_out, dq_in, kept, gq,
    twin_in, halves, early_a, early_b, early_sa, early_sb, early_ea, early_eb,
    late_a, late_b, late_sa, late_sb, late_ea, late_eb,
    from_z, from_x, to_x, heads, out_send, out_recv, dx_send, dx_recv, rowsum, y_send, y_recv,
    send, recv,
):
    net = Links(send, recv)
    xlo, core, xhi, z, y = net.xlo, net.core, net.xhi, net.z, net.y
    own = ((xlo * 2 + core) * 2 + xhi) * 4 + z
    block = xhi * 4 + z
    upper, lower = xhi == 1, xhi == 0
    both = jnp.logical_and
    either = jnp.logical_or
    brought = [
        pltpu.make_async_copy(source, target, loads.at[number])
        for number, (source, target) in enumerate(
            (
                (qkv_in, qkv),
                (dense_in, dense),
                (fc1_in, fc1),
                (fc2_in, fc2),
                (angle_in, angle_rows),
                (tok_in, tok),
                (cot_in, cot_own),
            )
        )
    ]
    start(brought)
    helps = both(lower, z <= 2)
    helped = both(upper, z >= 1)
    dq_t = kept.at[:, 0:HD, :]
    dqkv = n2.at[:, QKV]
    total_kv = gq.at[0:ROWS, 0:384]
    net.knock()

    wait(brought[0:4])
    narrow[...] = jnp.zeros_like(narrow)
    for which in range(3):
        narrow[which, :, 0:HD] = qkv[which, :, TILE:PART].astype(F32)
    narrow[3, :, 0:HD] = dense[:, TILE:PART].astype(F32)
    small_rows[...] = jnp.zeros_like(small_rows)
    small_rows[SMALL : SMALL + 2, 0:24] = gains[...].astype(F32)
    small_rows[SMALL + 2 : SMALL + 4, 0:24] = shifts[...].astype(F32)
    small_rows[SMALL + 4 : SMALL + 6, 0:24] = outs[...].astype(F32)
    columns = small_rows[...].T[0:24]

    small_rows[...] = jnp.zeros_like(small_rows)
    small_rows[0:2, 0:12] = fc1_small[...].astype(F32)
    for which in range(3):
        small_rows[8 + 8 * which : 10 + 8 * which, 0:3] = qkv_small[which].astype(F32)
    turned = small_rows[...].T[0:16]
    pair_lane = lanes((16, TILE)) < 2
    bias_rows[0:16, :] = jnp.where(pair_lane, turned, 0.0)
    bias_rows[16:24, :] = jnp.zeros((8, TILE), F32)
    for which in range(3):
        moved = pltpu.roll(turned, TILE - 8 - 8 * which, axis=1)
        bias_rows[12 + 3 * which : 15 + 3 * which, :] = jnp.where(pair_lane, moved, 0.0)[0:3]
    biases = pltpu.roll(bias_rows[...], 2 * own, axis=1)
    key = qkv[1, :, 0:TILE].astype(F32)
    value = qkv[2, :, 0:TILE].astype(F32)
    left = lanes((24, TILE)) < HD
    top_half = jnp.concatenate(
        [
            jnp.where(left, key, swap_halves(value)),
            jnp.where(left, swap_halves(key), value),
            narrow[1] + swap_halves(narrow[2]),
            dense[:, 0:TILE].astype(F32),
        ],
        axis=1,
    )
    bottom_half = jnp.concatenate(
        [qkv[0, :, 0:TILE].astype(F32), narrow[0] + columns, narrow[3], biases], axis=1
    )
    slots[own, :, 0:EARLY] = jnp.concatenate([top_half, bottom_half], axis=0).astype(BF16)
    slots[own, :, EARLY:HALF] = jnp.concatenate([fc1[...].astype(F32), fc2[...].astype(F32)], axis=0).astype(BF16)
    net.enter()
    early = Gather(net, slots, own, 0, 256, EARLY)
    late = Gather(net, slots, own, EARLY, 896, HALF)
    early.one()

    wait(brought[4:7])
    row_cos, row_sin = angle_rows[0], angle_rows[1]
    block_cos, block_sin = angle_block[0, pl.ds(block, 1), :], angle_block[1, pl.ds(block, 1), :]
    cosine[...] = row_cos * block_cos - row_sin * block_sin
    sine = row_sin * block_cos + row_cos * block_sin
    upward = lanes((ROWS, TILE)) >= ROT // 2
    sine_up[...] = jnp.where(upward, sine, 0.0)
    sine_down[...] = jnp.where(upward, 0.0, -sine)

    early.two()
    late.one()
    mine_t = cot_t.at[pl.ds(pl.multiple_of(y * PART, 16), PART), :]
    gather_y = [net.copy(cot_own, mine_t, net.at_y(step)) for step in (1, 2, 3)]
    start(gather_y)
    mine_t[...] = cot_own[...]

    @pl.loop(0, 4)
    def _(index):
        rows = tile_at(index)
        normed, scale = standardize(tok[rows, :])
        xhat[rows, :] = normed
        rstd[rows, :] = jnp.broadcast_to(scale, (TILE, TILE))


    @pl.loop(0, 4)
    def _(index):
        rows = tile_at(index)
        tok_t[:, rows] = tok[rows, :].astype(F32).T.astype(BF16)

    early.three()
    dkv[...] = jnp.zeros_like(dkv)
    early.end()
    bias_rows[...] = jnp.zeros_like(bias_rows)

    @pl.loop(0, 16)
    def _(pair):
        rows = pl.ds(pl.multiple_of(pair * 48, 16), 48)
        one = slots[2 * pair, :, 0:EARLY].astype(F32)
        two = slots[2 * pair + 1, :, 0:EARLY].astype(F32)
        upper_rows = jnp.concatenate([one[0:24], two[0:24]], axis=0).astype(BF16)
        lower_rows = jnp.concatenate([one[24:48], two[24:48]], axis=0).astype(BF16)
        w2[rows, 0:384] = upper_rows[:, 0:384]
        w2[rows, 640:768] = upper_rows[:, 384:512]
        w2[rows, 384:640] = lower_rows[:, 0:256]
        w2[rows, 768:896] = lower_rows[:, 256:384]
        bias_rows[...] += one[24:48, 384:512] + two[24:48, 384:512]

    column_form = w2[:, 512:640].astype(F32)
    out_col[...] = jnp.broadcast_to(
        column_form[:, SMALL + 4 : SMALL + 5] + column_form[:, SMALL + 5 : SMALL + 6], (WIDE, TILE)
    )
    turned = column_form.T[SMALL : SMALL + 16, :]
    small[...] = turned
    even, odd = bias_rows[...], swap_halves(bias_rows[...])
    for number in range(6):
        bias[1:2, number * TILE : number * TILE + TILE] = (
            even[2 * number : 2 * number + 1] + odd[2 * number + 1 : 2 * number + 2]
        )
    for head in range(3):
        bias[0:1, head * TILE : head * TILE + TILE] = even[15 + head : 16 + head] + odd[18 + head : 19 + head]
    bias[0:1, 384:512] = even[12:13] + odd[13:14]
    bias[0:1, 512:640] = even[14:15]

    @pl.loop(0, 4)
    def _(index):
        rows = tile_at(index)
        normed = xhat[rows, :]
        one = (normed * small[0:1, :] + small[2:3, :]).astype(BF16)
        n1[rows, :] = one
        n2[rows, :] = (normed * small[1:2, :] + small[3:4, :]).astype(BF16)
        projected = dot(one, w2[:, QKV]) + bias[0:1, 0:640]
        turning = (cosine[rows, :], sine_up[rows, :], sine_down[rows, :])
        for head in range(3):
            span = slice(head * TILE, head * TILE + TILE)
            kv[block, rows, span] = turn(projected[:, span], *turning).astype(BF16)
        pair, last = projected[:, 384:512], projected[:, 512:640]
        for head, tile in enumerate((pair, swap_halves(pair), last)):
            span = slice(head * TILE, head * TILE + TILE)
            qd[rows, span] = (low_half(turn(low_half(tile), *turning)) * 0.125).astype(BF16)

    spans = [slice(head * TILE, head * TILE + TILE) for head in range(3)]
    send_own, send_prior, receive, given = [], [], [], []
    for step in (1, 2, 3):
        behind = z + step <= 3
        send_own.append(either(behind, both(lower, both(z + step == 4, z <= 2))))
        send_prior.append(both(upper, z + step > 3))
        receive.append(either(upper, either(z - step >= 0, both(z == 0, step >= 2))))
        given.append((z - step + 4) % 4 + 4 * xhi * ((z - step + 4) // 4))
    head_span = lambda head: pl.ds(pl.multiple_of(head * TILE, TILE), TILE)
    across_at, along_at, return_at, relay_at, part_at, stat_at, dq_at = (
        net.take(count) for count in (3, 9, 9, 3, 3, 3, 3)
    )

    def across(head):
        mine = kv.at[block, :, head_span(head)]
        return net.copy(mine, mine, net.at_x(2), across_at + head)

    def along(head, step):
        piece = kv.at[block - 4 * xhi * ((z + step + 1) // 4), :, head_span(head)]
        return net.copy(piece, piece, net.at_z(step + 1), along_at + 3 * head + step)

    @pl.loop(0, 3)
    def _(head):
        pl.when(lower)(across(head).start)
        for step in range(3):
            pl.when(send_own[step])(along(head, step).start)


    wait(gather_y)

    @pl.loop(0, 4)
    def _(index):
        rows = tile_at(index)
        cot[rows, :] = cot_t[:, rows].astype(F32).T.astype(BF16)

    out_sums = jnp.sum(cot_t[...].astype(F32), axis=1, keepdims=True)

    @pl.loop(0, 4)
    def _(index):
        rows = tile_at(index)
        d_heads = dot(cot[rows, :], w2[:, DENSE])
        pair, last = d_heads[:, 0:TILE], d_heads[:, TILE : 2 * TILE]
        for head, tile in enumerate((swap_halves(pair), pair, swap_halves(last))):
            qd[rows, spans[head]] = (qd[rows, spans[head]].astype(F32) + high_half(tile)).astype(BF16)

    lend = net.copy(qd, qd_in, net.pal())
    pl.when(helped)(lend.start)

    @pl.loop(0, 3)
    def _(head):
        pl.when(upper)(across(head).wait_recv)
        for step in range(3):
            pl.when(send_prior[step])(along(head, step).start)

    row_is_low = lax.broadcasted_iota(jnp.int32, (TILE, ROWS), 0) < HD
    lent_count = (1 - xhi) * (3 - z)
    chunk_count = 4 + xhi

    def chunk_place(index):
        which = (lent_count + 7 - index) // 8
        return which, index - lent_count * (1 - which) + xhi * z

    def partial(head):
        return net.copy(part_out.at[head], part_in.at[head], net.pal(), part_at + head)

    def stat_copy(head):
        return net.copy(stat.at[0, head], stat.at[1, head], net.pal(), stat_at + head)

    def dq_copy(head):
        return net.copy(dq_out.at[head], dq_in.at[head], net.pal(), dq_at + head)

    def outcome(target, head, which):
        target[head, 0:HD, :] = summed[which, HD:TILE, :]
        target[head, HD : HD + 8, :] = top[which]
        target[head, HD + 8 : HD + 16, :] = jnp.broadcast_to(column_sum(totals[which]), (8, ROWS))

    @pl.when(jnp.logical_not(helped))
    def _():
        part_in[...] = jnp.zeros_like(part_in)
        part_in[:, HD : HD + 8, :] = jnp.full((3, 8, ROWS), -1e30, F32)
        dq_in[...] = jnp.zeros_like(dq_in)

    pl.when(helps)(lend.wait_recv)

    @pl.loop(0, 3)
    def _(head):
        span = head_span(head)
        pl.when(lower)(across(head).wait_send)
        for step in range(3):
            pl.when(receive[step])(along(head, step).wait_recv)

        def turn_queries(source, which):
            turned = source[:, span].astype(F32).T
            qdt[which * 3 + head] = turned.astype(BF16)
            query_t[which] = jnp.where(row_is_low, turned, 0.0).astype(BF16)

        turn_queries(qd, 0)
        pl.when(helps)(lambda: turn_queries(qd_in, 1))
        top[...] = jnp.full_like(top, -1e30)
        totals[...] = jnp.zeros_like(totals)
        summed[...] = jnp.zeros_like(summed)

        @pl.loop(0, chunk_count)
        def _(index):
            which, at = chunk_place(index)
            chunk = head * 5 + index
            tile = kv[at, :, span]
            tile_t = tile.astype(F32).T.astype(BF16)
            kv_t[chunk] = tile_t
            key_shift = (at - block - which * (7 - 2 * block)) * ROWS
            parts = [slice(half * 256, half * 256 + 256) for half in (0, 1)]
            scores = [dot(tile, query_t[which, :, part]) for part in parts]
            before = [top[which, 0:1, part] for part in parts]
            old_total = [totals[which, :, part] for part in parts]
            old_sum = [summed[which, :, part] for part in parts]
            for half, part in enumerate(parts):
                score = scores[half]
                key_at = lax.broadcasted_iota(jnp.int32, score.shape, 0) + key_shift
                query_at = lax.broadcasted_iota(jnp.int32, score.shape, 1) + half * 256
                score = jnp.where(key_at <= query_at, score, -1e30)
                peak = jnp.maximum(before[half], jnp.max(score, axis=0, keepdims=True))
                weight = jnp.exp(score - peak)
                shrink = jnp.exp(before[half] - peak)
                rounded = weight.astype(BF16)
                weights[chunk, :, part] = rounded
                peaks = jnp.broadcast_to(peak, (8, 256))
                tops[chunk, :, part] = peaks
                top[which, :, part] = peaks
                totals[which, :, part] = old_total[half] * shrink + fold(weight)
                summed[which, :, part] = old_sum[half] * shrink + dot(tile_t, rounded)

            @pl.when(both(helps, index == lent_count - 1))
            def _():
                outcome(part_out, head, 1)
                partial(head).start()

        outcome(kept, head, 0)
        pl.when(head == 1)(late.two)

    @pl.loop(0, 3)
    def _(head):
        pl.when(helped)(partial(head).wait_recv)
        top_one, top_two = kept[head, HD : HD + 1, :], part_in[head, HD : HD + 1, :]
        peak = jnp.maximum(top_one, top_two)
        share_one, share_two = jnp.exp(top_one - peak), jnp.exp(top_two - peak)
        total = kept[head, HD + 8 : HD + 9, :] * share_one + part_in[head, HD + 8 : HD + 9, :] * share_two
        inverse = 1.0 / total
        result = (kept[head, 0:HD, :] * share_one + part_in[head, 0:HD, :] * share_two) * inverse
        delta = column_sum(qdt[head, HD:TILE, :].astype(F32) * result)
        kept[head, 0:HD, :] = result
        stat[0, head, 0:8, :] = jnp.broadcast_to(peak, (8, ROWS))
        stat[0, head, 8:16, :] = jnp.broadcast_to(inverse, (8, ROWS))
        stat[0, head, 16:24, :] = jnp.broadcast_to(delta, (8, ROWS))
        pl.when(helped)(stat_copy(head).start)

    heads[:, 0:TILE] = jnp.concatenate([kept[0, 0:HD, :], kept[1, 0:HD, :]], axis=0).T.astype(BF16)
    heads[:, TILE : 2 * TILE] = jnp.concatenate(
        [kept[2, 0:HD, :], jnp.zeros((HD, ROWS), F32)], axis=0
    ).T.astype(BF16)
    late.three()

    def give_back(head, step):
        return net.copy(
            dkv.at[given[step], :, head_span(head)],
            from_z.at[step, :, head_span(head)],
            net.at_z(3 - step),
            return_at + 3 * head + step,
        )

    def relay_copy(head):
        return net.copy(to_x.at[:, head_span(head)], from_x.at[:, head_span(head)], net.at_x(2), relay_at + head)

    def relay(head):
        span = head_span(head)
        for step in range(3):
            pl.when(either(send_own[step], send_prior[step]))(give_back(head, step).wait_recv)

        @pl.when(upper)
        def _():
            total_kv[:, span] = dkv[z, :, span].astype(F32)
            for step in range(3):

                @pl.when(send_prior[step])
                def _():
                    total_kv[:, span] += from_z[step, :, span].astype(F32)

            to_x[:, span] = total_kv[:, span].astype(BF16)
            relay_copy(head).start()

    @pl.loop(0, 3)
    def _(head):
        span = head_span(head)
        query_n[0] = low_half(qd[:, span].astype(F32)).astype(BF16)

        @pl.when(helps)
        def _():
            query_n[1] = low_half(qd_in[:, span].astype(F32)).astype(BF16)

        summed[...] = jnp.zeros_like(summed)

        @pl.loop(0, chunk_count)
        def _(turn_of):
            index = (turn_of + lent_count) % chunk_count
            which, at = chunk_place(index)
            chunk = head * 5 + index
            pl.when(both(helps, turn_of == chunk_count - lent_count))(stat_copy(head).wait_recv)
            change = dkv[at, :, span].astype(F32)
            for half in (0, 1):
                part = slice(half * 256, half * 256 + 256)
                factor = jnp.exp(tops[chunk, 0:1, part] - stat[which, head, 0:1, part]) * stat[which, head, 8:9, part]
                weight = weights[chunk, :, part]
                scaled = jnp.where(
                    row_is_low[:, 0:256], 0.0, qdt[which * 3 + head, :, part].astype(F32) * factor
                )
                d_weight = dot(kv[at, :, span], scaled.astype(BF16))
                d_score = (
                    weight.astype(F32) * (d_weight - stat[which, head, 16:17, part] * factor)
                ).astype(BF16)
                change = change + dot(d_score, query_n[which, part, :]) + dot(weight, scaled.T.astype(BF16))
                summed[which, :, part] += dot(kv_t[chunk], d_score)
            dkv[at, :, span] = change.astype(BF16)

        dq_t[head] = summed[0, 0:HD, :]

        @pl.when(helps)
        def _():
            dq_out[head] = summed[1, 0:HD, :].astype(BF16)
            dq_copy(head).start()

        for step in range(3):
            pl.when(receive[step])(give_back(head, step).start)
        pl.when(head > 0)(lambda: relay(head - 1))

    late.end()

    @pl.loop(0, 16)
    def _(pair):
        rows = pl.ds(pl.multiple_of(pair * 48, 16), 48)
        one = slots[2 * pair, :, EARLY:HALF].astype(F32)
        two = slots[2 * pair + 1, :, EARLY:HALF].astype(F32)
        w2[rows, FC1] = jnp.concatenate([one[0:24], two[0:24]], axis=0).astype(BF16)
        w2[rows, FC2] = jnp.concatenate([one[24:48], two[24:48]], axis=0).astype(BF16)

    srow[...] = jnp.zeros_like(srow)

    @pl.loop(0, 4)
    def _(index):
        rows = tile_at(index)
        hidden = dot(n2[rows, :], w2[:, FC1]) + bias[1:2, :]
        spread_to = 0.5 + 0.5 * lax.erf(hidden * (0.5**0.5))
        act[rows, :] = (hidden * spread_to).astype(BF16)
        slope = spread_to + hidden * jnp.exp(-0.5 * hidden * hidden) * 0.3989422804014327
        d_hidden = (slope * dot(cot[rows, :], w2[:, FC2])).astype(BF16)
        dhid[rows, :] = d_hidden
        d_norm = dot_nt(d_hidden, w2[:, FC1])
        normed = xhat[rows, :]
        dx2[rows, :] = norm_back(small[1:2, :] * d_norm, normed, rstd[rows, 0:1])
        srow[0:8, :] += fold(d_norm * normed)
        srow[8:16, :] += fold(d_norm)
        srow[16:24, :] += fold(d_hidden.astype(F32))

    relay(2)

    for half in (0, 1):
        span = slice(half * 384, half * 384 + 384)
        mlp_t[span, :] = dot_nt(w2[span, FC2], act[...])
        gq[0:384, 0:WIDE] = dot_tn(n2[:, span], dhid[...])
        gq[384:768, 0:WIDE] = dot(cot_t[span, :], act[...])

        @pl.loop(0, 16)
        def _(index):
            first = pl.ds(pl.multiple_of(index * 24, 8), 24)
            second = pl.ds(pl.multiple_of(384 + index * 24, 8), 24)
            slots[half * 16 + index, :, EARLY:HALF] = jnp.concatenate(
                [gq[first, 0:WIDE], gq[second, 0:WIDE]], axis=0
            ).astype(BF16)

    fc_sum = Reduce(
        net, slots, EARLY, 896, HALF, twin_in, halves, late_a, late_b, late_sa, late_sb, late_ea, late_eb
    )
    fc_sum.one()

    for half in (0, 1):
        span = slice(half * 384, half * 384 + 384)
        out_send[span, :] = (mlp_t[span, :] + dot_nt(w2[span, DENSE], heads[...])).astype(BF16)
        gq[span, DENSE] = dot(cot_t[span, :], heads[...])

    def part_of(number):
        return pl.ds(pl.multiple_of(number * PART, 16), PART)

    out_copies = [
        net.copy(out_send.at[part_of((y + step) % 4), :], out_recv.at[step - 1], net.at_y(step))
        for step in (1, 2, 3)
    ]
    start(out_copies)


    @pl.loop(0, 3)
    def _(head):
        pl.when(helped)(dq_copy(head).wait_recv)
        pl.when(lower)(relay_copy(head).wait_recv)

    total_kv[...] = dkv[block].astype(F32)
    for step in range(3):

        @pl.when(send_own[step])
        def _():
            total_kv[...] += from_z[step].astype(F32)

    @pl.when(lower)
    def _():
        total_kv[...] += from_x[...].astype(F32)

    fc_sum.two()
    rowsum[...] = jnp.zeros_like(rowsum)

    @pl.loop(0, 4)
    def _(index):
        rows = tile_at(index)
        turning = (cosine[rows, :], -sine_up[rows, :], -sine_down[rows, :])
        pieces = [turn(total_kv[rows, spans[head]], *turning) for head in range(3)]
        query = []
        for head in range(3):
            grad = (dq_t[head, :, rows] + dq_in[head, :, rows].astype(F32)) * 0.125
            grad = jnp.concatenate([grad, jnp.zeros((HD, TILE), F32)], axis=0).T
            query.append(turn(grad, *turning))
        pieces.append(low_half(query[0]) + swap_halves(low_half(query[1])))
        pieces.append(low_half(query[2]))
        stacked = jnp.concatenate(pieces, axis=1).astype(BF16)
        dqkv[rows, :] = stacked
        d_norm = dot_nt(stacked, w2[:, QKV])
        normed = xhat[rows, :]
        d_input = dx2[rows, :] + norm_back(small[0:1, :] * d_norm, normed, rstd[rows, 0:1])
        rowsum[0:8, :] += fold(d_norm * normed)
        rowsum[8:16, :] += fold(d_norm)
        rowsum[16:24, 0:640] += fold(stacked.astype(F32))
        dx_send[:, rows] = d_input.T.astype(BF16)

    dx_copies = [
        net.copy(dx_send.at[part_of((y + step) % 4), :], dx_recv.at[step - 1], net.at_y(step))
        for step in (1, 2, 3)
    ]

    def whole(ref, at):
        return column_sum(ref[at : at + 8, :])

    y_send[...] = jnp.concatenate(
        [whole(rowsum, 0), whole(srow, 0), whole(rowsum, 8), whole(srow, 8), jnp.zeros((4, WIDE), F32)], axis=0
    )
    y_copies = [net.copy(y_send, y_recv.at[step - 1], net.at_y(step)) for step in (1, 2, 3)]
    start(y_copies + dx_copies)
    for half in (0, 1):
        span = slice(half * 384, half * 384 + 384)
        gq[span, QKV] = dot_tn(n1[:, span], dqkv[...])
    fc1_sum, qkv_total = whole(srow, 16), whole(rowsum, 16)
    pieces = []
    for number in range(12):
        pieces.append(fc1_sum[:, number // 2 * TILE : number // 2 * TILE + TILE])
    for number in (3, 3, 4, 0, 1, 2, 0, 1, 2):
        pieces.append(qkv_total[:, number * TILE : number * TILE + TILE])
    pieces.append(jnp.zeros((3, TILE), F32))
    bias_grads = jnp.concatenate(pieces, axis=0)
    row = lax.broadcasted_iota(jnp.int32, (24, TILE), 0)
    swapped = ((row < 12) & (row % 2 == 1)) | (row == 13) | (row >= 18)
    bias_rows[...] = jnp.where(swapped, swap_halves(bias_grads), bias_grads)
    wait(y_copies)
    shared = y_send[...] + y_recv[0] + y_recv[1] + y_recv[2]
    columns = jnp.concatenate(
        [
            jnp.zeros((SMALL, WIDE), F32),
            shared[0:4],
            jnp.zeros((2, WIDE), F32),
            jnp.zeros((58, WIDE), F32),
        ],
        axis=0,
    ).T
    lane = lanes((WIDE, TILE))
    columns = jnp.where((lane == SMALL + 4) | (lane == SMALL + 5), out_sums, columns)
    gq[:, 512:640] = jnp.where(lane < HD, gq[:, 512:640], columns)

    @pl.loop(0, 32)
    def _(index):
        rows = pl.ds(pl.multiple_of(index * 24, 8), 24)
        first = jnp.concatenate([gq[rows, 0:384], gq[rows, 640:768]], axis=1)
        second = jnp.concatenate([gq[rows, 384:640], gq[rows, 768:896], bias_rows[...]], axis=1)
        slots[index, :, 0:EARLY] = jnp.concatenate([first, second], axis=0).astype(BF16)

    fc_sum.three()
    qkv_sum = Reduce(
        net, slots, 0, 256, EARLY, twin_in, halves, early_a, early_b, early_sa, early_sb, early_ea, early_eb
    )
    qkv_sum.one()
    qkv_sum.two()

    wait(out_copies + dx_copies)
    mine = part_of(y)
    total = out_send[mine, :].astype(F32) + tok_t[mine, :].astype(F32) + out_col[mine, 0:1]
    grad = dx_send[mine, :].astype(F32) + cot_own[...].astype(F32)
    for step in range(3):
        total = total + out_recv[step].astype(F32)
        grad = grad + dx_recv[step].astype(F32)
    out_t[...] = total.astype(BF16)
    grad_t[...] = grad
    qkv_sum.three()

    @pl.loop(0, 3)
    def _(head):
        pl.when(helps)(partial(head).wait_send)
        pl.when(helped)(stat_copy(head).wait_send)
        pl.when(helps)(dq_copy(head).wait_send)
        pl.when(upper)(relay_copy(head).wait_send)
        for step in range(3):
            pl.when(either(send_own[step], send_prior[step]))(along(head, step).wait_send)
            pl.when(receive[step])(give_back(head, step).wait_send)

    pl.when(helped)(lend.wait_send)
    fc_sum.end(final)
    qkv_sum.end(final)


def finish_kernel(
    out_in, grad_in, final, out_t, grad_t, gain, shift, qkv, qkv_small, dense, fc1, fc1_small, fc2, outs
):
    out_t[...] = out_in[...]
    grad_t[...] = grad_in[...]
    fc1[...] = final[0:24, EARLY:HALF]
    fc2[...] = final[24:48, EARLY:HALF]
    left = lanes((24, TILE)) < HD
    one, two, three = (final[0:24, head * TILE : head * TILE + TILE] for head in range(3))
    qkv[1, :, 0:TILE] = jnp.where(left, one, swap_halves(two))
    qkv[1, :, TILE:PART] = three[:, 0:HD]
    qkv[2, :, 0:TILE] = jnp.where(left, swap_halves(one), two)
    qkv[2, :, TILE:PART] = swap_halves(three)[:, 0:HD]
    qkv[0, :, 0:TILE] = final[24:48, 0:TILE]
    mixed = final[24:48, TILE : 2 * TILE]
    qkv[0, :, TILE:PART] = mixed[:, 0:HD]
    dense[:, 0:TILE] = final[0:24, 384:512]
    dense[:, TILE:PART] = final[24:48, 256 : 256 + HD]
    rows = jnp.concatenate([mixed, jnp.zeros((TILE - 24, TILE), F32)], axis=0).T
    gain[...] = rows[SMALL : SMALL + 2, 0:24]
    shift[...] = rows[SMALL + 2 : SMALL + 4, 0:24]
    outs[...] = rows[SMALL + 4 : SMALL + 6, 0:24]
    own = lax.axis_index("dp") * 8 + lax.axis_index("ctx")
    moved = pltpu.roll(final[24:48, 384:512], TILE - 2 * own, axis=1)
    rows = jnp.concatenate([moved, jnp.zeros((TILE - 24, TILE), F32)], axis=0).T
    fc1_small[...] = rows[0:2, 0:12]
    for which in range(3):
        qkv_small[which] = pltpu.roll(rows[0:8], TILE - 12 - 3 * which, axis=1)[0:2, 0:3]


def angle_tables():
    frequency = 10000.0 ** (-2.0 * np.arange(ROT // 2) / ROT)
    result = []
    for positions in (np.arange(ROWS), ROWS * np.arange(8)):
        phases = np.zeros((len(positions), TILE))
        phases[:, 0:ROT] = positions[:, None] * np.concatenate([frequency, frequency])[None, :]
        result.append(np.stack([np.cos(phases), np.sin(phases)]).astype(np.float32))
    return result


def call(kernel, name, shapes, scratch, collective, inputs, outside=()):
    options = dict(vmem_limit_bytes=VMEM_LIMIT)
    if collective is not None:
        options.update(collective_id=collective, has_side_effects=True)
    return pl.pallas_call(
        kernel,
        name=name,
        out_shape=[jax.ShapeDtypeStruct(shape, kind) for shape, kind in shapes],
        in_specs=[
            pl.BlockSpec(memory_space=pl.ANY if number in outside else pltpu.VMEM)
            for number in range(len(inputs))
        ],
        out_specs=[pl.BlockSpec(memory_space=pltpu.VMEM)] * len(shapes),
        scratch_shapes=scratch,
        compiler_params=pltpu.CompilerParams(**options),
    )(*inputs)


def shards(
    tokens,
    norm_gain,
    norm_bias,
    qkv_weight,
    qkv_bias,
    dense_weight,
    fc1_weight,
    fc1_bias,
    fc2_weight,
    out_bias,
    cotangent,
):
    vm = pltpu.VMEM
    dma = pltpu.SemaphoreType.DMA
    wide = (ROWS, WIDE)
    row_angles, block_angles = angle_tables()
    out_t, grad_t, final = call(
        layer_kernel,
        "layer",
        [((PART, ROWS), BF16), ((PART, ROWS), F32), ((48, HALF), F32)],
        [
            vm(wide, BF16),
            vm((3, 24, PART), BF16),
            vm((24, PART), BF16),
            vm((24, WIDE), BF16),
            vm((24, WIDE), BF16),
            vm((PART, ROWS), BF16),
            vm((2, ROWS, TILE), F32),
            dma((7,)),
            vm((32, 48, HALF), BF16),
            vm((WIDE, 2432), BF16),
            vm((16, WIDE), F32),
            vm((8, WIDE), F32),
            vm((TILE, TILE), F32),
            vm((4, 24, TILE), F32),
            vm((24, TILE), F32),
            vm((WIDE, TILE), F32),
            vm((ROWS, TILE), F32),
            vm((ROWS, TILE), F32),
            vm((ROWS, TILE), F32),
            vm(wide, F32),
            vm((ROWS, TILE), F32),
            vm((WIDE, ROWS), BF16),
            vm(wide, BF16),
            vm(wide, BF16),
            vm(wide, BF16),
            vm(wide, BF16),
            vm((WIDE, ROWS), BF16),
            vm(wide, BF16),
            vm((WIDE, ROWS), F32),
            vm(wide, F32),
            vm((24, WIDE), F32),
            vm((ROWS, 384), BF16),
            vm((ROWS, 384), BF16),
            vm((6, TILE, ROWS), BF16),
            vm((8, ROWS, 384), BF16),
            vm((8, ROWS, 384), BF16),
            vm((15, TILE, ROWS), BF16),
            vm((15, ROWS, ROWS), BF16),
            vm((15, 8, ROWS), F32),
            vm((2, 8, ROWS), F32),
            vm((2, 8, ROWS), F32),
            vm((2, TILE, ROWS), F32),
            vm((2, TILE, ROWS), BF16),
            vm((2, ROWS, TILE), BF16),
            vm((3, 80, ROWS), F32),
            vm((3, 80, ROWS), F32),
            vm((2, 3, 24, ROWS), F32),
            vm((3, HD, ROWS), BF16),
            vm((3, HD, ROWS), BF16),
            vm((3, 80, ROWS), F32),
            vm((WIDE, 896), F32),
            vm((16, 48, HALF), BF16),
            vm((16, 48, HALF), BF16),
            vm((3, 4, 48, 256), BF16),
            vm((3, 4, 48, 256), BF16),
            vm((4, 48, 256), BF16),
            vm((4, 48, 256), BF16),
            vm((3, 48, 256), BF16),
            vm((3, 48, 256), BF16),
            vm((3, 4, 48, 384), BF16),
            vm((3, 4, 48, 384), BF16),
            vm((4, 48, 384), BF16),
            vm((4, 48, 384), BF16),
            vm((3, 48, 384), BF16),
            vm((3, 48, 384), BF16),
            vm((3, ROWS, 384), BF16),
            vm((ROWS, 384), BF16),
            vm((ROWS, 384), BF16),
            vm((ROWS, 256), BF16),
            vm((WIDE, ROWS), BF16),
            vm((3, PART, ROWS), BF16),
            vm((WIDE, ROWS), BF16),
            vm((3, PART, ROWS), BF16),
            vm((24, WIDE), F32),
            vm((8, WIDE), F32),
            vm((3, 8, WIDE), F32),
            dma((144,)),
            dma((144,)),
        ],
        0,
        [
            tokens[0],
            norm_gain,
            norm_bias,
            out_bias,
            jnp.transpose(qkv_weight, (1, 0, 2)),
            jnp.transpose(qkv_bias, (0, 2, 1)),
            dense_weight.T,
            fc1_weight,
            fc1_bias.T,
            fc2_weight.T,
            cotangent[0].T,
            jnp.asarray(row_angles),
            jnp.asarray(block_angles),
        ],
        (0, 4, 6, 7, 9, 10, 11),
    )
    out_t, grad_t, gain, shift, qkv, qkv_small, dense, fc1, fc1_small, fc2, outs = call(
        finish_kernel,
        "finish",
        [
            ((PART, ROWS), BF16),
            ((PART, ROWS), F32),
            ((2, 24), F32),
            ((2, 24), F32),
            ((3, 24, PART), F32),
            ((3, 2, 3), F32),
            ((24, PART), F32),
            ((24, WIDE), F32),
            ((2, 12), F32),
            ((24, WIDE), F32),
            ((2, 24), F32),
        ],
        [],
        None,
        [out_t, grad_t, final],
    )
    return (
        out_t.T[None],
        grad_t.T[None],
        gain,
        shift,
        jnp.transpose(qkv, (1, 0, 2)),
        jnp.transpose(qkv_small, (0, 2, 1)),
        dense.T,
        fc1,
        fc1_small.T,
        fc2.T,
        outs,
    )


def solution(mesh):
    return jax.shard_map(
        shards,
        mesh=mesh,
        in_specs=(
            P("dp", "ctx", None),
            P(None, ("dp", "ctx")),
            P(None, ("dp", "ctx")),
            P(("dp", "ctx"), None, "tensor"),
            P(None, "tensor", ("dp", "ctx")),
            P("tensor", ("dp", "ctx")),
            P(("dp", "ctx"), "tensor"),
            P("tensor", ("dp", "ctx")),
            P("tensor", ("dp", "ctx")),
            P(None, ("dp", "ctx")),
            P("dp", "ctx", "tensor"),
        ),
        out_specs=(
            P("dp", "ctx", "tensor"),
            P("dp", "ctx", "tensor"),
            P(None, ("dp", "ctx")),
            P(None, ("dp", "ctx")),
            P(("dp", "ctx"), None, "tensor"),
            P(None, "tensor", ("dp", "ctx")),
            P("tensor", ("dp", "ctx")),
            P(("dp", "ctx"), "tensor"),
            P("tensor", ("dp", "ctx")),
            P("tensor", ("dp", "ctx")),
            P(None, ("dp", "ctx")),
        ),
        check_vma=False,
    )
```

```python
import jax
import jax.numpy as jnp
import numpy as np
from jax import lax
from jax.experimental import pallas as pl
from jax.experimental.pallas import tpu as pltpu
from jax.sharding import PartitionSpec as P

HD = 64
ROT = 16
EPSILON = 1e-05
ROWS = 512
WIDE = 768
HALF = 1280
PART = 192
TILE = 128
MESH = pl.DeviceIdType.MESH
VMEM_LIMIT = 61 << 20
F32 = jnp.float32
BF16 = jnp.bfloat16

QKV = slice(0, 640)
DENSE = slice(640, 896)
FC1 = slice(896, 1664)
FC2 = slice(1664, 2432)
EARLY = 512
SMALL = 64


def dot(a, b):
    return lax.dot_general(a, b, (((1,), (0,)), ((), ())), preferred_element_type=F32)


def dot_nt(a, b):
    return lax.dot_general(a, b, (((1,), (1,)), ((), ())), preferred_element_type=F32)


def dot_tn(a, b):
    return lax.dot_general(a, b, (((0,), (0,)), ((), ())), preferred_element_type=F32)


def device(x, y, z, core):
    return {"dp": (x % 2) * 2 + core, "ctx": (x // 2) * 4 + z, "tensor": y}


class Links:
    def __init__(self, send, recv):
        dp = lax.axis_index("dp")
        cx = lax.axis_index("ctx")
        self.xlo, self.core, self.xhi, self.z = dp // 2, dp % 2, cx // 4, cx % 4
        self.y = lax.axis_index("tensor")
        self.x = self.xhi * 2 + self.xlo
        self.send, self.recv, self.used = send, recv, 0

    def at_x(self, step):
        return device((self.x + step) % 4, self.y, self.z, self.core)

    def at_z(self, step):
        return device(self.x, self.y, (self.z + step) % 4, self.core)

    def at_y(self, step):
        return device(self.x, (self.y + step) % 4, self.z, self.core)

    def twin(self):
        return device(self.x, self.y, self.z, 1 - self.core)

    def pal(self):
        return device((self.x + 2) % 4, self.y, 3 - self.z, self.core)

    def knock(self):
        self.barrier = pltpu.get_barrier_semaphore()
        peers = [self.twin(), self.pal()]
        for step in (1, 2, 3):
            peers += [self.at_x(step), self.at_z(step), self.at_y(step)]
        for peer in peers:
            pl.semaphore_signal(self.barrier, inc=1, device_id=peer, device_id_type=MESH)
        self.expected = len(peers)

    def enter(self):
        pl.semaphore_wait(self.barrier, self.expected)

    def take(self, count):
        self.used += count
        return self.used - count

    def copy(self, source, target, peer, number=None):
        if number is None:
            number = self.take(1)
        return pltpu.make_async_remote_copy(
            src_ref=source,
            dst_ref=target,
            send_sem=self.send.at[number],
            recv_sem=self.recv.at[number],
            device_id=peer,
            device_id_type=MESH,
        )


def start(copies):
    for item in copies:
        item.start()


def wait(copies):
    for item in copies:
        item.wait()


def lanes(shape):
    return lax.broadcasted_iota(jnp.int32, shape, len(shape) - 1)


def low_half(tile):
    return jnp.where(lanes(tile.shape) < HD, tile, 0.0)


def high_half(tile):
    return jnp.where(lanes(tile.shape) >= HD, tile, 0.0)


def swap_halves(tile):
    return pltpu.roll(tile, HD, axis=1)


def turn(tile, cosine, sine_up, sine_down):
    return (
        tile * cosine
        + pltpu.roll(tile, ROT // 2, axis=1) * sine_up
        + pltpu.roll(tile, TILE - ROT // 2, axis=1) * sine_down
    )


def fold(block):
    rows, width = block.shape
    return jnp.sum(block.reshape(rows // 8, 8, width), axis=0)


def column_sum(block):
    return jnp.sum(block, axis=0, keepdims=True)


def standardize(rows_in):
    values = rows_in.astype(F32)
    centred = values - jnp.mean(values, axis=-1, keepdims=True)
    scale = lax.rsqrt(jnp.mean(centred * centred, axis=-1, keepdims=True) + EPSILON)
    return centred * scale, scale


def norm_back(gradient, xhat, scale):
    return scale * (
        gradient
        - jnp.mean(gradient, axis=-1, keepdims=True)
        - xhat * jnp.mean(gradient * xhat, axis=-1, keepdims=True)
    )


def tile_at(index):
    return pl.ds(pl.multiple_of(index * TILE, TILE), TILE)


def quad(position):
    return (position % 2) * 2 + position // 2


class Gather:
    def __init__(self, net, slots, own, low, middle, high):
        first, second = slice(low, middle), slice(middle, high)
        mine_a, mine_b = slots.at[own, :, first], slots.at[own, :, second]
        four = slots.at[pl.ds(own - net.z, 4), :, first]
        steps = (1, 2, 3)
        self.a = [net.copy(mine_a, mine_a, net.at_z(step)) for step in steps]
        self.b = [net.copy(mine_b, mine_b, net.at_x(step)) for step in steps]
        self.mid_a = [net.copy(four, four, net.at_x(step)) for step in steps]
        self.mid_b, self.last_a, self.last_b = [], [], []
        for low in (0, 1):
            for high in (0, 1):
                piece = slots.at[((low * 2 + net.core) * 2 + high) * 4 + net.z, :, second]
                self.mid_b += [net.copy(piece, piece, net.at_z(step)) for step in steps]
            for span, copies in ((first, self.last_a), (second, self.last_b)):
                piece = slots.at[pl.ds((low * 2 + net.core) * 8, 8), :, span]
                copies.append(net.copy(piece, piece, net.twin()))

    def one(self):
        start(self.a + self.b)

    def two(self):
        wait(self.a)
        start(self.mid_a)
        wait(self.b)
        start(self.mid_b)

    def three(self):
        wait(self.mid_a)
        start(self.last_a)
        wait(self.mid_b)
        start(self.last_b)

    def end(self):
        wait(self.last_a + self.last_b)


class Reduce:
    def __init__(self, net, slots, low, middle, high, twin_in, halves, in_a, in_b, sum_a, sum_b, end_a, end_b):
        self.net, self.slots = net, slots
        self.whole, self.first, self.second = slice(low, high), slice(low, middle), slice(middle, high)
        self.bufs = (twin_in, halves, in_a, in_b, sum_a, sum_b, end_a, end_b)
        self.me = quad(net.x)
        self.twins = [
            net.copy(
                slots.at[pl.ds((low * 2 + 1 - net.core) * 8, 8), :, self.whole],
                twin_in.at[pl.ds(low * 8, 8), :, self.whole],
                net.twin(),
            )
            for low in (0, 1)
        ]
        self.mid_a, self.mid_b, self.last_a, self.last_b = [], [], [], []
        for step in (1, 2, 3):
            there = quad((net.x + step) % 4)
            self.mid_a.append(
                net.copy(halves.at[pl.ds(there * 4, 4), :, self.first], in_a.at[step - 1], net.at_x(step))
            )
            for which in range(4):
                self.mid_b.append(
                    net.copy(
                        halves.at[which * 4 + (net.z + step) % 4, :, self.second],
                        in_b.at[step - 1, which],
                        net.at_z(step),
                    )
                )
            self.last_a.append(net.copy(sum_a.at[(net.z + step) % 4], end_a.at[step - 1], net.at_z(step)))
            self.last_b.append(net.copy(sum_b.at[there], end_b.at[step - 1], net.at_x(step)))

    def one(self):
        start(self.twins)

    def two(self):
        twin_in, halves = self.bufs[:2]
        wait(self.twins)

        @pl.loop(0, 16)
        def _(index):
            source = (index // 8 * 2 + self.net.core) * 8 + index % 8
            halves[index, :, self.whole] = (
                self.slots[source, :, self.whole].astype(F32) + twin_in[index, :, self.whole].astype(F32)
            ).astype(BF16)

        start(self.mid_a + self.mid_b)

    def three(self):
        halves, in_a, in_b, sum_a, sum_b = self.bufs[1:6]
        wait(self.mid_a)

        @pl.loop(0, 4)
        def _(index):
            total = halves[self.me * 4 + index, :, self.first].astype(F32)
            for step in range(3):
                total = total + in_a[step, index].astype(F32)
            sum_a[index] = total.astype(BF16)

        start(self.last_a)
        wait(self.mid_b)

        @pl.loop(0, 4)
        def _(index):
            total = halves[index * 4 + self.net.z, :, self.second].astype(F32)
            for step in range(3):
                total = total + in_b[step, index].astype(F32)
            sum_b[index] = total.astype(BF16)

        start(self.last_b)

    def end(self, target):
        sum_a, sum_b, end_a, end_b = self.bufs[4:]
        for copies, own, arrived, span in (
            (self.last_a, sum_a.at[self.net.z], end_a, self.first),
            (self.last_b, sum_b.at[self.me], end_b, self.second),
        ):
            wait(copies)
            total = own[...].astype(F32)
            for step in range(3):
                total = total + arrived[step].astype(F32)
            target[:, span] = total


def layer_kernel(
    tok_in, gains, shifts, outs, qkv_in, qkv_small, dense_in, fc1_in, fc1_small, fc2_in, cot_in, angle_in, angle_block,
    out_t, grad_t, final,
    tok, qkv, dense, fc1, fc2, cot_own, angle_rows, loads,
    slots, w2, small, bias, small_rows, narrow, bias_rows, out_col, cosine, sine_up, sine_down, xhat, rstd, tok_t, n1, n2, dhid, act,
    cot_t, cot, mlp_t, dx2, srow, qd, qd_in, qdt, kv, dkv, kv_t, weights, tops, top, totals, summed, query_t, query_n,
    part_out, part_in, stat, dq_out, dq_in, dq_t, kept, gq,
    twin_in, halves, early_a, early_b, early_sa, early_sb, early_ea, early_eb,
    late_a, late_b, late_sa, late_sb, late_ea, late_eb,
    from_z, from_x, to_x, heads, out_send, out_recv, dx_send, dx_recv, rowsum, y_send, y_recv,
    send, recv,
):
    net = Links(send, recv)
    xlo, core, xhi, z, y = net.xlo, net.core, net.xhi, net.z, net.y
    own = ((xlo * 2 + core) * 2 + xhi) * 4 + z
    block = xhi * 4 + z
    upper, lower = xhi == 1, xhi == 0
    both = jnp.logical_and
    either = jnp.logical_or
    brought = [
        pltpu.make_async_copy(source, target, loads.at[number])
        for number, (source, target) in enumerate(
            (
                (qkv_in, qkv),
                (dense_in, dense),
                (fc1_in, fc1),
                (fc2_in, fc2),
                (angle_in, angle_rows),
                (tok_in, tok),
                (cot_in, cot_own),
            )
        )
    ]
    start(brought)
    helps = both(lower, z <= 2)
    helped = both(upper, z >= 1)
    dqkv = n2.at[:, QKV]
    total_kv = gq.at[0:ROWS, 0:384]
    net.knock()

    wait(brought[0:4])
    narrow[...] = jnp.zeros_like(narrow)
    for which in range(3):
        narrow[which, :, 0:HD] = qkv[which, :, TILE:PART].astype(F32)
    narrow[3, :, 0:HD] = dense[:, TILE:PART].astype(F32)
    small_rows[...] = jnp.zeros_like(small_rows)
    small_rows[SMALL : SMALL + 2, 0:24] = gains[...].astype(F32)
    small_rows[SMALL + 2 : SMALL + 4, 0:24] = shifts[...].astype(F32)
    small_rows[SMALL + 4 : SMALL + 6, 0:24] = outs[...].astype(F32)
    columns = small_rows[...].T[0:24]

    small_rows[...] = jnp.zeros_like(small_rows)
    small_rows[0:2, 0:12] = fc1_small[...].astype(F32)
    for which in range(3):
        small_rows[8 + 8 * which : 10 + 8 * which, 0:3] = qkv_small[which].astype(F32)
    turned = small_rows[...].T[0:16]
    pair_lane = lanes((16, TILE)) < 2
    bias_rows[0:16, :] = jnp.where(pair_lane, turned, 0.0)
    bias_rows[16:24, :] = jnp.zeros((8, TILE), F32)
    for which in range(3):
        moved = pltpu.roll(turned, TILE - 8 - 8 * which, axis=1)
        bias_rows[12 + 3 * which : 15 + 3 * which, :] = jnp.where(pair_lane, moved, 0.0)[0:3]
    biases = pltpu.roll(bias_rows[...], 2 * own, axis=1)
    key = qkv[1, :, 0:TILE].astype(F32)
    value = qkv[2, :, 0:TILE].astype(F32)
    left = lanes((24, TILE)) < HD
    top_half = jnp.concatenate(
        [
            jnp.where(left, key, swap_halves(value)),
            jnp.where(left, swap_halves(key), value),
            narrow[1] + swap_halves(narrow[2]),
            dense[:, 0:TILE].astype(F32),
        ],
        axis=1,
    )
    bottom_half = jnp.concatenate(
        [qkv[0, :, 0:TILE].astype(F32), narrow[0] + columns, narrow[3], biases], axis=1
    )
    slots[own, :, 0:EARLY] = jnp.concatenate([top_half, bottom_half], axis=0).astype(BF16)
    slots[own, :, EARLY:HALF] = jnp.concatenate([fc1[...].astype(F32), fc2[...].astype(F32)], axis=0).astype(BF16)
    net.enter()
    early = Gather(net, slots, own, 0, 256, EARLY)
    late = Gather(net, slots, own, EARLY, 896, HALF)
    early.one()

    wait(brought[4:7])
    row_cos, row_sin = angle_rows[0], angle_rows[1]
    block_cos, block_sin = angle_block[0, pl.ds(block, 1), :], angle_block[1, pl.ds(block, 1), :]
    cosine[...] = row_cos * block_cos - row_sin * block_sin
    sine = row_sin * block_cos + row_cos * block_sin
    upward = lanes((ROWS, TILE)) >= ROT // 2
    sine_up[...] = jnp.where(upward, sine, 0.0)
    sine_down[...] = jnp.where(upward, 0.0, -sine)

    early.two()
    late.one()
    mine_t = cot_t.at[pl.ds(pl.multiple_of(y * PART, 16), PART), :]
    gather_y = [net.copy(cot_own, mine_t, net.at_y(step)) for step in (1, 2, 3)]
    start(gather_y)
    mine_t[...] = cot_own[...]

    @pl.loop(0, 4)
    def _(index):
        rows = tile_at(index)
        normed, scale = standardize(tok[rows, :])
        xhat[rows, :] = normed
        rstd[rows, :] = jnp.broadcast_to(scale, (TILE, TILE))


    @pl.loop(0, 4)
    def _(index):
        rows = tile_at(index)
        tok_t[:, rows] = tok[rows, :].astype(F32).T.astype(BF16)

    early.three()
    dkv[...] = jnp.zeros_like(dkv)
    early.end()
    bias_rows[...] = jnp.zeros_like(bias_rows)

    @pl.loop(0, 16)
    def _(pair):
        rows = pl.ds(pl.multiple_of(pair * 48, 16), 48)
        one = slots[2 * pair, :, 0:EARLY].astype(F32)
        two = slots[2 * pair + 1, :, 0:EARLY].astype(F32)
        upper_rows = jnp.concatenate([one[0:24], two[0:24]], axis=0).astype(BF16)
        lower_rows = jnp.concatenate([one[24:48], two[24:48]], axis=0).astype(BF16)
        w2[rows, 0:384] = upper_rows[:, 0:384]
        w2[rows, 640:768] = upper_rows[:, 384:512]
        w2[rows, 384:640] = lower_rows[:, 0:256]
        w2[rows, 768:896] = lower_rows[:, 256:384]
        bias_rows[...] += one[24:48, 384:512] + two[24:48, 384:512]

    column_form = w2[:, 512:640].astype(F32)
    out_col[...] = jnp.broadcast_to(
        column_form[:, SMALL + 4 : SMALL + 5] + column_form[:, SMALL + 5 : SMALL + 6], (WIDE, TILE)
    )
    turned = column_form.T[SMALL : SMALL + 16, :]
    small[...] = turned
    even, odd = bias_rows[...], swap_halves(bias_rows[...])
    for number in range(6):
        bias[1:2, number * TILE : number * TILE + TILE] = (
            even[2 * number : 2 * number + 1] + odd[2 * number + 1 : 2 * number + 2]
        )
    for head in range(3):
        bias[0:1, head * TILE : head * TILE + TILE] = even[15 + head : 16 + head] + odd[18 + head : 19 + head]
    bias[0:1, 384:512] = even[12:13] + odd[13:14]
    bias[0:1, 512:640] = even[14:15]

    @pl.loop(0, 4)
    def _(index):
        rows = tile_at(index)
        normed = xhat[rows, :]
        one = (normed * small[0:1, :] + small[2:3, :]).astype(BF16)
        n1[rows, :] = one
        n2[rows, :] = (normed * small[1:2, :] + small[3:4, :]).astype(BF16)
        projected = dot(one, w2[:, QKV]) + bias[0:1, 0:640]
        turning = (cosine[rows, :], sine_up[rows, :], sine_down[rows, :])
        for head in range(3):
            span = slice(head * TILE, head * TILE + TILE)
            kv[block, rows, span] = turn(projected[:, span], *turning).astype(BF16)
        pair, last = projected[:, 384:512], projected[:, 512:640]
        for head, tile in enumerate((pair, swap_halves(pair), last)):
            span = slice(head * TILE, head * TILE + TILE)
            qd[rows, span] = (low_half(turn(low_half(tile), *turning)) * 0.125).astype(BF16)

    spans = [slice(head * TILE, head * TILE + TILE) for head in range(3)]
    send_own, send_prior, receive, given = [], [], [], []
    for step in (1, 2, 3):
        behind = z + step <= 3
        send_own.append(either(behind, both(lower, both(z + step == 4, z <= 2))))
        send_prior.append(both(upper, z + step > 3))
        receive.append(either(upper, either(z - step >= 0, both(z == 0, step >= 2))))
        given.append((z - step + 4) % 4 + 4 * xhi * ((z - step + 4) // 4))
    head_span = lambda head: pl.ds(pl.multiple_of(head * TILE, TILE), TILE)
    across_at, along_at, return_at, relay_at, part_at, stat_at, dq_at = (
        net.take(count) for count in (3, 9, 9, 3, 3, 3, 3)
    )

    def across(head):
        mine = kv.at[block, :, head_span(head)]
        return net.copy(mine, mine, net.at_x(2), across_at + head)

    def along(head, step):
        piece = kv.at[block - 4 * xhi * ((z + step + 1) // 4), :, head_span(head)]
        return net.copy(piece, piece, net.at_z(step + 1), along_at + 3 * head + step)

    @pl.loop(0, 3)
    def _(head):
        pl.when(lower)(across(head).start)
        for step in range(3):
            pl.when(send_own[step])(along(head, step).start)


    wait(gather_y)

    @pl.loop(0, 4)
    def _(index):
        rows = tile_at(index)
        cot[rows, :] = cot_t[:, rows].astype(F32).T.astype(BF16)

    out_sums = jnp.sum(cot_t[...].astype(F32), axis=1, keepdims=True)

    @pl.loop(0, 4)
    def _(index):
        rows = tile_at(index)
        d_heads = dot(cot[rows, :], w2[:, DENSE])
        pair, last = d_heads[:, 0:TILE], d_heads[:, TILE : 2 * TILE]
        for head, tile in enumerate((swap_halves(pair), pair, swap_halves(last))):
            qd[rows, spans[head]] = (qd[rows, spans[head]].astype(F32) + high_half(tile)).astype(BF16)

    lend = net.copy(qd, qd_in, net.pal())
    pl.when(helped)(lend.start)

    @pl.loop(0, 3)
    def _(head):
        pl.when(upper)(across(head).wait_recv)
        for step in range(3):
            pl.when(send_prior[step])(along(head, step).start)

    row_is_low = lax.broadcasted_iota(jnp.int32, (TILE, ROWS), 0) < HD
    lent_count = (1 - xhi) * (3 - z)
    chunk_count = 4 + xhi

    def chunk_place(index):
        which = (lent_count + 7 - index) // 8
        return which, index - lent_count * (1 - which) + xhi * z

    def partial(head):
        return net.copy(part_out.at[head], part_in.at[head], net.pal(), part_at + head)

    def stat_copy(head):
        return net.copy(stat.at[0, head], stat.at[1, head], net.pal(), stat_at + head)

    def dq_copy(head):
        return net.copy(dq_out.at[head], dq_in.at[head], net.pal(), dq_at + head)

    def outcome(target, head, which):
        target[head, 0:HD, :] = summed[which, HD:TILE, :]
        target[head, HD : HD + 8, :] = top[which]
        target[head, HD + 8 : HD + 16, :] = jnp.broadcast_to(column_sum(totals[which]), (8, ROWS))

    @pl.when(jnp.logical_not(helped))
    def _():
        part_in[...] = jnp.zeros_like(part_in)
        part_in[:, HD : HD + 8, :] = jnp.full((3, 8, ROWS), -1e30, F32)
        dq_in[...] = jnp.zeros_like(dq_in)

    def ahead(head):
        span = head_span(head)
        pl.when(lower)(across(head).wait_send)
        for step in range(3):
            pl.when(receive[step])(along(head, step).wait_recv)

        def turn_queries(source, which):
            turned = source[:, span].astype(F32).T
            qdt[which * 3 + head] = turned.astype(BF16)
            query_t[which] = jnp.where(row_is_low, turned, 0.0).astype(BF16)

        turn_queries(qd, 0)
        top[...] = jnp.full_like(top, -1e30)
        totals[...] = jnp.zeros_like(totals)
        summed[...] = jnp.zeros_like(summed)

        @pl.loop(0, chunk_count)
        def _(turn_of):
            index = (turn_of + lent_count) % chunk_count

            @pl.when(both(helps, turn_of == chunk_count - lent_count))
            def _():
                pl.when(head == 0)(lend.wait_recv)
                turn_queries(qd_in, 1)

            which, at = chunk_place(index)
            chunk = head * 5 + index
            tile = kv[at, :, span]
            tile_t = tile.astype(F32).T.astype(BF16)
            kv_t[chunk] = tile_t
            key_shift = (at - block - which * (7 - 2 * block)) * ROWS
            parts = [slice(half * 256, half * 256 + 256) for half in (0, 1)]
            scores = [dot(tile, query_t[which, :, part]) for part in parts]
            before = [top[which, 0:1, part] for part in parts]
            old_total = [totals[which, :, part] for part in parts]
            old_sum = [summed[which, :, part] for part in parts]
            for half, part in enumerate(parts):
                score = scores[half]
                key_at = lax.broadcasted_iota(jnp.int32, score.shape, 0) + key_shift
                query_at = lax.broadcasted_iota(jnp.int32, score.shape, 1) + half * 256
                score = jnp.where(key_at <= query_at, score, -1e30)
                peak = jnp.maximum(before[half], jnp.max(score, axis=0, keepdims=True))
                weight = jnp.exp(score - peak)
                shrink = jnp.exp(before[half] - peak)
                rounded = weight.astype(BF16)
                weights[chunk, :, part] = rounded
                peaks = jnp.broadcast_to(peak, (8, 256))
                tops[chunk, :, part] = peaks
                top[which, :, part] = peaks
                totals[which, :, part] = old_total[half] * shrink + fold(weight)
                summed[which, :, part] = old_sum[half] * shrink + dot(tile_t, rounded)

            @pl.when(both(helps, turn_of == chunk_count - 1))
            def _():
                outcome(part_out, head, 1)
                partial(head).start()

        outcome(kept, head, 0)
        pl.when(head == 1)(late.two)

    def merge(head):
        pl.when(helped)(partial(head).wait_recv)
        top_one, top_two = kept[head, HD : HD + 1, :], part_in[head, HD : HD + 1, :]
        peak = jnp.maximum(top_one, top_two)
        share_one, share_two = jnp.exp(top_one - peak), jnp.exp(top_two - peak)
        total = kept[head, HD + 8 : HD + 9, :] * share_one + part_in[head, HD + 8 : HD + 9, :] * share_two
        inverse = 1.0 / total
        result = (kept[head, 0:HD, :] * share_one + part_in[head, 0:HD, :] * share_two) * inverse
        delta = column_sum(qdt[head, HD:TILE, :].astype(F32) * result)
        kept[head, 0:HD, :] = result
        stat[0, head, 0:8, :] = jnp.broadcast_to(peak, (8, ROWS))
        stat[0, head, 8:16, :] = jnp.broadcast_to(inverse, (8, ROWS))
        stat[0, head, 16:24, :] = jnp.broadcast_to(delta, (8, ROWS))
        pl.when(helped)(stat_copy(head).start)

    def give_back(head, step):
        return net.copy(
            dkv.at[given[step], :, head_span(head)],
            from_z.at[step, :, head_span(head)],
            net.at_z(3 - step),
            return_at + 3 * head + step,
        )

    def relay_copy(head):
        return net.copy(to_x.at[:, head_span(head)], from_x.at[:, head_span(head)], net.at_x(2), relay_at + head)

    def relay(head):
        span = head_span(head)
        for step in range(3):
            pl.when(either(send_own[step], send_prior[step]))(give_back(head, step).wait_recv)

        @pl.when(upper)
        def _():
            total_kv[:, span] = dkv[z, :, span].astype(F32)
            for step in range(3):

                @pl.when(send_prior[step])
                def _():
                    total_kv[:, span] += from_z[step, :, span].astype(F32)

            to_x[:, span] = total_kv[:, span].astype(BF16)
            relay_copy(head).start()

    def back(head):
        span = head_span(head)
        query_n[0] = low_half(qd[:, span].astype(F32)).astype(BF16)

        @pl.when(helps)
        def _():
            query_n[1] = low_half(qd_in[:, span].astype(F32)).astype(BF16)

        summed[...] = jnp.zeros_like(summed)

        @pl.loop(0, chunk_count)
        def _(turn_of):
            index = (turn_of + lent_count) % chunk_count
            which, at = chunk_place(index)
            chunk = head * 5 + index
            pl.when(both(helps, turn_of == chunk_count - lent_count))(stat_copy(head).wait_recv)
            change = dkv[at, :, span].astype(F32)
            for half in (0, 1):
                part = slice(half * 256, half * 256 + 256)
                factor = jnp.exp(tops[chunk, 0:1, part] - stat[which, head, 0:1, part]) * stat[which, head, 8:9, part]
                weight = weights[chunk, :, part]
                scaled = jnp.where(
                    row_is_low[:, 0:256], 0.0, qdt[which * 3 + head, :, part].astype(F32) * factor
                )
                d_weight = dot(kv[at, :, span], scaled.astype(BF16))
                d_score = (
                    weight.astype(F32) * (d_weight - stat[which, head, 16:17, part] * factor)
                ).astype(BF16)
                change = change + dot(d_score, query_n[which, part, :]) + dot(weight, scaled.T.astype(BF16))
                summed[which, :, part] += dot(kv_t[chunk], d_score)
            dkv[at, :, span] = change.astype(BF16)

        dq_t[head] = summed[0, 0:HD, :]

        @pl.when(helps)
        def _():
            dq_out[head] = summed[1, 0:HD, :].astype(BF16)
            dq_copy(head).start()

        for step in range(3):
            pl.when(receive[step])(give_back(head, step).start)

    @pl.loop(0, 4)
    def _(index):
        pl.when(index < 3)(lambda: ahead(index))
        pl.when(index == 3)(late.three)
        pl.when(index > 0)(lambda: back(index - 1))
        pl.when(index < 3)(lambda: merge(index))

    heads[:, 0:TILE] = jnp.concatenate([kept[0, 0:HD, :], kept[1, 0:HD, :]], axis=0).T.astype(BF16)
    heads[:, TILE : 2 * TILE] = jnp.concatenate(
        [kept[2, 0:HD, :], jnp.zeros((HD, ROWS), F32)], axis=0
    ).T.astype(BF16)


    late.end()

    @pl.loop(0, 16)
    def _(pair):
        rows = pl.ds(pl.multiple_of(pair * 48, 16), 48)
        one = slots[2 * pair, :, EARLY:HALF].astype(F32)
        two = slots[2 * pair + 1, :, EARLY:HALF].astype(F32)
        w2[rows, FC1] = jnp.concatenate([one[0:24], two[0:24]], axis=0).astype(BF16)
        w2[rows, FC2] = jnp.concatenate([one[24:48], two[24:48]], axis=0).astype(BF16)

    relay(0)
    srow[...] = jnp.zeros_like(srow)

    @pl.loop(0, 4)
    def _(index):
        rows = tile_at(index)
        hidden = dot(n2[rows, :], w2[:, FC1]) + bias[1:2, :]
        spread_to = 0.5 + 0.5 * lax.erf(hidden * (0.5**0.5))
        act[rows, :] = (hidden * spread_to).astype(BF16)
        slope = spread_to + hidden * jnp.exp(-0.5 * hidden * hidden) * 0.3989422804014327
        d_hidden = (slope * dot(cot[rows, :], w2[:, FC2])).astype(BF16)
        dhid[rows, :] = d_hidden
        d_norm = dot_nt(d_hidden, w2[:, FC1])
        normed = xhat[rows, :]
        dx2[rows, :] = norm_back(small[1:2, :] * d_norm, normed, rstd[rows, 0:1])
        srow[0:8, :] += fold(d_norm * normed)
        srow[8:16, :] += fold(d_norm)
        srow[16:24, :] += fold(d_hidden.astype(F32))
        pl.when(index == 2)(lambda: relay(1))

    for half in (0, 1):
        span = slice(half * 384, half * 384 + 384)
        mlp_t[span, :] = dot_nt(w2[span, FC2], act[...])
        gq[0:384, 0:WIDE] = dot_tn(n2[:, span], dhid[...])
        gq[384:768, 0:WIDE] = dot(cot_t[span, :], act[...])

        @pl.loop(0, 16)
        def _(index):
            first = pl.ds(pl.multiple_of(index * 24, 8), 24)
            second = pl.ds(pl.multiple_of(384 + index * 24, 8), 24)
            slots[half * 16 + index, :, EARLY:HALF] = jnp.concatenate(
                [gq[first, 0:WIDE], gq[second, 0:WIDE]], axis=0
            ).astype(BF16)

    fc_sum = Reduce(
        net, slots, EARLY, 896, HALF, twin_in, halves, late_a, late_b, late_sa, late_sb, late_ea, late_eb
    )
    fc_sum.one()

    for half in (0, 1):
        span = slice(half * 384, half * 384 + 384)
        out_send[span, :] = (mlp_t[span, :] + dot_nt(w2[span, DENSE], heads[...])).astype(BF16)
        gq[span, DENSE] = dot(cot_t[span, :], heads[...])

    def part_of(number):
        return pl.ds(pl.multiple_of(number * PART, 16), PART)

    out_copies = [
        net.copy(out_send.at[part_of((y + step) % 4), :], out_recv.at[step - 1], net.at_y(step))
        for step in (1, 2, 3)
    ]
    start(out_copies)


    relay(2)

    @pl.loop(0, 3)
    def _(head):
        pl.when(helped)(dq_copy(head).wait_recv)
        pl.when(lower)(relay_copy(head).wait_recv)

    total_kv[...] = dkv[block].astype(F32)
    for step in range(3):

        @pl.when(send_own[step])
        def _():
            total_kv[...] += from_z[step].astype(F32)

    @pl.when(lower)
    def _():
        total_kv[...] += from_x[...].astype(F32)

    fc_sum.two()
    rowsum[...] = jnp.zeros_like(rowsum)

    @pl.loop(0, 4)
    def _(index):
        rows = tile_at(index)
        turning = (cosine[rows, :], -sine_up[rows, :], -sine_down[rows, :])
        pieces = [turn(total_kv[rows, spans[head]], *turning) for head in range(3)]
        query = []
        for head in range(3):
            grad = (dq_t[head, :, rows] + dq_in[head, :, rows].astype(F32)) * 0.125
            grad = jnp.concatenate([grad, jnp.zeros((HD, TILE), F32)], axis=0).T
            query.append(turn(grad, *turning))
        pieces.append(low_half(query[0]) + swap_halves(low_half(query[1])))
        pieces.append(low_half(query[2]))
        stacked = jnp.concatenate(pieces, axis=1).astype(BF16)
        dqkv[rows, :] = stacked
        d_norm = dot_nt(stacked, w2[:, QKV])
        normed = xhat[rows, :]
        d_input = dx2[rows, :] + norm_back(small[0:1, :] * d_norm, normed, rstd[rows, 0:1])
        rowsum[0:8, :] += fold(d_norm * normed)
        rowsum[8:16, :] += fold(d_norm)
        rowsum[16:24, 0:640] += fold(stacked.astype(F32))
        dx_send[:, rows] = d_input.T.astype(BF16)

    dx_copies = [
        net.copy(dx_send.at[part_of((y + step) % 4), :], dx_recv.at[step - 1], net.at_y(step))
        for step in (1, 2, 3)
    ]

    def whole(ref, at):
        return column_sum(ref[at : at + 8, :])

    y_send[...] = jnp.concatenate(
        [whole(rowsum, 0), whole(srow, 0), whole(rowsum, 8), whole(srow, 8), jnp.zeros((4, WIDE), F32)], axis=0
    )
    y_copies = [net.copy(y_send, y_recv.at[step - 1], net.at_y(step)) for step in (1, 2, 3)]
    start(y_copies + dx_copies)
    for half in (0, 1):
        span = slice(half * 384, half * 384 + 384)
        gq[span, QKV] = dot_tn(n1[:, span], dqkv[...])
    fc1_sum, qkv_total = whole(srow, 16), whole(rowsum, 16)
    pieces = []
    for number in range(12):
        pieces.append(fc1_sum[:, number // 2 * TILE : number // 2 * TILE + TILE])
    for number in (3, 3, 4, 0, 1, 2, 0, 1, 2):
        pieces.append(qkv_total[:, number * TILE : number * TILE + TILE])
    pieces.append(jnp.zeros((3, TILE), F32))
    bias_grads = jnp.concatenate(pieces, axis=0)
    row = lax.broadcasted_iota(jnp.int32, (24, TILE), 0)
    swapped = ((row < 12) & (row % 2 == 1)) | (row == 13) | (row >= 18)
    bias_rows[...] = jnp.where(swapped, swap_halves(bias_grads), bias_grads)
    wait(y_copies)
    shared = y_send[...] + y_recv[0] + y_recv[1] + y_recv[2]
    columns = jnp.concatenate(
        [
            jnp.zeros((SMALL, WIDE), F32),
            shared[0:4],
            jnp.zeros((2, WIDE), F32),
            jnp.zeros((58, WIDE), F32),
        ],
        axis=0,
    ).T
    lane = lanes((WIDE, TILE))
    columns = jnp.where((lane == SMALL + 4) | (lane == SMALL + 5), out_sums, columns)
    gq[:, 512:640] = jnp.where(lane < HD, gq[:, 512:640], columns)

    @pl.loop(0, 32)
    def _(index):
        rows = pl.ds(pl.multiple_of(index * 24, 8), 24)
        first = jnp.concatenate([gq[rows, 0:384], gq[rows, 640:768]], axis=1)
        second = jnp.concatenate([gq[rows, 384:640], gq[rows, 768:896], bias_rows[...]], axis=1)
        slots[index, :, 0:EARLY] = jnp.concatenate([first, second], axis=0).astype(BF16)

    fc_sum.three()
    qkv_sum = Reduce(
        net, slots, 0, 256, EARLY, twin_in, halves, early_a, early_b, early_sa, early_sb, early_ea, early_eb
    )
    qkv_sum.one()
    qkv_sum.two()

    wait(out_copies + dx_copies)
    mine = part_of(y)
    total = out_send[mine, :].astype(F32) + tok_t[mine, :].astype(F32) + out_col[mine, 0:1]
    grad = dx_send[mine, :].astype(F32) + cot_own[...].astype(F32)
    for step in range(3):
        total = total + out_recv[step].astype(F32)
        grad = grad + dx_recv[step].astype(F32)
    out_t[...] = total.astype(BF16)
    grad_t[...] = grad
    qkv_sum.three()

    @pl.loop(0, 3)
    def _(head):
        pl.when(helps)(partial(head).wait_send)
        pl.when(helped)(stat_copy(head).wait_send)
        pl.when(helps)(dq_copy(head).wait_send)
        pl.when(upper)(relay_copy(head).wait_send)
        for step in range(3):
            pl.when(either(send_own[step], send_prior[step]))(along(head, step).wait_send)
            pl.when(receive[step])(give_back(head, step).wait_send)

    pl.when(helped)(lend.wait_send)
    fc_sum.end(final)
    qkv_sum.end(final)


def finish_kernel(
    out_in, grad_in, final, out_t, grad_t, gain, shift, qkv, qkv_small, dense, fc1, fc1_small, fc2, outs
):
    out_t[...] = out_in[...]
    grad_t[...] = grad_in[...]
    fc1[...] = final[0:24, EARLY:HALF]
    fc2[...] = final[24:48, EARLY:HALF]
    left = lanes((24, TILE)) < HD
    one, two, three = (final[0:24, head * TILE : head * TILE + TILE] for head in range(3))
    qkv[1, :, 0:TILE] = jnp.where(left, one, swap_halves(two))
    qkv[1, :, TILE:PART] = three[:, 0:HD]
    qkv[2, :, 0:TILE] = jnp.where(left, swap_halves(one), two)
    qkv[2, :, TILE:PART] = swap_halves(three)[:, 0:HD]
    qkv[0, :, 0:TILE] = final[24:48, 0:TILE]
    mixed = final[24:48, TILE : 2 * TILE]
    qkv[0, :, TILE:PART] = mixed[:, 0:HD]
    dense[:, 0:TILE] = final[0:24, 384:512]
    dense[:, TILE:PART] = final[24:48, 256 : 256 + HD]
    rows = jnp.concatenate([mixed, jnp.zeros((TILE - 24, TILE), F32)], axis=0).T
    gain[...] = rows[SMALL : SMALL + 2, 0:24]
    shift[...] = rows[SMALL + 2 : SMALL + 4, 0:24]
    outs[...] = rows[SMALL + 4 : SMALL + 6, 0:24]
    own = lax.axis_index("dp") * 8 + lax.axis_index("ctx")
    moved = pltpu.roll(final[24:48, 384:512], TILE - 2 * own, axis=1)
    rows = jnp.concatenate([moved, jnp.zeros((TILE - 24, TILE), F32)], axis=0).T
    fc1_small[...] = rows[0:2, 0:12]
    for which in range(3):
        qkv_small[which] = pltpu.roll(rows[0:8], TILE - 12 - 3 * which, axis=1)[0:2, 0:3]


def angle_tables():
    frequency = 10000.0 ** (-2.0 * np.arange(ROT // 2) / ROT)
    result = []
    for positions in (np.arange(ROWS), ROWS * np.arange(8)):
        phases = np.zeros((len(positions), TILE))
        phases[:, 0:ROT] = positions[:, None] * np.concatenate([frequency, frequency])[None, :]
        result.append(np.stack([np.cos(phases), np.sin(phases)]).astype(np.float32))
    return result


def call(kernel, name, shapes, scratch, collective, inputs, outside=()):
    options = dict(vmem_limit_bytes=VMEM_LIMIT)
    if collective is not None:
        options.update(collective_id=collective, has_side_effects=True)
    return pl.pallas_call(
        kernel,
        name=name,
        out_shape=[jax.ShapeDtypeStruct(shape, kind) for shape, kind in shapes],
        in_specs=[
            pl.BlockSpec(memory_space=pl.ANY if number in outside else pltpu.VMEM)
            for number in range(len(inputs))
        ],
        out_specs=[pl.BlockSpec(memory_space=pltpu.VMEM)] * len(shapes),
        scratch_shapes=scratch,
        compiler_params=pltpu.CompilerParams(**options),
    )(*inputs)


def shards(
    tokens,
    norm_gain,
    norm_bias,
    qkv_weight,
    qkv_bias,
    dense_weight,
    fc1_weight,
    fc1_bias,
    fc2_weight,
    out_bias,
    cotangent,
):
    vm = pltpu.VMEM
    dma = pltpu.SemaphoreType.DMA
    wide = (ROWS, WIDE)
    row_angles, block_angles = angle_tables()
    out_t, grad_t, final = call(
        layer_kernel,
        "layer",
        [((PART, ROWS), BF16), ((PART, ROWS), F32), ((48, HALF), F32)],
        [
            vm(wide, BF16),
            vm((3, 24, PART), BF16),
            vm((24, PART), BF16),
            vm((24, WIDE), BF16),
            vm((24, WIDE), BF16),
            vm((PART, ROWS), BF16),
            vm((2, ROWS, TILE), F32),
            dma((7,)),
            vm((32, 48, HALF), BF16),
            vm((WIDE, 2432), BF16),
            vm((16, WIDE), F32),
            vm((8, WIDE), F32),
            vm((TILE, TILE), F32),
            vm((4, 24, TILE), F32),
            vm((24, TILE), F32),
            vm((WIDE, TILE), F32),
            vm((ROWS, TILE), F32),
            vm((ROWS, TILE), F32),
            vm((ROWS, TILE), F32),
            vm(wide, F32),
            vm((ROWS, TILE), F32),
            vm((WIDE, ROWS), BF16),
            vm(wide, BF16),
            vm(wide, BF16),
            vm(wide, BF16),
            vm(wide, BF16),
            vm((WIDE, ROWS), BF16),
            vm(wide, BF16),
            vm((WIDE, ROWS), F32),
            vm(wide, F32),
            vm((24, WIDE), F32),
            vm((ROWS, 384), BF16),
            vm((ROWS, 384), BF16),
            vm((6, TILE, ROWS), BF16),
            vm((8, ROWS, 384), BF16),
            vm((8, ROWS, 384), BF16),
            vm((15, TILE, ROWS), BF16),
            vm((15, ROWS, ROWS), BF16),
            vm((15, 8, ROWS), F32),
            vm((2, 8, ROWS), F32),
            vm((2, 8, ROWS), F32),
            vm((2, TILE, ROWS), F32),
            vm((2, TILE, ROWS), BF16),
            vm((2, ROWS, TILE), BF16),
            vm((3, 80, ROWS), F32),
            vm((3, 80, ROWS), F32),
            vm((2, 3, 24, ROWS), F32),
            vm((3, HD, ROWS), BF16),
            vm((3, HD, ROWS), BF16),
            vm((3, HD, ROWS), F32),
            vm((3, 80, ROWS), F32),
            vm((WIDE, 896), F32),
            vm((16, 48, HALF), BF16),
            vm((16, 48, HALF), BF16),
            vm((3, 4, 48, 256), BF16),
            vm((3, 4, 48, 256), BF16),
            vm((4, 48, 256), BF16),
            vm((4, 48, 256), BF16),
            vm((3, 48, 256), BF16),
            vm((3, 48, 256), BF16),
            vm((3, 4, 48, 384), BF16),
            vm((3, 4, 48, 384), BF16),
            vm((4, 48, 384), BF16),
            vm((4, 48, 384), BF16),
            vm((3, 48, 384), BF16),
            vm((3, 48, 384), BF16),
            vm((3, ROWS, 384), BF16),
            vm((ROWS, 384), BF16),
            vm((ROWS, 384), BF16),
            vm((ROWS, 256), BF16),
            vm((WIDE, ROWS), BF16),
            vm((3, PART, ROWS), BF16),
            vm((WIDE, ROWS), BF16),
            vm((3, PART, ROWS), BF16),
            vm((24, WIDE), F32),
            vm((8, WIDE), F32),
            vm((3, 8, WIDE), F32),
            dma((144,)),
            dma((144,)),
        ],
        0,
        [
            tokens[0],
            norm_gain,
            norm_bias,
            out_bias,
            jnp.transpose(qkv_weight, (1, 0, 2)),
            jnp.transpose(qkv_bias, (0, 2, 1)),
            dense_weight.T,
            fc1_weight,
            fc1_bias.T,
            fc2_weight.T,
            cotangent[0].T,
            jnp.asarray(row_angles),
            jnp.asarray(block_angles),
        ],
        (0, 4, 6, 7, 9, 10, 11),
    )
    out_t, grad_t, gain, shift, qkv, qkv_small, dense, fc1, fc1_small, fc2, outs = call(
        finish_kernel,
        "finish",
        [
            ((PART, ROWS), BF16),
            ((PART, ROWS), F32),
            ((2, 24), F32),
            ((2, 24), F32),
            ((3, 24, PART), F32),
            ((3, 2, 3), F32),
            ((24, PART), F32),
            ((24, WIDE), F32),
            ((2, 12), F32),
            ((24, WIDE), F32),
            ((2, 24), F32),
        ],
        [],
        None,
        [out_t, grad_t, final],
    )
    return (
        out_t.T[None],
        grad_t.T[None],
        gain,
        shift,
        jnp.transpose(qkv, (1, 0, 2)),
        jnp.transpose(qkv_small, (0, 2, 1)),
        dense.T,
        fc1,
        fc1_small.T,
        fc2.T,
        outs,
    )


def solution(mesh):
    return jax.shard_map(
        shards,
        mesh=mesh,
        in_specs=(
            P("dp", "ctx", None),
            P(None, ("dp", "ctx")),
            P(None, ("dp", "ctx")),
            P(("dp", "ctx"), None, "tensor"),
            P(None, "tensor", ("dp", "ctx")),
            P("tensor", ("dp", "ctx")),
            P(("dp", "ctx"), "tensor"),
            P("tensor", ("dp", "ctx")),
            P("tensor", ("dp", "ctx")),
            P(None, ("dp", "ctx")),
            P("dp", "ctx", "tensor"),
        ),
        out_specs=(
            P("dp", "ctx", "tensor"),
            P("dp", "ctx", "tensor"),
            P(None, ("dp", "ctx")),
            P(None, ("dp", "ctx")),
            P(("dp", "ctx"), None, "tensor"),
            P(None, "tensor", ("dp", "ctx")),
            P("tensor", ("dp", "ctx")),
            P(("dp", "ctx"), "tensor"),
            P("tensor", ("dp", "ctx")),
            P("tensor", ("dp", "ctx")),
            P(None, ("dp", "ctx")),
        ),
        check_vma=False,
    )
```

```python
import jax
import jax.numpy as jnp
import numpy as np
from jax import lax
from jax.experimental import pallas as pl
from jax.experimental.pallas import tpu as pltpu
from jax.sharding import PartitionSpec as P

HD = 64
ROT = 16
EPSILON = 1e-05
ROWS = 512
WIDE = 768
HALF = 1280
PART = 192
TILE = 128
MESH = pl.DeviceIdType.MESH
VMEM_LIMIT = 61 << 20
F32 = jnp.float32
BF16 = jnp.bfloat16

QKV = slice(0, 640)
DENSE = slice(640, 896)
FC1 = slice(896, 1664)
FC2 = slice(1664, 2432)
EARLY = 512
SMALL = 64


def dot(a, b):
    return lax.dot_general(a, b, (((1,), (0,)), ((), ())), preferred_element_type=F32)


def dot_nt(a, b):
    return lax.dot_general(a, b, (((1,), (1,)), ((), ())), preferred_element_type=F32)


def dot_tn(a, b):
    return lax.dot_general(a, b, (((0,), (0,)), ((), ())), preferred_element_type=F32)


def device(x, y, z, core):
    return {"dp": (x % 2) * 2 + core, "ctx": (x // 2) * 4 + z, "tensor": y}


class Links:
    def __init__(self, send, recv):
        dp = lax.axis_index("dp")
        cx = lax.axis_index("ctx")
        self.xlo, self.core, self.xhi, self.z = dp // 2, dp % 2, cx // 4, cx % 4
        self.y = lax.axis_index("tensor")
        self.x = self.xhi * 2 + self.xlo
        self.send, self.recv, self.used = send, recv, 0

    def at_x(self, step):
        return device((self.x + step) % 4, self.y, self.z, self.core)

    def at_z(self, step):
        return device(self.x, self.y, (self.z + step) % 4, self.core)

    def at_y(self, step):
        return device(self.x, (self.y + step) % 4, self.z, self.core)

    def twin(self):
        return device(self.x, self.y, self.z, 1 - self.core)

    def pal(self):
        return device((self.x + 2) % 4, self.y, 3 - self.z, self.core)

    def knock(self):
        self.barrier = pltpu.get_barrier_semaphore()
        peers = [self.twin(), self.pal()]
        for step in (1, 2, 3):
            peers += [self.at_x(step), self.at_z(step), self.at_y(step)]
        for peer in peers:
            pl.semaphore_signal(self.barrier, inc=1, device_id=peer, device_id_type=MESH)
        self.expected = len(peers)

    def enter(self):
        pl.semaphore_wait(self.barrier, self.expected)

    def take(self, count):
        self.used += count
        return self.used - count

    def copy(self, source, target, peer, number=None):
        if number is None:
            number = self.take(1)
        return pltpu.make_async_remote_copy(
            src_ref=source,
            dst_ref=target,
            send_sem=self.send.at[number],
            recv_sem=self.recv.at[number],
            device_id=peer,
            device_id_type=MESH,
        )


def start(copies):
    for item in copies:
        item.start()


def wait(copies):
    for item in copies:
        item.wait()


def lanes(shape):
    return lax.broadcasted_iota(jnp.int32, shape, len(shape) - 1)


def low_half(tile):
    return jnp.where(lanes(tile.shape) < HD, tile, 0.0)


def high_half(tile):
    return jnp.where(lanes(tile.shape) >= HD, tile, 0.0)


def swap_halves(tile):
    return pltpu.roll(tile, HD, axis=1)


def turn(tile, cosine, sine_up, sine_down):
    return (
        tile * cosine
        + pltpu.roll(tile, ROT // 2, axis=1) * sine_up
        + pltpu.roll(tile, TILE - ROT // 2, axis=1) * sine_down
    )


def fold(block):
    rows, width = block.shape
    return jnp.sum(block.reshape(rows // 8, 8, width), axis=0)


def column_sum(block):
    return jnp.sum(block, axis=0, keepdims=True)


def standardize(rows_in):
    values = rows_in.astype(F32)
    centred = values - jnp.mean(values, axis=-1, keepdims=True)
    scale = lax.rsqrt(jnp.mean(centred * centred, axis=-1, keepdims=True) + EPSILON)
    return centred * scale, scale


def norm_back(gradient, xhat, scale):
    return scale * (
        gradient
        - jnp.mean(gradient, axis=-1, keepdims=True)
        - xhat * jnp.mean(gradient * xhat, axis=-1, keepdims=True)
    )


def tile_at(index):
    return pl.ds(pl.multiple_of(index * TILE, TILE), TILE)


def quad(position):
    return (position % 2) * 2 + position // 2


class Gather:
    def __init__(self, net, slots, own, low, middle, high):
        first, second = slice(low, middle), slice(middle, high)
        mine_a, mine_b = slots.at[own, :, first], slots.at[own, :, second]
        four = slots.at[pl.ds(own - net.z, 4), :, first]
        steps = (1, 2, 3)
        self.a = [net.copy(mine_a, mine_a, net.at_z(step)) for step in steps]
        self.b = [net.copy(mine_b, mine_b, net.at_x(step)) for step in steps]
        self.mid_a = [net.copy(four, four, net.at_x(step)) for step in steps]
        self.mid_b, self.last_a, self.last_b = [], [], []
        for low in (0, 1):
            for high in (0, 1):
                piece = slots.at[((low * 2 + net.core) * 2 + high) * 4 + net.z, :, second]
                self.mid_b += [net.copy(piece, piece, net.at_z(step)) for step in steps]
            for span, copies in ((first, self.last_a), (second, self.last_b)):
                piece = slots.at[pl.ds((low * 2 + net.core) * 8, 8), :, span]
                copies.append(net.copy(piece, piece, net.twin()))

    def one(self):
        start(self.a + self.b)

    def two(self):
        wait(self.a)
        start(self.mid_a)
        wait(self.b)
        start(self.mid_b)

    def three(self):
        wait(self.mid_a)
        start(self.last_a)
        wait(self.mid_b)
        start(self.last_b)

    def end(self):
        wait(self.last_a + self.last_b)


class Reduce:
    def __init__(self, net, slots, low, middle, high, twin_in, halves, in_a, in_b, sum_a, sum_b, end_a, end_b):
        self.net, self.slots = net, slots
        self.whole, self.first, self.second = slice(low, high), slice(low, middle), slice(middle, high)
        self.bufs = (twin_in, halves, in_a, in_b, sum_a, sum_b, end_a, end_b)
        self.me = quad(net.x)
        self.twins = [
            net.copy(
                slots.at[pl.ds((low * 2 + 1 - net.core) * 8, 8), :, self.whole],
                twin_in.at[pl.ds(low * 8, 8), :, self.whole],
                net.twin(),
            )
            for low in (0, 1)
        ]
        self.mid_a, self.mid_b, self.last_a, self.last_b = [], [], [], []
        for step in (1, 2, 3):
            there = quad((net.x + step) % 4)
            self.mid_a.append(
                net.copy(halves.at[pl.ds(there * 4, 4), :, self.first], in_a.at[step - 1], net.at_x(step))
            )
            for which in range(4):
                self.mid_b.append(
                    net.copy(
                        halves.at[which * 4 + (net.z + step) % 4, :, self.second],
                        in_b.at[step - 1, which],
                        net.at_z(step),
                    )
                )
            self.last_a.append(net.copy(sum_a.at[(net.z + step) % 4], end_a.at[step - 1], net.at_z(step)))
            self.last_b.append(net.copy(sum_b.at[there], end_b.at[step - 1], net.at_x(step)))

    def one(self):
        start(self.twins)

    def two(self):
        twin_in, halves = self.bufs[:2]
        wait(self.twins)

        @pl.loop(0, 16)
        def _(index):
            source = (index // 8 * 2 + self.net.core) * 8 + index % 8
            halves[index, :, self.whole] = (
                self.slots[source, :, self.whole].astype(F32) + twin_in[index, :, self.whole].astype(F32)
            ).astype(BF16)

        start(self.mid_a + self.mid_b)

    def three(self):
        halves, in_a, in_b, sum_a, sum_b = self.bufs[1:6]
        wait(self.mid_a)

        @pl.loop(0, 4)
        def _(index):
            total = halves[self.me * 4 + index, :, self.first].astype(F32)
            for step in range(3):
                total = total + in_a[step, index].astype(F32)
            sum_a[index] = total.astype(BF16)

        start(self.last_a)
        wait(self.mid_b)

        @pl.loop(0, 4)
        def _(index):
            total = halves[index * 4 + self.net.z, :, self.second].astype(F32)
            for step in range(3):
                total = total + in_b[step, index].astype(F32)
            sum_b[index] = total.astype(BF16)

        start(self.last_b)

    def end(self, target):
        sum_a, sum_b, end_a, end_b = self.bufs[4:]
        for copies, own, arrived, span in (
            (self.last_a, sum_a.at[self.net.z], end_a, self.first),
            (self.last_b, sum_b.at[self.me], end_b, self.second),
        ):
            wait(copies)
            total = own[...].astype(F32)
            for step in range(3):
                total = total + arrived[step].astype(F32)
            target[:, span] = total


def layer_kernel(
    tok_in, gains, shifts, outs, qkv_in, qkv_small, dense_in, fc1_in, fc1_small, fc2_in, cot_in, angle_in, angle_block,
    out_t, grad_t, final,
    tok, qkv, dense, fc1, fc2, cot_own, angle_rows, loads,
    slots, w2, small, bias, small_rows, narrow, bias_rows, out_col, cosine, sine_up, sine_down, xhat, rstd, tok_t, n1, n2, dhid, act,
    cot_t, cot, mlp_t, dx2, srow, qd, qd_in, qdt, kv, dkv, kv_t, weights, tops, top, totals, summed, query_t, query_n,
    part_out, part_in, stat, dq_out, dq_in, dq_t, kept, gq,
    twin_in, halves, early_a, early_b, early_sa, early_sb, early_ea, early_eb,
    late_a, late_b, late_sa, late_sb, late_ea, late_eb,
    from_z, from_x, to_x, heads, out_send, out_recv, dx_send, dx_recv, rowsum, y_send, y_recv,
    send, recv,
):
    net = Links(send, recv)
    xlo, core, xhi, z, y = net.xlo, net.core, net.xhi, net.z, net.y
    own = ((xlo * 2 + core) * 2 + xhi) * 4 + z
    block = xhi * 4 + z
    upper, lower = xhi == 1, xhi == 0
    both = jnp.logical_and
    either = jnp.logical_or
    brought = [
        pltpu.make_async_copy(source, target, loads.at[number])
        for number, (source, target) in enumerate(
            (
                (qkv_in, qkv),
                (dense_in, dense),
                (fc1_in, fc1),
                (fc2_in, fc2),
                (angle_in, angle_rows),
                (tok_in, tok),
                (cot_in, cot_own),
            )
        )
    ]
    start(brought)
    helps = both(lower, z <= 2)
    helped = both(upper, z >= 1)
    dqkv = n2.at[:, QKV]
    total_kv = gq.at[0:ROWS, 0:384]
    net.knock()

    wait(brought[0:4])
    narrow[...] = jnp.zeros_like(narrow)
    for which in range(3):
        narrow[which, :, 0:HD] = qkv[which, :, TILE:PART].astype(F32)
    narrow[3, :, 0:HD] = dense[:, TILE:PART].astype(F32)
    small_rows[...] = jnp.zeros_like(small_rows)
    small_rows[SMALL : SMALL + 2, 0:24] = gains[...].astype(F32)
    small_rows[SMALL + 2 : SMALL + 4, 0:24] = shifts[...].astype(F32)
    small_rows[SMALL + 4 : SMALL + 6, 0:24] = outs[...].astype(F32)
    columns = small_rows[...].T[0:24]

    small_rows[...] = jnp.zeros_like(small_rows)
    small_rows[0:2, 0:12] = fc1_small[...].astype(F32)
    for which in range(3):
        small_rows[8 + 8 * which : 10 + 8 * which, 0:3] = qkv_small[which].astype(F32)
    turned = small_rows[...].T[0:16]
    pair_lane = lanes((16, TILE)) < 2
    bias_rows[0:16, :] = jnp.where(pair_lane, turned, 0.0)
    bias_rows[16:24, :] = jnp.zeros((8, TILE), F32)
    for which in range(3):
        moved = pltpu.roll(turned, TILE - 8 - 8 * which, axis=1)
        bias_rows[12 + 3 * which : 15 + 3 * which, :] = jnp.where(pair_lane, moved, 0.0)[0:3]
    biases = pltpu.roll(bias_rows[...], 2 * own, axis=1)
    key = qkv[1, :, 0:TILE].astype(F32)
    value = qkv[2, :, 0:TILE].astype(F32)
    left = lanes((24, TILE)) < HD
    top_half = jnp.concatenate(
        [
            jnp.where(left, key, swap_halves(value)),
            jnp.where(left, swap_halves(key), value),
            narrow[1] + swap_halves(narrow[2]),
            dense[:, 0:TILE].astype(F32),
        ],
        axis=1,
    )
    bottom_half = jnp.concatenate(
        [qkv[0, :, 0:TILE].astype(F32), narrow[0] + columns, narrow[3], biases], axis=1
    )
    slots[own, :, 0:EARLY] = jnp.concatenate([top_half, bottom_half], axis=0).astype(BF16)
    slots[own, :, EARLY:HALF] = jnp.concatenate([fc1[...].astype(F32), fc2[...].astype(F32)], axis=0).astype(BF16)
    net.enter()
    early = Gather(net, slots, own, 0, 256, EARLY)
    late = Gather(net, slots, own, EARLY, 896, HALF)
    early.one()

    wait(brought[4:7])
    row_cos, row_sin = angle_rows[0], angle_rows[1]
    block_cos, block_sin = angle_block[0, pl.ds(block, 1), :], angle_block[1, pl.ds(block, 1), :]
    cosine[...] = row_cos * block_cos - row_sin * block_sin
    sine = row_sin * block_cos + row_cos * block_sin
    upward = lanes((ROWS, TILE)) >= ROT // 2
    sine_up[...] = jnp.where(upward, sine, 0.0)
    sine_down[...] = jnp.where(upward, 0.0, -sine)

    early.two()
    late.one()
    mine_t = cot_t.at[pl.ds(pl.multiple_of(y * PART, 16), PART), :]
    gather_y = [net.copy(cot_own, mine_t, net.at_y(step)) for step in (1, 2, 3)]
    start(gather_y)
    mine_t[...] = cot_own[...]

    @pl.loop(0, 4)
    def _(index):
        rows = tile_at(index)
        normed, scale = standardize(tok[rows, :])
        xhat[rows, :] = normed
        rstd[rows, :] = jnp.broadcast_to(scale, (TILE, TILE))


    @pl.loop(0, 4)
    def _(index):
        rows = tile_at(index)
        tok_t[:, rows] = tok[rows, :].astype(F32).T.astype(BF16)

    early.three()
    dkv[...] = jnp.zeros_like(dkv)
    early.end()
    bias_rows[...] = jnp.zeros_like(bias_rows)

    @pl.loop(0, 16)
    def _(pair):
        rows = pl.ds(pl.multiple_of(pair * 48, 16), 48)
        one = slots[2 * pair, :, 0:EARLY].astype(F32)
        two = slots[2 * pair + 1, :, 0:EARLY].astype(F32)
        upper_rows = jnp.concatenate([one[0:24], two[0:24]], axis=0).astype(BF16)
        lower_rows = jnp.concatenate([one[24:48], two[24:48]], axis=0).astype(BF16)
        w2[rows, 0:384] = upper_rows[:, 0:384]
        w2[rows, 640:768] = upper_rows[:, 384:512]
        w2[rows, 384:640] = lower_rows[:, 0:256]
        w2[rows, 768:896] = lower_rows[:, 256:384]
        bias_rows[...] += one[24:48, 384:512] + two[24:48, 384:512]

    column_form = w2[:, 512:640].astype(F32)
    out_col[...] = jnp.broadcast_to(
        column_form[:, SMALL + 4 : SMALL + 5] + column_form[:, SMALL + 5 : SMALL + 6], (WIDE, TILE)
    )
    turned = column_form.T[SMALL : SMALL + 16, :]
    small[...] = turned
    even, odd = bias_rows[...], swap_halves(bias_rows[...])
    for number in range(6):
        bias[1:2, number * TILE : number * TILE + TILE] = (
            even[2 * number : 2 * number + 1] + odd[2 * number + 1 : 2 * number + 2]
        )
    for head in range(3):
        bias[0:1, head * TILE : head * TILE + TILE] = even[15 + head : 16 + head] + odd[18 + head : 19 + head]
    bias[0:1, 384:512] = even[12:13] + odd[13:14]
    bias[0:1, 512:640] = even[14:15]

    @pl.loop(0, 4)
    def _(index):
        rows = tile_at(index)
        normed = xhat[rows, :]
        one = (normed * small[0:1, :] + small[2:3, :]).astype(BF16)
        n1[rows, :] = one
        n2[rows, :] = (normed * small[1:2, :] + small[3:4, :]).astype(BF16)
        projected = dot(one, w2[:, QKV]) + bias[0:1, 0:640]
        turning = (cosine[rows, :], sine_up[rows, :], sine_down[rows, :])
        for head in range(3):
            span = slice(head * TILE, head * TILE + TILE)
            kv[block, rows, span] = turn(projected[:, span], *turning).astype(BF16)
        pair, last = projected[:, 384:512], projected[:, 512:640]
        for head, tile in enumerate((pair, swap_halves(pair), last)):
            span = slice(head * TILE, head * TILE + TILE)
            qd[rows, span] = (low_half(turn(low_half(tile), *turning)) * 0.125).astype(BF16)

    spans = [slice(head * TILE, head * TILE + TILE) for head in range(3)]
    send_own, send_prior, receive, given = [], [], [], []
    for step in (1, 2, 3):
        behind = z + step <= 3
        send_own.append(either(behind, both(lower, both(z + step == 4, z <= 2))))
        send_prior.append(both(upper, z + step > 3))
        receive.append(either(upper, either(z - step >= 0, both(z == 0, step >= 2))))
        given.append((z - step + 4) % 4 + 4 * xhi * ((z - step + 4) // 4))
    head_span = lambda head: pl.ds(pl.multiple_of(head * TILE, TILE), TILE)
    across_at, along_at, return_at, relay_at, part_at, stat_at, dq_at, lend_at = (
        net.take(count) for count in (3, 9, 9, 3, 3, 3, 3, 3)
    )

    def across(head):
        mine = kv.at[block, :, head_span(head)]
        return net.copy(mine, mine, net.at_x(2), across_at + head)

    def along(head, step):
        piece = kv.at[block - 4 * xhi * ((z + step + 1) // 4), :, head_span(head)]
        return net.copy(piece, piece, net.at_z(step + 1), along_at + 3 * head + step)

    def send_first(head):
        pl.when(lower)(across(head).start)
        for step in range(3):
            pl.when(send_own[step])(along(head, step).start)

    def send_second(head):
        pl.when(upper)(across(head).wait_recv)
        for step in range(3):
            pl.when(send_prior[step])(along(head, step).start)
        pl.when(helped)(lend(head).start)

    def lend(head):
        return net.copy(qd.at[:, head_span(head)], qd_in.at[:, head_span(head)], net.pal(), lend_at + head)

    send_first(0)


    wait(gather_y)

    @pl.loop(0, 4)
    def _(index):
        rows = tile_at(index)
        cot[rows, :] = cot_t[:, rows].astype(F32).T.astype(BF16)

    out_sums = jnp.sum(cot_t[...].astype(F32), axis=1, keepdims=True)

    @pl.loop(0, 4)
    def _(index):
        rows = tile_at(index)
        d_heads = dot(cot[rows, :], w2[:, DENSE])
        pair, last = d_heads[:, 0:TILE], d_heads[:, TILE : 2 * TILE]
        for head, tile in enumerate((swap_halves(pair), pair, swap_halves(last))):
            qd[rows, spans[head]] = (qd[rows, spans[head]].astype(F32) + high_half(tile)).astype(BF16)

    send_second(0)
    send_first(1)

    row_is_low = lax.broadcasted_iota(jnp.int32, (TILE, ROWS), 0) < HD
    lent_count = (1 - xhi) * (3 - z)
    chunk_count = 4 + xhi

    def chunk_place(index):
        which = (lent_count + 7 - index) // 8
        return which, index - lent_count * (1 - which) + xhi * z

    def partial(head):
        return net.copy(part_out.at[head], part_in.at[head], net.pal(), part_at + head)

    def stat_copy(head):
        return net.copy(stat.at[0, head], stat.at[1, head], net.pal(), stat_at + head)

    def dq_copy(head):
        return net.copy(dq_out.at[head], dq_in.at[head], net.pal(), dq_at + head)

    def outcome(target, head, which):
        target[head, 0:HD, :] = summed[which, HD:TILE, :]
        target[head, HD : HD + 8, :] = top[which]
        target[head, HD + 8 : HD + 16, :] = jnp.broadcast_to(column_sum(totals[which]), (8, ROWS))

    @pl.when(jnp.logical_not(helped))
    def _():
        part_in[...] = jnp.zeros_like(part_in)
        part_in[:, HD : HD + 8, :] = jnp.full((3, 8, ROWS), -1e30, F32)
        dq_in[...] = jnp.zeros_like(dq_in)

    def ahead(head):
        span = head_span(head)
        pl.when(lower)(across(head).wait_send)
        for step in range(3):
            pl.when(receive[step])(along(head, step).wait_recv)
        pl.when(head < 2)(lambda: send_second(head + 1))
        pl.when(head == 0)(lambda: send_first(2))

        def turn_queries(source, which):
            turned = source[:, span].astype(F32).T
            qdt[which * 3 + head] = turned.astype(BF16)
            query_t[which] = jnp.where(row_is_low, turned, 0.0).astype(BF16)

        turn_queries(qd, 0)
        top[...] = jnp.full_like(top, -1e30)
        totals[...] = jnp.zeros_like(totals)
        summed[...] = jnp.zeros_like(summed)

        @pl.loop(0, chunk_count)
        def _(turn_of):
            index = (turn_of + lent_count) % chunk_count

            @pl.when(both(helps, turn_of == chunk_count - lent_count))
            def _():
                lend(head).wait_recv()
                turn_queries(qd_in, 1)

            which, at = chunk_place(index)
            chunk = head * 5 + index
            tile = kv[at, :, span]
            tile_t = tile.astype(F32).T.astype(BF16)
            kv_t[chunk] = tile_t
            key_shift = (at - block - which * (7 - 2 * block)) * ROWS
            parts = [slice(half * 256, half * 256 + 256) for half in (0, 1)]
            scores = [dot(tile, query_t[which, :, part]) for part in parts]
            before = [top[which, 0:1, part] for part in parts]
            old_total = [totals[which, :, part] for part in parts]
            old_sum = [summed[which, :, part] for part in parts]
            for half, part in enumerate(parts):
                score = scores[half]
                key_at = lax.broadcasted_iota(jnp.int32, score.shape, 0) + key_shift
                query_at = lax.broadcasted_iota(jnp.int32, score.shape, 1) + half * 256
                score = jnp.where(key_at <= query_at, score, -1e30)
                peak = jnp.maximum(before[half], jnp.max(score, axis=0, keepdims=True))
                weight = jnp.exp(score - peak)
                shrink = jnp.exp(before[half] - peak)
                rounded = weight.astype(BF16)
                weights[chunk, :, part] = rounded
                peaks = jnp.broadcast_to(peak, (8, 256))
                tops[chunk, :, part] = peaks
                top[which, :, part] = peaks
                totals[which, :, part] = old_total[half] * shrink + fold(weight)
                summed[which, :, part] = old_sum[half] * shrink + dot(tile_t, rounded)

            @pl.when(both(helps, turn_of == chunk_count - 1))
            def _():
                outcome(part_out, head, 1)
                partial(head).start()

        outcome(kept, head, 0)
        pl.when(head == 2)(late.two)

    def merge(head):
        pl.when(helped)(partial(head).wait_recv)
        top_one, top_two = kept[head, HD : HD + 1, :], part_in[head, HD : HD + 1, :]
        peak = jnp.maximum(top_one, top_two)
        share_one, share_two = jnp.exp(top_one - peak), jnp.exp(top_two - peak)
        total = kept[head, HD + 8 : HD + 9, :] * share_one + part_in[head, HD + 8 : HD + 9, :] * share_two
        inverse = 1.0 / total
        result = (kept[head, 0:HD, :] * share_one + part_in[head, 0:HD, :] * share_two) * inverse
        delta = column_sum(qdt[head, HD:TILE, :].astype(F32) * result)
        kept[head, 0:HD, :] = result
        stat[0, head, 0:8, :] = jnp.broadcast_to(peak, (8, ROWS))
        stat[0, head, 8:16, :] = jnp.broadcast_to(inverse, (8, ROWS))
        stat[0, head, 16:24, :] = jnp.broadcast_to(delta, (8, ROWS))
        pl.when(helped)(stat_copy(head).start)

    def give_back(head, step):
        return net.copy(
            dkv.at[given[step], :, head_span(head)],
            from_z.at[step, :, head_span(head)],
            net.at_z(3 - step),
            return_at + 3 * head + step,
        )

    def relay_copy(head):
        return net.copy(to_x.at[:, head_span(head)], from_x.at[:, head_span(head)], net.at_x(2), relay_at + head)

    def relay(head):
        span = head_span(head)
        for step in range(3):
            pl.when(either(send_own[step], send_prior[step]))(give_back(head, step).wait_recv)

        @pl.when(upper)
        def _():
            total_kv[:, span] = dkv[z, :, span].astype(F32)
            for step in range(3):

                @pl.when(send_prior[step])
                def _():
                    total_kv[:, span] += from_z[step, :, span].astype(F32)

            to_x[:, span] = total_kv[:, span].astype(BF16)
            relay_copy(head).start()

    def back(head):
        span = head_span(head)
        query_n[0] = low_half(qd[:, span].astype(F32)).astype(BF16)

        @pl.when(helps)
        def _():
            query_n[1] = low_half(qd_in[:, span].astype(F32)).astype(BF16)

        summed[...] = jnp.zeros_like(summed)

        @pl.loop(0, chunk_count)
        def _(turn_of):
            index = (turn_of + lent_count) % chunk_count
            which, at = chunk_place(index)
            chunk = head * 5 + index
            pl.when(both(helps, turn_of == chunk_count - lent_count))(stat_copy(head).wait_recv)
            change = dkv[at, :, span].astype(F32)
            for half in (0, 1):
                part = slice(half * 256, half * 256 + 256)
                factor = jnp.exp(tops[chunk, 0:1, part] - stat[which, head, 0:1, part]) * stat[which, head, 8:9, part]
                weight = weights[chunk, :, part]
                scaled = jnp.where(
                    row_is_low[:, 0:256], 0.0, qdt[which * 3 + head, :, part].astype(F32) * factor
                )
                d_weight = dot(kv[at, :, span], scaled.astype(BF16))
                d_score = (
                    weight.astype(F32) * (d_weight - stat[which, head, 16:17, part] * factor)
                ).astype(BF16)
                change = change + dot(d_score, query_n[which, part, :]) + dot(weight, scaled.T.astype(BF16))
                summed[which, :, part] += dot(kv_t[chunk], d_score)
            dkv[at, :, span] = change.astype(BF16)

        dq_t[head] = summed[0, 0:HD, :]

        @pl.when(helps)
        def _():
            dq_out[head] = summed[1, 0:HD, :].astype(BF16)
            dq_copy(head).start()

        for step in range(3):
            pl.when(receive[step])(give_back(head, step).start)

    @pl.loop(0, 4)
    def _(index):
        pl.when(index < 3)(lambda: ahead(index))
        pl.when(index == 3)(late.three)
        pl.when(index > 0)(lambda: back(index - 1))
        pl.when(index < 3)(lambda: merge(index))

    heads[:, 0:TILE] = jnp.concatenate([kept[0, 0:HD, :], kept[1, 0:HD, :]], axis=0).T.astype(BF16)
    heads[:, TILE : 2 * TILE] = jnp.concatenate(
        [kept[2, 0:HD, :], jnp.zeros((HD, ROWS), F32)], axis=0
    ).T.astype(BF16)


    late.end()

    @pl.loop(0, 16)
    def _(pair):
        rows = pl.ds(pl.multiple_of(pair * 48, 16), 48)
        one = slots[2 * pair, :, EARLY:HALF].astype(F32)
        two = slots[2 * pair + 1, :, EARLY:HALF].astype(F32)
        w2[rows, FC1] = jnp.concatenate([one[0:24], two[0:24]], axis=0).astype(BF16)
        w2[rows, FC2] = jnp.concatenate([one[24:48], two[24:48]], axis=0).astype(BF16)

    relay(0)
    srow[...] = jnp.zeros_like(srow)

    @pl.loop(0, 4)
    def _(index):
        rows = tile_at(index)
        hidden = dot(n2[rows, :], w2[:, FC1]) + bias[1:2, :]
        spread_to = 0.5 + 0.5 * lax.erf(hidden * (0.5**0.5))
        act[rows, :] = (hidden * spread_to).astype(BF16)
        slope = spread_to + hidden * jnp.exp(-0.5 * hidden * hidden) * 0.3989422804014327
        d_hidden = (slope * dot(cot[rows, :], w2[:, FC2])).astype(BF16)
        dhid[rows, :] = d_hidden
        d_norm = dot_nt(d_hidden, w2[:, FC1])
        normed = xhat[rows, :]
        dx2[rows, :] = norm_back(small[1:2, :] * d_norm, normed, rstd[rows, 0:1])
        srow[0:8, :] += fold(d_norm * normed)
        srow[8:16, :] += fold(d_norm)
        srow[16:24, :] += fold(d_hidden.astype(F32))
        pl.when(index == 2)(lambda: relay(1))

    for half in (0, 1):
        span = slice(half * 384, half * 384 + 384)
        mlp_t[span, :] = dot_nt(w2[span, FC2], act[...])
        gq[0:384, 0:WIDE] = dot_tn(n2[:, span], dhid[...])
        gq[384:768, 0:WIDE] = dot(cot_t[span, :], act[...])

        @pl.loop(0, 16)
        def _(index):
            first = pl.ds(pl.multiple_of(index * 24, 8), 24)
            second = pl.ds(pl.multiple_of(384 + index * 24, 8), 24)
            slots[half * 16 + index, :, EARLY:HALF] = jnp.concatenate(
                [gq[first, 0:WIDE], gq[second, 0:WIDE]], axis=0
            ).astype(BF16)

    fc_sum = Reduce(
        net, slots, EARLY, 896, HALF, twin_in, halves, late_a, late_b, late_sa, late_sb, late_ea, late_eb
    )
    fc_sum.one()

    for half in (0, 1):
        span = slice(half * 384, half * 384 + 384)
        out_send[span, :] = (mlp_t[span, :] + dot_nt(w2[span, DENSE], heads[...])).astype(BF16)
        gq[span, DENSE] = dot(cot_t[span, :], heads[...])

    def part_of(number):
        return pl.ds(pl.multiple_of(number * PART, 16), PART)

    out_copies = [
        net.copy(out_send.at[part_of((y + step) % 4), :], out_recv.at[step - 1], net.at_y(step))
        for step in (1, 2, 3)
    ]
    start(out_copies)


    relay(2)

    @pl.loop(0, 3)
    def _(head):
        pl.when(helped)(dq_copy(head).wait_recv)
        pl.when(lower)(relay_copy(head).wait_recv)

    total_kv[...] = dkv[block].astype(F32)
    for step in range(3):

        @pl.when(send_own[step])
        def _():
            total_kv[...] += from_z[step].astype(F32)

    @pl.when(lower)
    def _():
        total_kv[...] += from_x[...].astype(F32)

    fc_sum.two()
    rowsum[...] = jnp.zeros_like(rowsum)

    @pl.loop(0, 4)
    def _(index):
        rows = tile_at(index)
        turning = (cosine[rows, :], -sine_up[rows, :], -sine_down[rows, :])
        pieces = [turn(total_kv[rows, spans[head]], *turning) for head in range(3)]
        query = []
        for head in range(3):
            grad = (dq_t[head, :, rows] + dq_in[head, :, rows].astype(F32)) * 0.125
            grad = jnp.concatenate([grad, jnp.zeros((HD, TILE), F32)], axis=0).T
            query.append(turn(grad, *turning))
        pieces.append(low_half(query[0]) + swap_halves(low_half(query[1])))
        pieces.append(low_half(query[2]))
        stacked = jnp.concatenate(pieces, axis=1).astype(BF16)
        dqkv[rows, :] = stacked
        d_norm = dot_nt(stacked, w2[:, QKV])
        normed = xhat[rows, :]
        d_input = dx2[rows, :] + norm_back(small[0:1, :] * d_norm, normed, rstd[rows, 0:1])
        rowsum[0:8, :] += fold(d_norm * normed)
        rowsum[8:16, :] += fold(d_norm)
        rowsum[16:24, 0:640] += fold(stacked.astype(F32))
        dx_send[:, rows] = d_input.T.astype(BF16)

    dx_copies = [
        net.copy(dx_send.at[part_of((y + step) % 4), :], dx_recv.at[step - 1], net.at_y(step))
        for step in (1, 2, 3)
    ]

    def whole(ref, at):
        return column_sum(ref[at : at + 8, :])

    y_send[...] = jnp.concatenate(
        [whole(rowsum, 0), whole(srow, 0), whole(rowsum, 8), whole(srow, 8), jnp.zeros((4, WIDE), F32)], axis=0
    )
    y_copies = [net.copy(y_send, y_recv.at[step - 1], net.at_y(step)) for step in (1, 2, 3)]
    start(y_copies + dx_copies)
    for half in (0, 1):
        span = slice(half * 384, half * 384 + 384)
        gq[span, QKV] = dot_tn(n1[:, span], dqkv[...])
    fc1_sum, qkv_total = whole(srow, 16), whole(rowsum, 16)
    pieces = []
    for number in range(12):
        pieces.append(fc1_sum[:, number // 2 * TILE : number // 2 * TILE + TILE])
    for number in (3, 3, 4, 0, 1, 2, 0, 1, 2):
        pieces.append(qkv_total[:, number * TILE : number * TILE + TILE])
    pieces.append(jnp.zeros((3, TILE), F32))
    bias_grads = jnp.concatenate(pieces, axis=0)
    row = lax.broadcasted_iota(jnp.int32, (24, TILE), 0)
    swapped = ((row < 12) & (row % 2 == 1)) | (row == 13) | (row >= 18)
    bias_rows[...] = jnp.where(swapped, swap_halves(bias_grads), bias_grads)
    wait(y_copies)
    shared = y_send[...] + y_recv[0] + y_recv[1] + y_recv[2]
    columns = jnp.concatenate(
        [
            jnp.zeros((SMALL, WIDE), F32),
            shared[0:4],
            jnp.zeros((2, WIDE), F32),
            jnp.zeros((58, WIDE), F32),
        ],
        axis=0,
    ).T
    lane = lanes((WIDE, TILE))
    columns = jnp.where((lane == SMALL + 4) | (lane == SMALL + 5), out_sums, columns)
    gq[:, 512:640] = jnp.where(lane < HD, gq[:, 512:640], columns)

    @pl.loop(0, 32)
    def _(index):
        rows = pl.ds(pl.multiple_of(index * 24, 8), 24)
        first = jnp.concatenate([gq[rows, 0:384], gq[rows, 640:768]], axis=1)
        second = jnp.concatenate([gq[rows, 384:640], gq[rows, 768:896], bias_rows[...]], axis=1)
        slots[index, :, 0:EARLY] = jnp.concatenate([first, second], axis=0).astype(BF16)

    fc_sum.three()
    qkv_sum = Reduce(
        net, slots, 0, 256, EARLY, twin_in, halves, early_a, early_b, early_sa, early_sb, early_ea, early_eb
    )
    qkv_sum.one()
    qkv_sum.two()

    wait(out_copies + dx_copies)
    mine = part_of(y)
    total = out_send[mine, :].astype(F32) + tok_t[mine, :].astype(F32) + out_col[mine, 0:1]
    grad = dx_send[mine, :].astype(F32) + cot_own[...].astype(F32)
    for step in range(3):
        total = total + out_recv[step].astype(F32)
        grad = grad + dx_recv[step].astype(F32)
    out_t[...] = total.astype(BF16)
    grad_t[...] = grad
    qkv_sum.three()

    @pl.loop(0, 3)
    def _(head):
        pl.when(helped)(lend(head).wait_send)
        pl.when(helps)(partial(head).wait_send)
        pl.when(helped)(stat_copy(head).wait_send)
        pl.when(helps)(dq_copy(head).wait_send)
        pl.when(upper)(relay_copy(head).wait_send)
        for step in range(3):
            pl.when(either(send_own[step], send_prior[step]))(along(head, step).wait_send)
            pl.when(receive[step])(give_back(head, step).wait_send)

    fc_sum.end(final)
    qkv_sum.end(final)


def finish_kernel(
    out_in, grad_in, final, out_t, grad_t, gain, shift, qkv, qkv_small, dense, fc1, fc1_small, fc2, outs
):
    out_t[...] = out_in[...]
    grad_t[...] = grad_in[...]
    fc1[...] = final[0:24, EARLY:HALF]
    fc2[...] = final[24:48, EARLY:HALF]
    left = lanes((24, TILE)) < HD
    one, two, three = (final[0:24, head * TILE : head * TILE + TILE] for head in range(3))
    qkv[1, :, 0:TILE] = jnp.where(left, one, swap_halves(two))
    qkv[1, :, TILE:PART] = three[:, 0:HD]
    qkv[2, :, 0:TILE] = jnp.where(left, swap_halves(one), two)
    qkv[2, :, TILE:PART] = swap_halves(three)[:, 0:HD]
    qkv[0, :, 0:TILE] = final[24:48, 0:TILE]
    mixed = final[24:48, TILE : 2 * TILE]
    qkv[0, :, TILE:PART] = mixed[:, 0:HD]
    dense[:, 0:TILE] = final[0:24, 384:512]
    dense[:, TILE:PART] = final[24:48, 256 : 256 + HD]
    rows = jnp.concatenate([mixed, jnp.zeros((TILE - 24, TILE), F32)], axis=0).T
    gain[...] = rows[SMALL : SMALL + 2, 0:24]
    shift[...] = rows[SMALL + 2 : SMALL + 4, 0:24]
    outs[...] = rows[SMALL + 4 : SMALL + 6, 0:24]
    own = lax.axis_index("dp") * 8 + lax.axis_index("ctx")
    moved = pltpu.roll(final[24:48, 384:512], TILE - 2 * own, axis=1)
    rows = jnp.concatenate([moved, jnp.zeros((TILE - 24, TILE), F32)], axis=0).T
    fc1_small[...] = rows[0:2, 0:12]
    for which in range(3):
        qkv_small[which] = pltpu.roll(rows[0:8], TILE - 12 - 3 * which, axis=1)[0:2, 0:3]


def angle_tables():
    frequency = 10000.0 ** (-2.0 * np.arange(ROT // 2) / ROT)
    result = []
    for positions in (np.arange(ROWS), ROWS * np.arange(8)):
        phases = np.zeros((len(positions), TILE))
        phases[:, 0:ROT] = positions[:, None] * np.concatenate([frequency, frequency])[None, :]
        result.append(np.stack([np.cos(phases), np.sin(phases)]).astype(np.float32))
    return result


def call(kernel, name, shapes, scratch, collective, inputs, outside=()):
    options = dict(vmem_limit_bytes=VMEM_LIMIT)
    if collective is not None:
        options.update(collective_id=collective, has_side_effects=True)
    return pl.pallas_call(
        kernel,
        name=name,
        out_shape=[jax.ShapeDtypeStruct(shape, kind) for shape, kind in shapes],
        in_specs=[
            pl.BlockSpec(memory_space=pl.ANY if number in outside else pltpu.VMEM)
            for number in range(len(inputs))
        ],
        out_specs=[pl.BlockSpec(memory_space=pltpu.VMEM)] * len(shapes),
        scratch_shapes=scratch,
        compiler_params=pltpu.CompilerParams(**options),
    )(*inputs)


def shards(
    tokens,
    norm_gain,
    norm_bias,
    qkv_weight,
    qkv_bias,
    dense_weight,
    fc1_weight,
    fc1_bias,
    fc2_weight,
    out_bias,
    cotangent,
):
    vm = pltpu.VMEM
    dma = pltpu.SemaphoreType.DMA
    wide = (ROWS, WIDE)
    row_angles, block_angles = angle_tables()
    out_t, grad_t, final = call(
        layer_kernel,
        "layer",
        [((PART, ROWS), BF16), ((PART, ROWS), F32), ((48, HALF), F32)],
        [
            vm(wide, BF16),
            vm((3, 24, PART), BF16),
            vm((24, PART), BF16),
            vm((24, WIDE), BF16),
            vm((24, WIDE), BF16),
            vm((PART, ROWS), BF16),
            vm((2, ROWS, TILE), F32),
            dma((7,)),
            vm((32, 48, HALF), BF16),
            vm((WIDE, 2432), BF16),
            vm((16, WIDE), F32),
            vm((8, WIDE), F32),
            vm((TILE, TILE), F32),
            vm((4, 24, TILE), F32),
            vm((24, TILE), F32),
            vm((WIDE, TILE), F32),
            vm((ROWS, TILE), F32),
            vm((ROWS, TILE), F32),
            vm((ROWS, TILE), F32),
            vm(wide, F32),
            vm((ROWS, TILE), F32),
            vm((WIDE, ROWS), BF16),
            vm(wide, BF16),
            vm(wide, BF16),
            vm(wide, BF16),
            vm(wide, BF16),
            vm((WIDE, ROWS), BF16),
            vm(wide, BF16),
            vm((WIDE, ROWS), F32),
            vm(wide, F32),
            vm((24, WIDE), F32),
            vm((ROWS, 384), BF16),
            vm((ROWS, 384), BF16),
            vm((6, TILE, ROWS), BF16),
            vm((8, ROWS, 384), BF16),
            vm((8, ROWS, 384), BF16),
            vm((15, TILE, ROWS), BF16),
            vm((15, ROWS, ROWS), BF16),
            vm((15, 8, ROWS), F32),
            vm((2, 8, ROWS), F32),
            vm((2, 8, ROWS), F32),
            vm((2, TILE, ROWS), F32),
            vm((2, TILE, ROWS), BF16),
            vm((2, ROWS, TILE), BF16),
            vm((3, 80, ROWS), F32),
            vm((3, 80, ROWS), F32),
            vm((2, 3, 24, ROWS), F32),
            vm((3, HD, ROWS), BF16),
            vm((3, HD, ROWS), BF16),
            vm((3, HD, ROWS), F32),
            vm((3, 80, ROWS), F32),
            vm((WIDE, 896), F32),
            vm((16, 48, HALF), BF16),
            vm((16, 48, HALF), BF16),
            vm((3, 4, 48, 256), BF16),
            vm((3, 4, 48, 256), BF16),
            vm((4, 48, 256), BF16),
            vm((4, 48, 256), BF16),
            vm((3, 48, 256), BF16),
            vm((3, 48, 256), BF16),
            vm((3, 4, 48, 384), BF16),
            vm((3, 4, 48, 384), BF16),
            vm((4, 48, 384), BF16),
            vm((4, 48, 384), BF16),
            vm((3, 48, 384), BF16),
            vm((3, 48, 384), BF16),
            vm((3, ROWS, 384), BF16),
            vm((ROWS, 384), BF16),
            vm((ROWS, 384), BF16),
            vm((ROWS, 256), BF16),
            vm((WIDE, ROWS), BF16),
            vm((3, PART, ROWS), BF16),
            vm((WIDE, ROWS), BF16),
            vm((3, PART, ROWS), BF16),
            vm((24, WIDE), F32),
            vm((8, WIDE), F32),
            vm((3, 8, WIDE), F32),
            dma((144,)),
            dma((144,)),
        ],
        0,
        [
            tokens[0],
            norm_gain,
            norm_bias,
            out_bias,
            jnp.transpose(qkv_weight, (1, 0, 2)),
            jnp.transpose(qkv_bias, (0, 2, 1)),
            dense_weight.T,
            fc1_weight,
            fc1_bias.T,
            fc2_weight.T,
            cotangent[0].T,
            jnp.asarray(row_angles),
            jnp.asarray(block_angles),
        ],
        (0, 4, 6, 7, 9, 10, 11),
    )
    out_t, grad_t, gain, shift, qkv, qkv_small, dense, fc1, fc1_small, fc2, outs = call(
        finish_kernel,
        "finish",
        [
            ((PART, ROWS), BF16),
            ((PART, ROWS), F32),
            ((2, 24), F32),
            ((2, 24), F32),
            ((3, 24, PART), F32),
            ((3, 2, 3), F32),
            ((24, PART), F32),
            ((24, WIDE), F32),
            ((2, 12), F32),
            ((24, WIDE), F32),
            ((2, 24), F32),
        ],
        [],
        None,
        [out_t, grad_t, final],
    )
    return (
        out_t.T[None],
        grad_t.T[None],
        gain,
        shift,
        jnp.transpose(qkv, (1, 0, 2)),
        jnp.transpose(qkv_small, (0, 2, 1)),
        dense.T,
        fc1,
        fc1_small.T,
        fc2.T,
        outs,
    )


def solution(mesh):
    return jax.shard_map(
        shards,
        mesh=mesh,
        in_specs=(
            P("dp", "ctx", None),
            P(None, ("dp", "ctx")),
            P(None, ("dp", "ctx")),
            P(("dp", "ctx"), None, "tensor"),
            P(None, "tensor", ("dp", "ctx")),
            P("tensor", ("dp", "ctx")),
            P(("dp", "ctx"), "tensor"),
            P("tensor", ("dp", "ctx")),
            P("tensor", ("dp", "ctx")),
            P(None, ("dp", "ctx")),
            P("dp", "ctx", "tensor"),
        ),
        out_specs=(
            P("dp", "ctx", "tensor"),
            P("dp", "ctx", "tensor"),
            P(None, ("dp", "ctx")),
            P(None, ("dp", "ctx")),
            P(("dp", "ctx"), None, "tensor"),
            P(None, "tensor", ("dp", "ctx")),
            P("tensor", ("dp", "ctx")),
            P(("dp", "ctx"), "tensor"),
            P("tensor", ("dp", "ctx")),
            P("tensor", ("dp", "ctx")),
            P(None, ("dp", "ctx")),
        ),
        check_vma=False,
    )
```

```python
import jax
import jax.numpy as jnp
import numpy as np
from jax import lax
from jax.experimental import pallas as pl
from jax.experimental.pallas import tpu as pltpu
from jax.sharding import PartitionSpec as P

HD = 64
ROT = 16
EPSILON = 1e-05
ROWS = 512
WIDE = 768
HALF = 1280
PART = 192
TILE = 128
MESH = pl.DeviceIdType.MESH
VMEM_LIMIT = 61 << 20
F32 = jnp.float32
BF16 = jnp.bfloat16

QKV = slice(0, 640)
DENSE = slice(640, 896)
FC1 = slice(896, 1664)
FC2 = slice(1664, 2432)
EARLY = 512
SMALL = 64


def dot(a, b):
    return lax.dot_general(a, b, (((1,), (0,)), ((), ())), preferred_element_type=F32)


def dot_nt(a, b):
    return lax.dot_general(a, b, (((1,), (1,)), ((), ())), preferred_element_type=F32)


def dot_tn(a, b):
    return lax.dot_general(a, b, (((0,), (0,)), ((), ())), preferred_element_type=F32)


def device(x, y, z, core):
    return {"dp": (x % 2) * 2 + core, "ctx": (x // 2) * 4 + z, "tensor": y}


class Links:
    def __init__(self, send, recv):
        dp = lax.axis_index("dp")
        cx = lax.axis_index("ctx")
        self.xlo, self.core, self.xhi, self.z = dp // 2, dp % 2, cx // 4, cx % 4
        self.y = lax.axis_index("tensor")
        self.x = self.xhi * 2 + self.xlo
        self.send, self.recv, self.used = send, recv, 0

    def at_x(self, step):
        return device((self.x + step) % 4, self.y, self.z, self.core)

    def at_z(self, step):
        return device(self.x, self.y, (self.z + step) % 4, self.core)

    def at_y(self, step):
        return device(self.x, (self.y + step) % 4, self.z, self.core)

    def twin(self):
        return device(self.x, self.y, self.z, 1 - self.core)

    def pal(self):
        return device((self.x + 2) % 4, self.y, 3 - self.z, self.core)

    def knock(self):
        self.barrier = pltpu.get_barrier_semaphore()
        peers = [self.twin(), self.pal()]
        for step in (1, 2, 3):
            peers += [self.at_x(step), self.at_z(step), self.at_y(step)]
        for peer in peers:
            pl.semaphore_signal(self.barrier, inc=1, device_id=peer, device_id_type=MESH)
        self.expected = len(peers)

    def enter(self):
        pl.semaphore_wait(self.barrier, self.expected)

    def take(self, count):
        self.used += count
        return self.used - count

    def copy(self, source, target, peer, number=None):
        if number is None:
            number = self.take(1)
        return pltpu.make_async_remote_copy(
            src_ref=source,
            dst_ref=target,
            send_sem=self.send.at[number],
            recv_sem=self.recv.at[number],
            device_id=peer,
            device_id_type=MESH,
        )


def start(copies):
    for item in copies:
        item.start()


def wait(copies):
    for item in copies:
        item.wait()


def lanes(shape):
    return lax.broadcasted_iota(jnp.int32, shape, len(shape) - 1)


def low_half(tile):
    return jnp.where(lanes(tile.shape) < HD, tile, 0.0)


def high_half(tile):
    return jnp.where(lanes(tile.shape) >= HD, tile, 0.0)


def swap_halves(tile):
    return pltpu.roll(tile, HD, axis=1)


def turn(tile, cosine, sine_up, sine_down):
    return (
        tile * cosine
        + pltpu.roll(tile, ROT // 2, axis=1) * sine_up
        + pltpu.roll(tile, TILE - ROT // 2, axis=1) * sine_down
    )


def fold(block):
    rows, width = block.shape
    return jnp.sum(block.reshape(rows // 8, 8, width), axis=0)


def column_sum(block):
    return jnp.sum(block, axis=0, keepdims=True)


def standardize(rows_in):
    values = rows_in.astype(F32)
    centred = values - jnp.mean(values, axis=-1, keepdims=True)
    scale = lax.rsqrt(jnp.mean(centred * centred, axis=-1, keepdims=True) + EPSILON)
    return centred * scale, scale


def norm_back(gradient, xhat, scale):
    return scale * (
        gradient
        - jnp.mean(gradient, axis=-1, keepdims=True)
        - xhat * jnp.mean(gradient * xhat, axis=-1, keepdims=True)
    )


def tile_at(index):
    return pl.ds(pl.multiple_of(index * TILE, TILE), TILE)


def quad(position):
    return (position % 2) * 2 + position // 2


class Gather:
    def __init__(self, net, slots, own, low, middle, high):
        first, second = slice(low, middle), slice(middle, high)
        mine_a, mine_b = slots.at[own, :, first], slots.at[own, :, second]
        four = slots.at[pl.ds(own - net.z, 4), :, first]
        steps = (1, 2, 3)
        self.a = [net.copy(mine_a, mine_a, net.at_z(step)) for step in steps]
        self.b = [net.copy(mine_b, mine_b, net.at_x(step)) for step in steps]
        self.mid_a = [net.copy(four, four, net.at_x(step)) for step in steps]
        self.mid_b, self.last_a, self.last_b = [], [], []
        for low in (0, 1):
            for high in (0, 1):
                piece = slots.at[((low * 2 + net.core) * 2 + high) * 4 + net.z, :, second]
                self.mid_b += [net.copy(piece, piece, net.at_z(step)) for step in steps]
            for span, copies in ((first, self.last_a), (second, self.last_b)):
                piece = slots.at[pl.ds((low * 2 + net.core) * 8, 8), :, span]
                copies.append(net.copy(piece, piece, net.twin()))

    def one(self):
        start(self.a + self.b)

    def two(self):
        wait(self.a)
        start(self.mid_a)
        wait(self.b)
        start(self.mid_b)

    def three(self):
        wait(self.mid_a)
        start(self.last_a)
        wait(self.mid_b)
        start(self.last_b)

    def end(self):
        wait(self.last_a + self.last_b)


class Reduce:
    def __init__(self, net, slots, low, middle, high, twin_in, halves, in_a, in_b, sum_a, sum_b, end_a, end_b):
        self.net, self.slots = net, slots
        self.whole, self.first, self.second = slice(low, high), slice(low, middle), slice(middle, high)
        self.bufs = (twin_in, halves, in_a, in_b, sum_a, sum_b, end_a, end_b)
        self.me = quad(net.x)
        self.twins = [
            net.copy(
                slots.at[pl.ds((low * 2 + 1 - net.core) * 8, 8), :, self.whole],
                twin_in.at[pl.ds(low * 8, 8), :, self.whole],
                net.twin(),
            )
            for low in (0, 1)
        ]
        self.mid_a, self.mid_b, self.last_a, self.last_b = [], [], [], []
        for step in (1, 2, 3):
            there = quad((net.x + step) % 4)
            self.mid_a.append(
                net.copy(halves.at[pl.ds(there * 4, 4), :, self.first], in_a.at[step - 1], net.at_x(step))
            )
            for which in range(4):
                self.mid_b.append(
                    net.copy(
                        halves.at[which * 4 + (net.z + step) % 4, :, self.second],
                        in_b.at[step - 1, which],
                        net.at_z(step),
                    )
                )
            self.last_a.append(net.copy(sum_a.at[(net.z + step) % 4], end_a.at[step - 1], net.at_z(step)))
            self.last_b.append(net.copy(sum_b.at[there], end_b.at[step - 1], net.at_x(step)))

    def one(self):
        start(self.twins)

    def two(self):
        twin_in, halves = self.bufs[:2]
        wait(self.twins)

        @pl.loop(0, 16)
        def _(index):
            source = (index // 8 * 2 + self.net.core) * 8 + index % 8
            halves[index, :, self.whole] = (
                self.slots[source, :, self.whole].astype(F32) + twin_in[index, :, self.whole].astype(F32)
            ).astype(BF16)

        start(self.mid_a + self.mid_b)

    def three(self):
        halves, in_a, in_b, sum_a, sum_b = self.bufs[1:6]
        wait(self.mid_a)

        @pl.loop(0, 4)
        def _(index):
            total = halves[self.me * 4 + index, :, self.first].astype(F32)
            for step in range(3):
                total = total + in_a[step, index].astype(F32)
            sum_a[index] = total.astype(BF16)

        start(self.last_a)
        wait(self.mid_b)

        @pl.loop(0, 4)
        def _(index):
            total = halves[index * 4 + self.net.z, :, self.second].astype(F32)
            for step in range(3):
                total = total + in_b[step, index].astype(F32)
            sum_b[index] = total.astype(BF16)

        start(self.last_b)

    def end(self, target):
        sum_a, sum_b, end_a, end_b = self.bufs[4:]
        for copies, own, arrived, span in (
            (self.last_a, sum_a.at[self.net.z], end_a, self.first),
            (self.last_b, sum_b.at[self.me], end_b, self.second),
        ):
            wait(copies)
            total = own[...].astype(F32)
            for step in range(3):
                total = total + arrived[step].astype(F32)
            target[:, span] = total


def layer_kernel(
    tok_in, gains, shifts, outs, qkv_in, qkv_small, dense_in, fc1_in, fc1_small, fc2_in, cot_in, angle_in, angle_block,
    out_t, grad_t, final,
    tok, qkv, dense, fc1, fc2, cot_own, angle_rows, loads,
    slots, w2, small, bias, small_rows, narrow, bias_rows, out_col, cosine, sine_up, sine_down, xhat, rstd, tok_t, n1, n2, dhid, act,
    cot_t, cot, mlp_t, dx2, srow, qd, qd_in, qdt, kv, dkv, kv_t, weights, tops, top, totals, summed, query_t, query_n,
    part_out, part_in, part_top, part_top_in, stat, dq_out, dq_in, dq_t, kept, gq,
    twin_in, halves, early_a, early_b, early_sa, early_sb, early_ea, early_eb,
    late_a, late_b, late_sa, late_sb, late_ea, late_eb,
    from_z, from_x, to_x, heads, out_send, out_recv, dx_send, dx_recv, rowsum, y_send, y_recv,
    send, recv,
):
    net = Links(send, recv)
    xlo, core, xhi, z, y = net.xlo, net.core, net.xhi, net.z, net.y
    own = ((xlo * 2 + core) * 2 + xhi) * 4 + z
    block = xhi * 4 + z
    upper, lower = xhi == 1, xhi == 0
    both = jnp.logical_and
    either = jnp.logical_or
    brought = [
        pltpu.make_async_copy(source, target, loads.at[number])
        for number, (source, target) in enumerate(
            (
                (qkv_in, qkv),
                (dense_in, dense),
                (fc1_in, fc1),
                (fc2_in, fc2),
                (angle_in, angle_rows),
                (tok_in, tok),
                (cot_in, cot_own),
            )
        )
    ]
    start(brought)
    helps = both(lower, z <= 2)
    helped = both(upper, z >= 1)
    dqkv = n2.at[:, QKV]
    total_kv = gq.at[0:ROWS, 0:384]
    net.knock()

    wait(brought[0:4])
    narrow[...] = jnp.zeros_like(narrow)
    for which in range(3):
        narrow[which, :, 0:HD] = qkv[which, :, TILE:PART].astype(F32)
    narrow[3, :, 0:HD] = dense[:, TILE:PART].astype(F32)
    small_rows[...] = jnp.zeros_like(small_rows)
    small_rows[SMALL : SMALL + 2, 0:24] = gains[...].astype(F32)
    small_rows[SMALL + 2 : SMALL + 4, 0:24] = shifts[...].astype(F32)
    small_rows[SMALL + 4 : SMALL + 6, 0:24] = outs[...].astype(F32)
    columns = small_rows[...].T[0:24]

    small_rows[...] = jnp.zeros_like(small_rows)
    small_rows[0:2, 0:12] = fc1_small[...].astype(F32)
    for which in range(3):
        small_rows[8 + 8 * which : 10 + 8 * which, 0:3] = qkv_small[which].astype(F32)
    turned = small_rows[...].T[0:16]
    pair_lane = lanes((16, TILE)) < 2
    bias_rows[0:16, :] = jnp.where(pair_lane, turned, 0.0)
    bias_rows[16:24, :] = jnp.zeros((8, TILE), F32)
    for which in range(3):
        moved = pltpu.roll(turned, TILE - 8 - 8 * which, axis=1)
        bias_rows[12 + 3 * which : 15 + 3 * which, :] = jnp.where(pair_lane, moved, 0.0)[0:3]
    biases = pltpu.roll(bias_rows[...], 2 * own, axis=1)
    key = qkv[1, :, 0:TILE].astype(F32)
    value = qkv[2, :, 0:TILE].astype(F32)
    left = lanes((24, TILE)) < HD
    top_half = jnp.concatenate(
        [
            jnp.where(left, key, swap_halves(value)),
            jnp.where(left, swap_halves(key), value),
            narrow[1] + swap_halves(narrow[2]),
            dense[:, 0:TILE].astype(F32),
        ],
        axis=1,
    )
    bottom_half = jnp.concatenate(
        [qkv[0, :, 0:TILE].astype(F32), narrow[0] + columns, narrow[3], biases], axis=1
    )
    slots[own, :, 0:EARLY] = jnp.concatenate([top_half, bottom_half], axis=0).astype(BF16)
    slots[own, :, EARLY:HALF] = jnp.concatenate([fc1[...].astype(F32), fc2[...].astype(F32)], axis=0).astype(BF16)
    net.enter()
    early = Gather(net, slots, own, 0, 256, EARLY)
    late = Gather(net, slots, own, EARLY, 896, HALF)
    early.one()

    wait(brought[4:7])
    row_cos, row_sin = angle_rows[0], angle_rows[1]
    block_cos, block_sin = angle_block[0, pl.ds(block, 1), :], angle_block[1, pl.ds(block, 1), :]
    cosine[...] = row_cos * block_cos - row_sin * block_sin
    sine = row_sin * block_cos + row_cos * block_sin
    upward = lanes((ROWS, TILE)) >= ROT // 2
    sine_up[...] = jnp.where(upward, sine, 0.0)
    sine_down[...] = jnp.where(upward, 0.0, -sine)

    early.two()
    late.one()
    mine_t = cot_t.at[pl.ds(pl.multiple_of(y * PART, 16), PART), :]
    gather_y = [net.copy(cot_own, mine_t, net.at_y(step)) for step in (1, 2, 3)]
    start(gather_y)
    mine_t[...] = cot_own[...]

    @pl.loop(0, 4)
    def _(index):
        rows = tile_at(index)
        normed, scale = standardize(tok[rows, :])
        xhat[rows, :] = normed
        rstd[rows, :] = jnp.broadcast_to(scale, (TILE, TILE))


    @pl.loop(0, 4)
    def _(index):
        rows = tile_at(index)
        tok_t[:, rows] = tok[rows, :].astype(F32).T.astype(BF16)

    early.three()
    late.two()
    dkv[...] = jnp.zeros_like(dkv)
    early.end()
    bias_rows[...] = jnp.zeros_like(bias_rows)

    @pl.loop(0, 16)
    def _(pair):
        rows = pl.ds(pl.multiple_of(pair * 48, 16), 48)
        one = slots[2 * pair, :, 0:EARLY].astype(F32)
        two = slots[2 * pair + 1, :, 0:EARLY].astype(F32)
        upper_rows = jnp.concatenate([one[0:24], two[0:24]], axis=0).astype(BF16)
        lower_rows = jnp.concatenate([one[24:48], two[24:48]], axis=0).astype(BF16)
        w2[rows, 0:384] = upper_rows[:, 0:384]
        w2[rows, 640:768] = upper_rows[:, 384:512]
        w2[rows, 384:640] = lower_rows[:, 0:256]
        w2[rows, 768:896] = lower_rows[:, 256:384]
        bias_rows[...] += one[24:48, 384:512] + two[24:48, 384:512]

    column_form = w2[:, 512:640].astype(F32)
    out_col[...] = jnp.broadcast_to(
        column_form[:, SMALL + 4 : SMALL + 5] + column_form[:, SMALL + 5 : SMALL + 6], (WIDE, TILE)
    )
    turned = column_form.T[SMALL : SMALL + 16, :]
    small[...] = turned
    even, odd = bias_rows[...], swap_halves(bias_rows[...])
    for number in range(6):
        bias[1:2, number * TILE : number * TILE + TILE] = (
            even[2 * number : 2 * number + 1] + odd[2 * number + 1 : 2 * number + 2]
        )
    for head in range(3):
        bias[0:1, head * TILE : head * TILE + TILE] = even[15 + head : 16 + head] + odd[18 + head : 19 + head]
    bias[0:1, 384:512] = even[12:13] + odd[13:14]
    bias[0:1, 512:640] = even[14:15]

    @pl.loop(0, 4)
    def _(index):
        rows = tile_at(index)
        normed = xhat[rows, :]
        one = (normed * small[0:1, :] + small[2:3, :]).astype(BF16)
        n1[rows, :] = one
        n2[rows, :] = (normed * small[1:2, :] + small[3:4, :]).astype(BF16)
        projected = dot(one, w2[:, QKV]) + bias[0:1, 0:640]
        turning = (cosine[rows, :], sine_up[rows, :], sine_down[rows, :])
        for head in range(3):
            span = slice(head * TILE, head * TILE + TILE)
            kv[block, rows, span] = turn(projected[:, span], *turning).astype(BF16)
        pair, last = projected[:, 384:512], projected[:, 512:640]
        for head, tile in enumerate((pair, swap_halves(pair), last)):
            span = slice(head * TILE, head * TILE + TILE)
            qd[rows, span] = (low_half(turn(low_half(tile), *turning)) * 0.125).astype(BF16)

    spans = [slice(head * TILE, head * TILE + TILE) for head in range(3)]
    send_own, send_prior, receive, given = [], [], [], []
    for step in (1, 2, 3):
        behind = z + step <= 3
        send_own.append(either(behind, both(lower, both(z + step == 4, z <= 2))))
        send_prior.append(both(upper, z + step > 3))
        receive.append(either(upper, either(z - step >= 0, both(z == 0, step >= 2))))
        given.append((z - step + 4) % 4 + 4 * xhi * ((z - step + 4) // 4))
    head_span = lambda head: pl.ds(pl.multiple_of(head * TILE, TILE), TILE)
    across_at, along_at, return_at, relay_at, part_at, stat_at, dq_at, top_at = (
        net.take(count) for count in (3, 9, 9, 3, 3, 3, 3, 3)
    )

    def across(head):
        mine = kv.at[block, :, head_span(head)]
        return net.copy(mine, mine, net.at_x(2), across_at + head)

    def along(head, step):
        piece = kv.at[block - 4 * xhi * ((z + step + 1) // 4), :, head_span(head)]
        return net.copy(piece, piece, net.at_z(step + 1), along_at + 3 * head + step)

    @pl.loop(0, 3)
    def _(head):
        pl.when(lower)(across(head).start)
        for step in range(3):
            pl.when(send_own[step])(along(head, step).start)

    late.three()


    wait(gather_y)

    @pl.loop(0, 4)
    def _(index):
        rows = tile_at(index)
        cot[rows, :] = cot_t[:, rows].astype(F32).T.astype(BF16)

    out_sums = jnp.sum(cot_t[...].astype(F32), axis=1, keepdims=True)

    @pl.loop(0, 4)
    def _(index):
        rows = tile_at(index)
        d_heads = dot(cot[rows, :], w2[:, DENSE])
        pair, last = d_heads[:, 0:TILE], d_heads[:, TILE : 2 * TILE]
        for head, tile in enumerate((swap_halves(pair), pair, swap_halves(last))):
            qd[rows, spans[head]] = (qd[rows, spans[head]].astype(F32) + high_half(tile)).astype(BF16)

    lend = net.copy(qd, qd_in, net.pal())
    pl.when(helped)(lend.start)

    @pl.loop(0, 3)
    def _(head):
        pl.when(upper)(across(head).wait_recv)
        for step in range(3):
            pl.when(send_prior[step])(along(head, step).start)

    late.end()

    @pl.loop(0, 16)
    def _(pair):
        rows = pl.ds(pl.multiple_of(pair * 48, 16), 48)
        one = slots[2 * pair, :, EARLY:HALF].astype(F32)
        two = slots[2 * pair + 1, :, EARLY:HALF].astype(F32)
        w2[rows, FC1] = jnp.concatenate([one[0:24], two[0:24]], axis=0).astype(BF16)
        w2[rows, FC2] = jnp.concatenate([one[24:48], two[24:48]], axis=0).astype(BF16)

    srow[...] = jnp.zeros_like(srow)

    @pl.loop(0, 4)
    def _(index):
        rows = tile_at(index)
        hidden = dot(n2[rows, :], w2[:, FC1]) + bias[1:2, :]
        spread_to = 0.5 + 0.5 * lax.erf(hidden * (0.5**0.5))
        act[rows, :] = (hidden * spread_to).astype(BF16)
        slope = spread_to + hidden * jnp.exp(-0.5 * hidden * hidden) * 0.3989422804014327
        d_hidden = (slope * dot(cot[rows, :], w2[:, FC2])).astype(BF16)
        dhid[rows, :] = d_hidden
        d_norm = dot_nt(d_hidden, w2[:, FC1])
        normed = xhat[rows, :]
        dx2[rows, :] = norm_back(small[1:2, :] * d_norm, normed, rstd[rows, 0:1])
        srow[0:8, :] += fold(d_norm * normed)
        srow[8:16, :] += fold(d_norm)
        srow[16:24, :] += fold(d_hidden.astype(F32))

    for half in (0, 1):
        span = slice(half * 384, half * 384 + 384)
        mlp_t[span, :] = dot_nt(w2[span, FC2], act[...])
        gq[0:384, 0:WIDE] = dot_tn(n2[:, span], dhid[...])
        gq[384:768, 0:WIDE] = dot(cot_t[span, :], act[...])

        @pl.loop(0, 16)
        def _(index):
            first = pl.ds(pl.multiple_of(index * 24, 8), 24)
            second = pl.ds(pl.multiple_of(384 + index * 24, 8), 24)
            slots[half * 16 + index, :, EARLY:HALF] = jnp.concatenate(
                [gq[first, 0:WIDE], gq[second, 0:WIDE]], axis=0
            ).astype(BF16)

    fc_sum = Reduce(
        net, slots, EARLY, 896, HALF, twin_in, halves, late_a, late_b, late_sa, late_sb, late_ea, late_eb
    )
    fc_sum.one()

    row_is_low = lax.broadcasted_iota(jnp.int32, (TILE, ROWS), 0) < HD
    lent_count = (1 - xhi) * (3 - z)
    chunk_count = 4 + xhi

    def chunk_place(index):
        which = (lent_count + 7 - index) // 8
        return which, index - lent_count * (1 - which) + xhi * z

    def partial(head):
        return net.copy(part_out.at[head], part_in.at[head], net.pal(), part_at + head)

    def partial_top(head):
        return net.copy(part_top.at[head], part_top_in.at[head], net.pal(), top_at + head)

    def stat_copy(head):
        return net.copy(stat.at[0, head], stat.at[1, head], net.pal(), stat_at + head)

    def dq_copy(head):
        return net.copy(dq_out.at[head], dq_in.at[head], net.pal(), dq_at + head)

    def tops_of(which):
        total = jnp.broadcast_to(column_sum(totals[which]), (8, ROWS))
        return jnp.where(lax.broadcasted_iota(jnp.int32, (8, ROWS), 0) == 0, top[which], total)

    @pl.when(jnp.logical_not(helped))
    def _():
        part_in[...] = jnp.zeros_like(part_in)
        is_top = lax.broadcasted_iota(jnp.int32, (3, 8, ROWS), 1) == 0
        part_top_in[...] = jnp.where(is_top, -1e30, 0.0)
        dq_in[...] = jnp.zeros_like(dq_in)

    def ahead(head):
        span = head_span(head)
        pl.when(lower)(across(head).wait_send)
        for step in range(3):
            pl.when(receive[step])(along(head, step).wait_recv)

        def turn_queries(source, which):
            turned = source[:, span].astype(F32).T
            qdt[which * 3 + head] = turned.astype(BF16)
            query_t[which] = jnp.where(row_is_low, turned, 0.0).astype(BF16)

        turn_queries(qd, 0)
        top[...] = jnp.full_like(top, -1e30)
        totals[...] = jnp.zeros_like(totals)
        summed[...] = jnp.zeros_like(summed)

        @pl.loop(0, chunk_count)
        def _(turn_of):
            index = (turn_of + lent_count) % chunk_count

            @pl.when(both(helps, turn_of == chunk_count - lent_count))
            def _():
                pl.when(head == 0)(lend.wait_recv)
                turn_queries(qd_in, 1)

            which, at = chunk_place(index)
            chunk = head * 5 + index
            tile = kv[at, :, span]
            tile_t = tile.astype(F32).T.astype(BF16)
            kv_t[chunk] = tile_t
            key_shift = (at - block - which * (7 - 2 * block)) * ROWS
            parts = [slice(half * 256, half * 256 + 256) for half in (0, 1)]
            scores = [dot(tile, query_t[which, :, part]) for part in parts]
            before = [top[which, 0:1, part] for part in parts]
            old_total = [totals[which, :, part] for part in parts]
            old_sum = [summed[which, :, part] for part in parts]
            for half, part in enumerate(parts):
                score = scores[half]
                key_at = lax.broadcasted_iota(jnp.int32, score.shape, 0) + key_shift
                query_at = lax.broadcasted_iota(jnp.int32, score.shape, 1) + half * 256
                score = jnp.where(key_at <= query_at, score, -1e30)
                peak = jnp.maximum(before[half], jnp.max(score, axis=0, keepdims=True))
                weight = jnp.exp(score - peak)
                shrink = jnp.exp(before[half] - peak)
                rounded = weight.astype(BF16)
                weights[chunk, :, part] = rounded
                peaks = jnp.broadcast_to(peak, (8, 256))
                tops[chunk, :, part] = peaks
                top[which, :, part] = peaks
                totals[which, :, part] = old_total[half] * shrink + fold(weight)
                summed[which, :, part] = old_sum[half] * shrink + dot(tile_t, rounded)

            @pl.when(both(helps, turn_of == chunk_count - 1))
            def _():
                part_out[head] = summed[1, HD:TILE, :].astype(BF16)
                part_top[head] = tops_of(1)
                partial(head).start()
                partial_top(head).start()

        kept[head, 0:HD, :] = summed[0, HD:TILE, :]
        kept[head, HD : HD + 8, :] = tops_of(0)

    def merge(head):
        pl.when(helped)(partial(head).wait_recv)
        pl.when(helped)(partial_top(head).wait_recv)
        top_one, top_two = kept[head, HD : HD + 1, :], part_top_in[head, 0:1, :]
        peak = jnp.maximum(top_one, top_two)
        share_one, share_two = jnp.exp(top_one - peak), jnp.exp(top_two - peak)
        total = kept[head, HD + 1 : HD + 2, :] * share_one + part_top_in[head, 1:2, :] * share_two
        inverse = 1.0 / total
        result = (kept[head, 0:HD, :] * share_one + part_in[head].astype(F32) * share_two) * inverse
        delta = column_sum(qdt[head, HD:TILE, :].astype(F32) * result)
        kept[head, 0:HD, :] = result
        row = lax.broadcasted_iota(jnp.int32, (8, ROWS), 0)
        stat[0, head] = jnp.where(row == 0, peak, jnp.where(row == 1, inverse, delta))
        pl.when(helped)(stat_copy(head).start)

    def give_back(head, step):
        return net.copy(
            dkv.at[given[step], :, head_span(head)],
            from_z.at[step, :, head_span(head)],
            net.at_z(3 - step),
            return_at + 3 * head + step,
        )

    def relay_copy(head):
        return net.copy(to_x.at[:, head_span(head)], from_x.at[:, head_span(head)], net.at_x(2), relay_at + head)

    def relay(head):
        span = head_span(head)
        for step in range(3):
            pl.when(either(send_own[step], send_prior[step]))(give_back(head, step).wait_recv)

        @pl.when(upper)
        def _():
            total_kv[:, span] = dkv[z, :, span].astype(F32)
            for step in range(3):

                @pl.when(send_prior[step])
                def _():
                    total_kv[:, span] += from_z[step, :, span].astype(F32)

            to_x[:, span] = total_kv[:, span].astype(BF16)
            relay_copy(head).start()

    def back(head):
        span = head_span(head)
        query_n[0] = low_half(qd[:, span].astype(F32)).astype(BF16)

        @pl.when(helps)
        def _():
            query_n[1] = low_half(qd_in[:, span].astype(F32)).astype(BF16)

        summed[...] = jnp.zeros_like(summed)

        @pl.loop(0, chunk_count)
        def _(turn_of):
            index = (turn_of + lent_count) % chunk_count
            which, at = chunk_place(index)
            chunk = head * 5 + index
            pl.when(both(helps, turn_of == chunk_count - lent_count))(stat_copy(head).wait_recv)
            change = dkv[at, :, span].astype(F32)
            for half in (0, 1):
                part = slice(half * 256, half * 256 + 256)
                factor = jnp.exp(tops[chunk, 0:1, part] - stat[which, head, 0:1, part]) * stat[which, head, 1:2, part]
                weight = weights[chunk, :, part]
                scaled = jnp.where(
                    row_is_low[:, 0:256], 0.0, qdt[which * 3 + head, :, part].astype(F32) * factor
                )
                d_weight = dot(kv[at, :, span], scaled.astype(BF16))
                d_score = (
                    weight.astype(F32) * (d_weight - stat[which, head, 2:3, part] * factor)
                ).astype(BF16)
                change = change + dot(d_score, query_n[which, part, :]) + dot(weight, scaled.T.astype(BF16))
                summed[which, :, part] += dot(kv_t[chunk], d_score)
            dkv[at, :, span] = change.astype(BF16)

        dq_t[head] = summed[0, 0:HD, :]

        @pl.when(helps)
        def _():
            dq_out[head] = summed[1, 0:HD, :].astype(BF16)
            dq_copy(head).start()

        for step in range(3):
            pl.when(receive[step])(give_back(head, step).start)

    @pl.loop(0, 4)
    def _(index):
        pl.when(index < 3)(lambda: ahead(index))
        pl.when(index == 0)(fc_sum.two)
        pl.when(index == 3)(fc_sum.three)
        pl.when(index > 0)(lambda: back(index - 1))
        pl.when(index < 3)(lambda: merge(index))
        pl.when(index > 1)(lambda: relay(index - 2))

    heads[:, 0:TILE] = jnp.concatenate([kept[0, 0:HD, :], kept[1, 0:HD, :]], axis=0).T.astype(BF16)
    heads[:, TILE : 2 * TILE] = jnp.concatenate(
        [kept[2, 0:HD, :], jnp.zeros((HD, ROWS), F32)], axis=0
    ).T.astype(BF16)


    for half in (0, 1):
        span = slice(half * 384, half * 384 + 384)
        out_send[span, :] = (mlp_t[span, :] + dot_nt(w2[span, DENSE], heads[...])).astype(BF16)
        gq[span, DENSE] = dot(cot_t[span, :], heads[...])

    def part_of(number):
        return pl.ds(pl.multiple_of(number * PART, 16), PART)

    out_copies = [
        net.copy(out_send.at[part_of((y + step) % 4), :], out_recv.at[step - 1], net.at_y(step))
        for step in (1, 2, 3)
    ]
    start(out_copies)


    relay(2)

    @pl.loop(0, 3)
    def _(head):
        pl.when(helped)(dq_copy(head).wait_recv)
        pl.when(lower)(relay_copy(head).wait_recv)

    total_kv[...] = dkv[block].astype(F32)
    for step in range(3):

        @pl.when(send_own[step])
        def _():
            total_kv[...] += from_z[step].astype(F32)

    @pl.when(lower)
    def _():
        total_kv[...] += from_x[...].astype(F32)

    rowsum[...] = jnp.zeros_like(rowsum)

    @pl.loop(0, 4)
    def _(index):
        rows = tile_at(index)
        turning = (cosine[rows, :], -sine_up[rows, :], -sine_down[rows, :])
        pieces = [turn(total_kv[rows, spans[head]], *turning) for head in range(3)]
        query = []
        for head in range(3):
            grad = (dq_t[head, :, rows] + dq_in[head, :, rows].astype(F32)) * 0.125
            grad = jnp.concatenate([grad, jnp.zeros((HD, TILE), F32)], axis=0).T
            query.append(turn(grad, *turning))
        pieces.append(low_half(query[0]) + swap_halves(low_half(query[1])))
        pieces.append(low_half(query[2]))
        stacked = jnp.concatenate(pieces, axis=1).astype(BF16)
        dqkv[rows, :] = stacked
        d_norm = dot_nt(stacked, w2[:, QKV])
        normed = xhat[rows, :]
        d_input = dx2[rows, :] + norm_back(small[0:1, :] * d_norm, normed, rstd[rows, 0:1])
        rowsum[0:8, :] += fold(d_norm * normed)
        rowsum[8:16, :] += fold(d_norm)
        rowsum[16:24, 0:640] += fold(stacked.astype(F32))
        dx_send[:, rows] = d_input.T.astype(BF16)

    dx_copies = [
        net.copy(dx_send.at[part_of((y + step) % 4), :], dx_recv.at[step - 1], net.at_y(step))
        for step in (1, 2, 3)
    ]

    def whole(ref, at):
        return column_sum(ref[at : at + 8, :])

    y_send[...] = jnp.concatenate(
        [whole(rowsum, 0), whole(srow, 0), whole(rowsum, 8), whole(srow, 8), jnp.zeros((4, WIDE), F32)], axis=0
    )
    y_copies = [net.copy(y_send, y_recv.at[step - 1], net.at_y(step)) for step in (1, 2, 3)]
    start(y_copies + dx_copies)
    for half in (0, 1):
        span = slice(half * 384, half * 384 + 384)
        gq[span, QKV] = dot_tn(n1[:, span], dqkv[...])
    fc1_sum, qkv_total = whole(srow, 16), whole(rowsum, 16)
    pieces = []
    for number in range(12):
        pieces.append(fc1_sum[:, number // 2 * TILE : number // 2 * TILE + TILE])
    for number in (3, 3, 4, 0, 1, 2, 0, 1, 2):
        pieces.append(qkv_total[:, number * TILE : number * TILE + TILE])
    pieces.append(jnp.zeros((3, TILE), F32))
    bias_grads = jnp.concatenate(pieces, axis=0)
    row = lax.broadcasted_iota(jnp.int32, (24, TILE), 0)
    swapped = ((row < 12) & (row % 2 == 1)) | (row == 13) | (row >= 18)
    bias_rows[...] = jnp.where(swapped, swap_halves(bias_grads), bias_grads)
    wait(y_copies)
    shared = y_send[...] + y_recv[0] + y_recv[1] + y_recv[2]
    columns = jnp.concatenate(
        [
            jnp.zeros((SMALL, WIDE), F32),
            shared[0:4],
            jnp.zeros((2, WIDE), F32),
            jnp.zeros((58, WIDE), F32),
        ],
        axis=0,
    ).T
    lane = lanes((WIDE, TILE))
    columns = jnp.where((lane == SMALL + 4) | (lane == SMALL + 5), out_sums, columns)
    gq[:, 512:640] = jnp.where(lane < HD, gq[:, 512:640], columns)

    @pl.loop(0, 32)
    def _(index):
        rows = pl.ds(pl.multiple_of(index * 24, 8), 24)
        first = jnp.concatenate([gq[rows, 0:384], gq[rows, 640:768]], axis=1)
        second = jnp.concatenate([gq[rows, 384:640], gq[rows, 768:896], bias_rows[...]], axis=1)
        slots[index, :, 0:EARLY] = jnp.concatenate([first, second], axis=0).astype(BF16)

    qkv_sum = Reduce(
        net, slots, 0, 256, EARLY, twin_in, halves, early_a, early_b, early_sa, early_sb, early_ea, early_eb
    )
    qkv_sum.one()
    qkv_sum.two()

    wait(out_copies + dx_copies)
    mine = part_of(y)
    total = out_send[mine, :].astype(F32) + tok_t[mine, :].astype(F32) + out_col[mine, 0:1]
    grad = dx_send[mine, :].astype(F32) + cot_own[...].astype(F32)
    for step in range(3):
        total = total + out_recv[step].astype(F32)
        grad = grad + dx_recv[step].astype(F32)
    out_t[...] = total.astype(BF16)
    grad_t[...] = grad
    qkv_sum.three()

    @pl.loop(0, 3)
    def _(head):
        pl.when(helps)(partial(head).wait_send)
        pl.when(helps)(partial_top(head).wait_send)
        pl.when(helped)(stat_copy(head).wait_send)
        pl.when(helps)(dq_copy(head).wait_send)
        pl.when(upper)(relay_copy(head).wait_send)
        for step in range(3):
            pl.when(either(send_own[step], send_prior[step]))(along(head, step).wait_send)
            pl.when(receive[step])(give_back(head, step).wait_send)

    pl.when(helped)(lend.wait_send)
    fc_sum.end(final)
    qkv_sum.end(final)


def finish_kernel(
    out_in, grad_in, final, out_t, grad_t, gain, shift, qkv, qkv_small, dense, fc1, fc1_small, fc2, outs
):
    out_t[...] = out_in[...]
    grad_t[...] = grad_in[...]
    fc1[...] = final[0:24, EARLY:HALF]
    fc2[...] = final[24:48, EARLY:HALF]
    left = lanes((24, TILE)) < HD
    one, two, three = (final[0:24, head * TILE : head * TILE + TILE] for head in range(3))
    qkv[1, :, 0:TILE] = jnp.where(left, one, swap_halves(two))
    qkv[1, :, TILE:PART] = three[:, 0:HD]
    qkv[2, :, 0:TILE] = jnp.where(left, swap_halves(one), two)
    qkv[2, :, TILE:PART] = swap_halves(three)[:, 0:HD]
    qkv[0, :, 0:TILE] = final[24:48, 0:TILE]
    mixed = final[24:48, TILE : 2 * TILE]
    qkv[0, :, TILE:PART] = mixed[:, 0:HD]
    dense[:, 0:TILE] = final[0:24, 384:512]
    dense[:, TILE:PART] = final[24:48, 256 : 256 + HD]
    rows = jnp.concatenate([mixed, jnp.zeros((TILE - 24, TILE), F32)], axis=0).T
    gain[...] = rows[SMALL : SMALL + 2, 0:24]
    shift[...] = rows[SMALL + 2 : SMALL + 4, 0:24]
    outs[...] = rows[SMALL + 4 : SMALL + 6, 0:24]
    own = lax.axis_index("dp") * 8 + lax.axis_index("ctx")
    moved = pltpu.roll(final[24:48, 384:512], TILE - 2 * own, axis=1)
    rows = jnp.concatenate([moved, jnp.zeros((TILE - 24, TILE), F32)], axis=0).T
    fc1_small[...] = rows[0:2, 0:12]
    for which in range(3):
        qkv_small[which] = pltpu.roll(rows[0:8], TILE - 12 - 3 * which, axis=1)[0:2, 0:3]


def angle_tables():
    frequency = 10000.0 ** (-2.0 * np.arange(ROT // 2) / ROT)
    result = []
    for positions in (np.arange(ROWS), ROWS * np.arange(8)):
        phases = np.zeros((len(positions), TILE))
        phases[:, 0:ROT] = positions[:, None] * np.concatenate([frequency, frequency])[None, :]
        result.append(np.stack([np.cos(phases), np.sin(phases)]).astype(np.float32))
    return result


def call(kernel, name, shapes, scratch, collective, inputs, outside=()):
    options = dict(vmem_limit_bytes=VMEM_LIMIT)
    if collective is not None:
        options.update(collective_id=collective, has_side_effects=True)
    return pl.pallas_call(
        kernel,
        name=name,
        out_shape=[jax.ShapeDtypeStruct(shape, kind) for shape, kind in shapes],
        in_specs=[
            pl.BlockSpec(memory_space=pl.ANY if number in outside else pltpu.VMEM)
            for number in range(len(inputs))
        ],
        out_specs=[pl.BlockSpec(memory_space=pltpu.VMEM)] * len(shapes),
        scratch_shapes=scratch,
        compiler_params=pltpu.CompilerParams(**options),
    )(*inputs)


def shards(
    tokens,
    norm_gain,
    norm_bias,
    qkv_weight,
    qkv_bias,
    dense_weight,
    fc1_weight,
    fc1_bias,
    fc2_weight,
    out_bias,
    cotangent,
):
    vm = pltpu.VMEM
    dma = pltpu.SemaphoreType.DMA
    wide = (ROWS, WIDE)
    row_angles, block_angles = angle_tables()
    out_t, grad_t, final = call(
        layer_kernel,
        "layer",
        [((PART, ROWS), BF16), ((PART, ROWS), F32), ((48, HALF), F32)],
        [
            vm(wide, BF16),
            vm((3, 24, PART), BF16),
            vm((24, PART), BF16),
            vm((24, WIDE), BF16),
            vm((24, WIDE), BF16),
            vm((PART, ROWS), BF16),
            vm((2, ROWS, TILE), F32),
            dma((7,)),
            vm((32, 48, HALF), BF16),
            vm((WIDE, 2432), BF16),
            vm((16, WIDE), F32),
            vm((8, WIDE), F32),
            vm((TILE, TILE), F32),
            vm((4, 24, TILE), F32),
            vm((24, TILE), F32),
            vm((WIDE, TILE), F32),
            vm((ROWS, TILE), F32),
            vm((ROWS, TILE), F32),
            vm((ROWS, TILE), F32),
            vm(wide, F32),
            vm((ROWS, TILE), F32),
            vm((WIDE, ROWS), BF16),
            vm(wide, BF16),
            vm(wide, BF16),
            vm(wide, BF16),
            vm(wide, BF16),
            vm((WIDE, ROWS), BF16),
            vm(wide, BF16),
            vm((WIDE, ROWS), F32),
            vm(wide, F32),
            vm((24, WIDE), F32),
            vm((ROWS, 384), BF16),
            vm((ROWS, 384), BF16),
            vm((6, TILE, ROWS), BF16),
            vm((8, ROWS, 384), BF16),
            vm((8, ROWS, 384), BF16),
            vm((15, TILE, ROWS), BF16),
            vm((15, ROWS, ROWS), BF16),
            vm((15, 8, ROWS), F32),
            vm((2, 8, ROWS), F32),
            vm((2, 8, ROWS), F32),
            vm((2, TILE, ROWS), F32),
            vm((2, TILE, ROWS), BF16),
            vm((2, ROWS, TILE), BF16),
            vm((3, HD, ROWS), BF16),
            vm((3, HD, ROWS), BF16),
            vm((3, 8, ROWS), F32),
            vm((3, 8, ROWS), F32),
            vm((2, 3, 8, ROWS), F32),
            vm((3, HD, ROWS), BF16),
            vm((3, HD, ROWS), BF16),
            vm((3, HD, ROWS), F32),
            vm((3, 80, ROWS), F32),
            vm((WIDE, 896), F32),
            vm((16, 48, HALF), BF16),
            vm((16, 48, HALF), BF16),
            vm((3, 4, 48, 256), BF16),
            vm((3, 4, 48, 256), BF16),
            vm((4, 48, 256), BF16),
            vm((4, 48, 256), BF16),
            vm((3, 48, 256), BF16),
            vm((3, 48, 256), BF16),
            vm((3, 4, 48, 384), BF16),
            vm((3, 4, 48, 384), BF16),
            vm((4, 48, 384), BF16),
            vm((4, 48, 384), BF16),
            vm((3, 48, 384), BF16),
            vm((3, 48, 384), BF16),
            vm((3, ROWS, 384), BF16),
            vm((ROWS, 384), BF16),
            vm((ROWS, 384), BF16),
            vm((ROWS, 256), BF16),
            vm((WIDE, ROWS), BF16),
            vm((3, PART, ROWS), BF16),
            vm((WIDE, ROWS), BF16),
            vm((3, PART, ROWS), BF16),
            vm((24, WIDE), F32),
            vm((8, WIDE), F32),
            vm((3, 8, WIDE), F32),
            dma((192,)),
            dma((192,)),
        ],
        0,
        [
            tokens[0],
            norm_gain,
            norm_bias,
            out_bias,
            jnp.transpose(qkv_weight, (1, 0, 2)),
            jnp.transpose(qkv_bias, (0, 2, 1)),
            dense_weight.T,
            fc1_weight,
            fc1_bias.T,
            fc2_weight.T,
            cotangent[0].T,
            jnp.asarray(row_angles),
            jnp.asarray(block_angles),
        ],
        (0, 4, 6, 7, 9, 10, 11),
    )
    out_t, grad_t, gain, shift, qkv, qkv_small, dense, fc1, fc1_small, fc2, outs = call(
        finish_kernel,
        "finish",
        [
            ((PART, ROWS), BF16),
            ((PART, ROWS), F32),
            ((2, 24), F32),
            ((2, 24), F32),
            ((3, 24, PART), F32),
            ((3, 2, 3), F32),
            ((24, PART), F32),
            ((24, WIDE), F32),
            ((2, 12), F32),
            ((24, WIDE), F32),
            ((2, 24), F32),
        ],
        [],
        None,
        [out_t, grad_t, final],
    )
    return (
        out_t.T[None],
        grad_t.T[None],
        gain,
        shift,
        jnp.transpose(qkv, (1, 0, 2)),
        jnp.transpose(qkv_small, (0, 2, 1)),
        dense.T,
        fc1,
        fc1_small.T,
        fc2.T,
        outs,
    )


def solution(mesh):
    return jax.shard_map(
        shards,
        mesh=mesh,
        in_specs=(
            P("dp", "ctx", None),
            P(None, ("dp", "ctx")),
            P(None, ("dp", "ctx")),
            P(("dp", "ctx"), None, "tensor"),
            P(None, "tensor", ("dp", "ctx")),
            P("tensor", ("dp", "ctx")),
            P(("dp", "ctx"), "tensor"),
            P("tensor", ("dp", "ctx")),
            P("tensor", ("dp", "ctx")),
            P(None, ("dp", "ctx")),
            P("dp", "ctx", "tensor"),
        ),
        out_specs=(
            P("dp", "ctx", "tensor"),
            P("dp", "ctx", "tensor"),
            P(None, ("dp", "ctx")),
            P(None, ("dp", "ctx")),
            P(("dp", "ctx"), None, "tensor"),
            P(None, "tensor", ("dp", "ctx")),
            P("tensor", ("dp", "ctx")),
            P(("dp", "ctx"), "tensor"),
            P("tensor", ("dp", "ctx")),
            P("tensor", ("dp", "ctx")),
            P(None, ("dp", "ctx")),
        ),
        check_vma=False,
    )
```

```python
import jax
import jax.numpy as jnp
import numpy as np
from jax import lax
from jax.experimental import pallas as pl
from jax.experimental.pallas import tpu as pltpu
from jax.sharding import PartitionSpec as P

HD = 64
ROT = 16
EPSILON = 1e-05
ROWS = 512
WIDE = 768
HALF = 1280
PART = 192
TILE = 128
MESH = pl.DeviceIdType.MESH
VMEM_LIMIT = 61 << 20
F32 = jnp.float32
BF16 = jnp.bfloat16

QKV = slice(0, 640)
DENSE = slice(640, 896)
FC1 = slice(896, 1664)
FC2 = slice(1664, 2432)
EARLY = 512
SMALL = 64


def dot(a, b):
    return lax.dot_general(a, b, (((1,), (0,)), ((), ())), preferred_element_type=F32)


def dot_nt(a, b):
    return lax.dot_general(a, b, (((1,), (1,)), ((), ())), preferred_element_type=F32)


def dot_tn(a, b):
    return lax.dot_general(a, b, (((0,), (0,)), ((), ())), preferred_element_type=F32)


def device(x, y, z, core):
    return {"dp": (x % 2) * 2 + core, "ctx": (x // 2) * 4 + z, "tensor": y}


class Links:
    def __init__(self, send, recv):
        dp = lax.axis_index("dp")
        cx = lax.axis_index("ctx")
        self.xlo, self.core, self.xhi, self.z = dp // 2, dp % 2, cx // 4, cx % 4
        self.y = lax.axis_index("tensor")
        self.x = self.xhi * 2 + self.xlo
        self.send, self.recv, self.used = send, recv, 0

    def at_x(self, step):
        return device((self.x + step) % 4, self.y, self.z, self.core)

    def at_z(self, step):
        return device(self.x, self.y, (self.z + step) % 4, self.core)

    def at_y(self, step):
        return device(self.x, (self.y + step) % 4, self.z, self.core)

    def twin(self):
        return device(self.x, self.y, self.z, 1 - self.core)

    def pal(self):
        return device((self.x + 2) % 4, self.y, 3 - self.z, self.core)

    def knock(self):
        self.barrier = pltpu.get_barrier_semaphore()
        peers = [self.twin(), self.pal()]
        for step in (1, 2, 3):
            peers += [self.at_x(step), self.at_z(step), self.at_y(step)]
        for peer in peers:
            pl.semaphore_signal(self.barrier, inc=1, device_id=peer, device_id_type=MESH)
        self.expected = len(peers)

    def enter(self):
        pl.semaphore_wait(self.barrier, self.expected)

    def take(self, count):
        self.used += count
        return self.used - count

    def copy(self, source, target, peer, number=None):
        if number is None:
            number = self.take(1)
        return pltpu.make_async_remote_copy(
            src_ref=source,
            dst_ref=target,
            send_sem=self.send.at[number],
            recv_sem=self.recv.at[number],
            device_id=peer,
            device_id_type=MESH,
        )


def start(copies):
    for item in copies:
        item.start()


def wait(copies):
    for item in copies:
        item.wait()


def lanes(shape):
    return lax.broadcasted_iota(jnp.int32, shape, len(shape) - 1)


def low_half(tile):
    return jnp.where(lanes(tile.shape) < HD, tile, 0.0)


def high_half(tile):
    return jnp.where(lanes(tile.shape) >= HD, tile, 0.0)


def swap_halves(tile):
    return pltpu.roll(tile, HD, axis=1)


def turn(tile, cosine, sine_up, sine_down):
    return (
        tile * cosine
        + pltpu.roll(tile, ROT // 2, axis=1) * sine_up
        + pltpu.roll(tile, TILE - ROT // 2, axis=1) * sine_down
    )


def fold(block):
    rows, width = block.shape
    return jnp.sum(block.reshape(rows // 8, 8, width), axis=0)


def column_sum(block):
    return jnp.sum(block, axis=0, keepdims=True)


def standardize(rows_in):
    values = rows_in.astype(F32)
    centred = values - jnp.mean(values, axis=-1, keepdims=True)
    scale = lax.rsqrt(jnp.mean(centred * centred, axis=-1, keepdims=True) + EPSILON)
    return centred * scale, scale


def norm_back(gradient, xhat, scale):
    return scale * (
        gradient
        - jnp.mean(gradient, axis=-1, keepdims=True)
        - xhat * jnp.mean(gradient * xhat, axis=-1, keepdims=True)
    )


def tile_at(index):
    return pl.ds(pl.multiple_of(index * TILE, TILE), TILE)


def quad(position):
    return (position % 2) * 2 + position // 2


class Gather:
    def __init__(self, net, slots, own, low, middle, high):
        first, second = slice(low, middle), slice(middle, high)
        mine_a, mine_b = slots.at[own, :, first], slots.at[own, :, second]
        four = slots.at[pl.ds(own - net.z, 4), :, first]
        steps = (1, 2, 3)
        self.a = [net.copy(mine_a, mine_a, net.at_z(step)) for step in steps]
        self.b = [net.copy(mine_b, mine_b, net.at_x(step)) for step in steps]
        self.mid_a = [net.copy(four, four, net.at_x(step)) for step in steps]
        self.mid_b, self.last_a, self.last_b = [], [], []
        for low in (0, 1):
            for high in (0, 1):
                piece = slots.at[((low * 2 + net.core) * 2 + high) * 4 + net.z, :, second]
                self.mid_b += [net.copy(piece, piece, net.at_z(step)) for step in steps]
            for span, copies in ((first, self.last_a), (second, self.last_b)):
                piece = slots.at[pl.ds((low * 2 + net.core) * 8, 8), :, span]
                copies.append(net.copy(piece, piece, net.twin()))

    def one(self):
        start(self.a + self.b)

    def two(self):
        wait(self.a)
        start(self.mid_a)
        wait(self.b)
        start(self.mid_b)

    def three(self):
        wait(self.mid_a)
        start(self.last_a)
        wait(self.mid_b)
        start(self.last_b)

    def end(self):
        wait(self.last_a + self.last_b)


class Reduce:
    def __init__(self, net, slots, low, middle, high, twin_in, halves, in_a, in_b, sum_a, sum_b, end_a, end_b):
        self.net, self.slots = net, slots
        self.whole, self.first, self.second = slice(low, high), slice(low, middle), slice(middle, high)
        self.bufs = (twin_in, halves, in_a, in_b, sum_a, sum_b, end_a, end_b)
        self.me = quad(net.x)
        self.twins = [
            net.copy(
                slots.at[pl.ds((low * 2 + 1 - net.core) * 8, 8), :, self.whole],
                twin_in.at[pl.ds(low * 8, 8), :, self.whole],
                net.twin(),
            )
            for low in (0, 1)
        ]
        self.mid_a, self.mid_b, self.last_a, self.last_b = [], [], [], []
        for step in (1, 2, 3):
            there = quad((net.x + step) % 4)
            self.mid_a.append(
                net.copy(halves.at[pl.ds(there * 4, 4), :, self.first], in_a.at[step - 1], net.at_x(step))
            )
            for which in range(4):
                self.mid_b.append(
                    net.copy(
                        halves.at[which * 4 + (net.z + step) % 4, :, self.second],
                        in_b.at[step - 1, which],
                        net.at_z(step),
                    )
                )
            self.last_a.append(net.copy(sum_a.at[(net.z + step) % 4], end_a.at[step - 1], net.at_z(step)))
            self.last_b.append(net.copy(sum_b.at[there], end_b.at[step - 1], net.at_x(step)))

    def one(self):
        start(self.twins)

    def two(self):
        twin_in, halves = self.bufs[:2]
        wait(self.twins)

        @pl.loop(0, 16)
        def _(index):
            source = (index // 8 * 2 + self.net.core) * 8 + index % 8
            halves[index, :, self.whole] = (
                self.slots[source, :, self.whole].astype(F32) + twin_in[index, :, self.whole].astype(F32)
            ).astype(BF16)

        start(self.mid_a + self.mid_b)

    def three(self):
        halves, in_a, in_b, sum_a, sum_b = self.bufs[1:6]
        wait(self.mid_a)

        @pl.loop(0, 4)
        def _(index):
            total = halves[self.me * 4 + index, :, self.first].astype(F32)
            for step in range(3):
                total = total + in_a[step, index].astype(F32)
            sum_a[index] = total.astype(BF16)

        start(self.last_a)
        wait(self.mid_b)

        @pl.loop(0, 4)
        def _(index):
            total = halves[index * 4 + self.net.z, :, self.second].astype(F32)
            for step in range(3):
                total = total + in_b[step, index].astype(F32)
            sum_b[index] = total.astype(BF16)

        start(self.last_b)

    def end(self, target):
        sum_a, sum_b, end_a, end_b = self.bufs[4:]
        for copies, own, arrived, span in (
            (self.last_a, sum_a.at[self.net.z], end_a, self.first),
            (self.last_b, sum_b.at[self.me], end_b, self.second),
        ):
            wait(copies)
            total = own[...].astype(F32)
            for step in range(3):
                total = total + arrived[step].astype(F32)
            target[:, span] = total


def layer_kernel(
    tok_in, gains, shifts, outs, qkv_in, qkv_small, dense_in, fc1_in, fc1_small, fc2_in, cot_in, angle_in, angle_block,
    out_t, grad_t, final,
    tok, qkv, dense, fc1, fc2, cot_own, angle_rows, loads,
    slots, w2, small, bias, small_rows, narrow, bias_rows, out_col, cosine, sine_up, sine_down, xhat, rstd, tok_t, n1, n2, dhid, act,
    cot_t, cot, mlp_t, dx2, srow, qd, qd_in, qdt, kv, dkv, kv_t, weights, tops, top, totals, summed, query_t, query_n,
    part_out, part_in, part_top, part_top_in, stat, dq_out, dq_in, dq_t, kept, gq,
    twin_in, halves, early_a, early_b, early_sa, early_sb, early_ea, early_eb,
    late_a, late_b, late_sa, late_sb, late_ea, late_eb,
    from_z, from_x, to_x, heads, out_send, out_recv, dx_send, dx_recv, rowsum, y_send, y_recv,
    send, recv,
):
    net = Links(send, recv)
    xlo, core, xhi, z, y = net.xlo, net.core, net.xhi, net.z, net.y
    own = ((xlo * 2 + core) * 2 + xhi) * 4 + z
    block = xhi * 4 + z
    upper, lower = xhi == 1, xhi == 0
    both = jnp.logical_and
    either = jnp.logical_or
    brought = [
        pltpu.make_async_copy(source, target, loads.at[number])
        for number, (source, target) in enumerate(
            (
                (qkv_in, qkv),
                (dense_in, dense),
                (fc1_in, fc1),
                (fc2_in, fc2),
                (angle_in, angle_rows),
                (tok_in, tok),
                (cot_in, cot_own),
            )
        )
    ]
    start(brought)
    helps = both(lower, z <= 2)
    helped = both(upper, z >= 1)
    dqkv = n2.at[:, QKV]
    total_kv = gq.at[0:ROWS, 0:384]
    net.knock()

    wait(brought[0:4])
    narrow[...] = jnp.zeros_like(narrow)
    for which in range(3):
        narrow[which, :, 0:HD] = qkv[which, :, TILE:PART].astype(F32)
    narrow[3, :, 0:HD] = dense[:, TILE:PART].astype(F32)
    small_rows[...] = jnp.zeros_like(small_rows)
    small_rows[SMALL : SMALL + 2, 0:24] = gains[...].astype(F32)
    small_rows[SMALL + 2 : SMALL + 4, 0:24] = shifts[...].astype(F32)
    small_rows[SMALL + 4 : SMALL + 6, 0:24] = outs[...].astype(F32)
    columns = small_rows[...].T[0:24]

    small_rows[...] = jnp.zeros_like(small_rows)
    small_rows[0:2, 0:12] = fc1_small[...].astype(F32)
    for which in range(3):
        small_rows[8 + 8 * which : 10 + 8 * which, 0:3] = qkv_small[which].astype(F32)
    turned = small_rows[...].T[0:16]
    pair_lane = lanes((16, TILE)) < 2
    bias_rows[0:16, :] = jnp.where(pair_lane, turned, 0.0)
    bias_rows[16:24, :] = jnp.zeros((8, TILE), F32)
    for which in range(3):
        moved = pltpu.roll(turned, TILE - 8 - 8 * which, axis=1)
        bias_rows[12 + 3 * which : 15 + 3 * which, :] = jnp.where(pair_lane, moved, 0.0)[0:3]
    biases = pltpu.roll(bias_rows[...], 2 * own, axis=1)
    key = qkv[1, :, 0:TILE].astype(F32)
    value = qkv[2, :, 0:TILE].astype(F32)
    left = lanes((24, TILE)) < HD
    top_half = jnp.concatenate(
        [
            jnp.where(left, key, swap_halves(value)),
            jnp.where(left, swap_halves(key), value),
            narrow[1] + swap_halves(narrow[2]),
            dense[:, 0:TILE].astype(F32),
        ],
        axis=1,
    )
    bottom_half = jnp.concatenate(
        [qkv[0, :, 0:TILE].astype(F32), narrow[0] + columns, narrow[3], biases], axis=1
    )
    slots[own, :, 0:EARLY] = jnp.concatenate([top_half, bottom_half], axis=0).astype(BF16)
    slots[own, :, EARLY:HALF] = jnp.concatenate([fc1[...].astype(F32), fc2[...].astype(F32)], axis=0).astype(BF16)
    net.enter()
    early = Gather(net, slots, own, 0, 256, EARLY)
    late = Gather(net, slots, own, EARLY, 896, HALF)
    early.one()

    wait(brought[4:7])
    row_cos, row_sin = angle_rows[0], angle_rows[1]
    block_cos, block_sin = angle_block[0, pl.ds(block, 1), :], angle_block[1, pl.ds(block, 1), :]
    cosine[...] = row_cos * block_cos - row_sin * block_sin
    sine = row_sin * block_cos + row_cos * block_sin
    upward = lanes((ROWS, TILE)) >= ROT // 2
    sine_up[...] = jnp.where(upward, sine, 0.0)
    sine_down[...] = jnp.where(upward, 0.0, -sine)

    early.two()
    late.one()
    mine_t = cot_t.at[pl.ds(pl.multiple_of(y * PART, 16), PART), :]
    gather_y = [net.copy(cot_own, mine_t, net.at_y(step)) for step in (1, 2, 3)]
    start(gather_y)
    mine_t[...] = cot_own[...]

    @pl.loop(0, 4)
    def _(index):
        rows = tile_at(index)
        normed, scale = standardize(tok[rows, :])
        xhat[rows, :] = normed
        rstd[rows, :] = jnp.broadcast_to(scale, (TILE, TILE))


    @pl.loop(0, 4)
    def _(index):
        rows = tile_at(index)
        tok_t[:, rows] = tok[rows, :].astype(F32).T.astype(BF16)

    early.three()
    late.two()
    dkv[...] = jnp.zeros_like(dkv)
    early.end()
    bias_rows[...] = jnp.zeros_like(bias_rows)

    @pl.loop(0, 16)
    def _(pair):
        rows = pl.ds(pl.multiple_of(pair * 48, 16), 48)
        one = slots[2 * pair, :, 0:EARLY].astype(F32)
        two = slots[2 * pair + 1, :, 0:EARLY].astype(F32)
        upper_rows = jnp.concatenate([one[0:24], two[0:24]], axis=0).astype(BF16)
        lower_rows = jnp.concatenate([one[24:48], two[24:48]], axis=0).astype(BF16)
        w2[rows, 0:384] = upper_rows[:, 0:384]
        w2[rows, 640:768] = upper_rows[:, 384:512]
        w2[rows, 384:640] = lower_rows[:, 0:256]
        w2[rows, 768:896] = lower_rows[:, 256:384]
        bias_rows[...] += one[24:48, 384:512] + two[24:48, 384:512]

    column_form = w2[:, 512:640].astype(F32)
    out_col[...] = jnp.broadcast_to(
        column_form[:, SMALL + 4 : SMALL + 5] + column_form[:, SMALL + 5 : SMALL + 6], (WIDE, TILE)
    )
    turned = column_form.T[SMALL : SMALL + 16, :]
    small[...] = turned
    even, odd = bias_rows[...], swap_halves(bias_rows[...])
    for number in range(6):
        bias[1:2, number * TILE : number * TILE + TILE] = (
            even[2 * number : 2 * number + 1] + odd[2 * number + 1 : 2 * number + 2]
        )
    for head in range(3):
        bias[0:1, head * TILE : head * TILE + TILE] = even[15 + head : 16 + head] + odd[18 + head : 19 + head]
    bias[0:1, 384:512] = even[12:13] + odd[13:14]
    bias[0:1, 512:640] = even[14:15]

    @pl.loop(0, 4)
    def _(index):
        rows = tile_at(index)
        normed = xhat[rows, :]
        one = (normed * small[0:1, :] + small[2:3, :]).astype(BF16)
        n1[rows, :] = one
        n2[rows, :] = (normed * small[1:2, :] + small[3:4, :]).astype(BF16)
        projected = dot(one, w2[:, QKV]) + bias[0:1, 0:640]
        turning = (cosine[rows, :], sine_up[rows, :], sine_down[rows, :])
        for head in range(3):
            span = slice(head * TILE, head * TILE + TILE)
            kv[block, rows, span] = turn(projected[:, span], *turning).astype(BF16)
        pair, last = projected[:, 384:512], projected[:, 512:640]
        for head, tile in enumerate((pair, swap_halves(pair), last)):
            span = slice(head * TILE, head * TILE + TILE)
            qd[rows, span] = (low_half(turn(low_half(tile), *turning)) * 0.125).astype(BF16)

    spans = [slice(head * TILE, head * TILE + TILE) for head in range(3)]
    send_own, send_prior, receive, given = [], [], [], []
    for step in (1, 2, 3):
        behind = z + step <= 3
        send_own.append(either(behind, both(lower, both(z + step == 4, z <= 2))))
        send_prior.append(both(upper, z + step > 3))
        receive.append(either(upper, either(z - step >= 0, both(z == 0, step >= 2))))
        given.append((z - step + 4) % 4 + 4 * xhi * ((z - step + 4) // 4))
    head_span = lambda head: pl.ds(pl.multiple_of(head * TILE, TILE), TILE)
    across_at, along_at, return_at, relay_at, part_at, stat_at, dq_at, top_at = (
        net.take(count) for count in (3, 9, 9, 3, 3, 3, 3, 3)
    )

    def across(head):
        mine = kv.at[block, :, head_span(head)]
        return net.copy(mine, mine, net.at_x(2), across_at + head)

    def along(head, step):
        piece = kv.at[block - 4 * xhi * ((z + step + 1) // 4), :, head_span(head)]
        return net.copy(piece, piece, net.at_z(step + 1), along_at + 3 * head + step)

    @pl.loop(0, 3)
    def _(head):
        pl.when(lower)(across(head).start)
        for step in range(3):
            pl.when(send_own[step])(along(head, step).start)


    wait(gather_y)

    @pl.loop(0, 4)
    def _(index):
        rows = tile_at(index)
        cot[rows, :] = cot_t[:, rows].astype(F32).T.astype(BF16)

    out_sums = jnp.sum(cot_t[...].astype(F32), axis=1, keepdims=True)

    @pl.loop(0, 4)
    def _(index):
        rows = tile_at(index)
        d_heads = dot(cot[rows, :], w2[:, DENSE])
        pair, last = d_heads[:, 0:TILE], d_heads[:, TILE : 2 * TILE]
        for head, tile in enumerate((swap_halves(pair), pair, swap_halves(last))):
            qd[rows, spans[head]] = (qd[rows, spans[head]].astype(F32) + high_half(tile)).astype(BF16)

    lend = net.copy(qd, qd_in, net.pal())
    pl.when(helped)(lend.start)

    @pl.loop(0, 3)
    def _(head):
        pl.when(upper)(across(head).wait_recv)
        for step in range(3):
            pl.when(send_prior[step])(along(head, step).start)

    late.three()
    late.end()

    @pl.loop(0, 16)
    def _(pair):
        rows = pl.ds(pl.multiple_of(pair * 48, 16), 48)
        one = slots[2 * pair, :, EARLY:HALF].astype(F32)
        two = slots[2 * pair + 1, :, EARLY:HALF].astype(F32)
        w2[rows, FC1] = jnp.concatenate([one[0:24], two[0:24]], axis=0).astype(BF16)
        w2[rows, FC2] = jnp.concatenate([one[24:48], two[24:48]], axis=0).astype(BF16)

    srow[...] = jnp.zeros_like(srow)

    @pl.loop(0, 4)
    def _(index):
        rows = tile_at(index)
        hidden = dot(n2[rows, :], w2[:, FC1]) + bias[1:2, :]
        spread_to = 0.5 + 0.5 * lax.erf(hidden * (0.5**0.5))
        act[rows, :] = (hidden * spread_to).astype(BF16)
        slope = spread_to + hidden * jnp.exp(-0.5 * hidden * hidden) * 0.3989422804014327
        d_hidden = (slope * dot(cot[rows, :], w2[:, FC2])).astype(BF16)
        dhid[rows, :] = d_hidden
        d_norm = dot_nt(d_hidden, w2[:, FC1])
        normed = xhat[rows, :]
        dx2[rows, :] = norm_back(small[1:2, :] * d_norm, normed, rstd[rows, 0:1])
        srow[0:8, :] += fold(d_norm * normed)
        srow[8:16, :] += fold(d_norm)
        srow[16:24, :] += fold(d_hidden.astype(F32))

    for half in (0, 1):
        span = slice(half * 384, half * 384 + 384)
        mlp_t[span, :] = dot_nt(w2[span, FC2], act[...])
        gq[0:384, 0:WIDE] = dot_tn(n2[:, span], dhid[...])
        gq[384:768, 0:WIDE] = dot(cot_t[span, :], act[...])

        @pl.loop(0, 16)
        def _(index):
            first = pl.ds(pl.multiple_of(index * 24, 8), 24)
            second = pl.ds(pl.multiple_of(384 + index * 24, 8), 24)
            slots[half * 16 + index, :, EARLY:HALF] = jnp.concatenate(
                [gq[first, 0:WIDE], gq[second, 0:WIDE]], axis=0
            ).astype(BF16)

    fc_sum = Reduce(
        net, slots, EARLY, 896, HALF, twin_in, halves, late_a, late_b, late_sa, late_sb, late_ea, late_eb
    )
    fc_sum.one()

    row_is_low = lax.broadcasted_iota(jnp.int32, (TILE, ROWS), 0) < HD
    lent_count = (1 - xhi) * (3 - z)
    chunk_count = 4 + xhi

    def chunk_place(index):
        which = (lent_count + 7 - index) // 8
        return which, index - lent_count * (1 - which) + xhi * z

    def partial(head):
        return net.copy(part_out.at[head], part_in.at[head], net.pal(), part_at + head)

    def partial_top(head):
        return net.copy(part_top.at[head], part_top_in.at[head], net.pal(), top_at + head)

    def stat_copy(head):
        return net.copy(stat.at[0, head], stat.at[1, head], net.pal(), stat_at + head)

    def dq_copy(head):
        return net.copy(dq_out.at[head], dq_in.at[head], net.pal(), dq_at + head)

    def tops_of(which):
        total = jnp.broadcast_to(column_sum(totals[which]), (8, ROWS))
        return jnp.where(lax.broadcasted_iota(jnp.int32, (8, ROWS), 0) == 0, top[which], total)

    @pl.when(jnp.logical_not(helped))
    def _():
        part_in[...] = jnp.zeros_like(part_in)
        is_top = lax.broadcasted_iota(jnp.int32, (3, 8, ROWS), 1) == 0
        part_top_in[...] = jnp.where(is_top, -1e30, 0.0)
        dq_in[...] = jnp.zeros_like(dq_in)

    def ahead(head):
        span = head_span(head)
        pl.when(lower)(across(head).wait_send)
        for step in range(3):
            pl.when(receive[step])(along(head, step).wait_recv)

        def turn_queries(source, which):
            turned = source[:, span].astype(F32).T
            qdt[which * 3 + head] = turned.astype(BF16)
            query_t[which] = jnp.where(row_is_low, turned, 0.0).astype(BF16)

        turn_queries(qd, 0)
        top[...] = jnp.full_like(top, -1e30)
        totals[...] = jnp.zeros_like(totals)
        summed[...] = jnp.zeros_like(summed)

        @pl.loop(0, chunk_count)
        def _(turn_of):
            index = (turn_of + lent_count) % chunk_count

            @pl.when(both(helps, turn_of == chunk_count - lent_count))
            def _():
                pl.when(head == 0)(lend.wait_recv)
                turn_queries(qd_in, 1)

            which, at = chunk_place(index)
            chunk = head * 5 + index
            tile = kv[at, :, span]
            tile_t = tile.astype(F32).T.astype(BF16)
            kv_t[chunk] = tile_t
            key_shift = (at - block - which * (7 - 2 * block)) * ROWS
            parts = [slice(half * 256, half * 256 + 256) for half in (0, 1)]
            scores = [dot(tile, query_t[which, :, part]) for part in parts]
            before = [top[which, 0:1, part] for part in parts]
            old_total = [totals[which, :, part] for part in parts]
            old_sum = [summed[which, :, part] for part in parts]
            for half, part in enumerate(parts):
                score = scores[half]
                key_at = lax.broadcasted_iota(jnp.int32, score.shape, 0) + key_shift
                query_at = lax.broadcasted_iota(jnp.int32, score.shape, 1) + half * 256
                score = jnp.where(key_at <= query_at, score, -1e30)
                peak = jnp.maximum(before[half], jnp.max(score, axis=0, keepdims=True))
                weight = jnp.exp(score - peak)
                shrink = jnp.exp(before[half] - peak)
                rounded = weight.astype(BF16)
                weights[chunk, :, part] = rounded
                peaks = jnp.broadcast_to(peak, (8, 256))
                tops[chunk, :, part] = peaks
                top[which, :, part] = peaks
                totals[which, :, part] = old_total[half] * shrink + fold(weight)
                summed[which, :, part] = old_sum[half] * shrink + dot(tile_t, rounded)

            @pl.when(both(helps, turn_of == chunk_count - 1))
            def _():
                part_out[head] = summed[1, HD:TILE, :].astype(BF16)
                part_top[head] = tops_of(1)
                partial(head).start()
                partial_top(head).start()

        kept[head, 0:HD, :] = summed[0, HD:TILE, :]
        kept[head, HD : HD + 8, :] = tops_of(0)

    def merge(head):
        pl.when(helped)(partial(head).wait_recv)
        pl.when(helped)(partial_top(head).wait_recv)
        top_one, top_two = kept[head, HD : HD + 1, :], part_top_in[head, 0:1, :]
        peak = jnp.maximum(top_one, top_two)
        share_one, share_two = jnp.exp(top_one - peak), jnp.exp(top_two - peak)
        total = kept[head, HD + 1 : HD + 2, :] * share_one + part_top_in[head, 1:2, :] * share_two
        inverse = 1.0 / total
        result = (kept[head, 0:HD, :] * share_one + part_in[head].astype(F32) * share_two) * inverse
        delta = column_sum(qdt[head, HD:TILE, :].astype(F32) * result)
        kept[head, 0:HD, :] = result
        row = lax.broadcasted_iota(jnp.int32, (8, ROWS), 0)
        stat[0, head] = jnp.where(row == 0, peak, jnp.where(row == 1, inverse, delta))
        pl.when(helped)(stat_copy(head).start)

    def give_back(head, step):
        return net.copy(
            dkv.at[given[step], :, head_span(head)],
            from_z.at[step, :, head_span(head)],
            net.at_z(3 - step),
            return_at + 3 * head + step,
        )

    def relay_copy(head):
        return net.copy(to_x.at[:, head_span(head)], from_x.at[:, head_span(head)], net.at_x(2), relay_at + head)

    def relay(head):
        span = head_span(head)
        for step in range(3):
            pl.when(either(send_own[step], send_prior[step]))(give_back(head, step).wait_recv)

        @pl.when(upper)
        def _():
            total_kv[:, span] = dkv[z, :, span].astype(F32)
            for step in range(3):

                @pl.when(send_prior[step])
                def _():
                    total_kv[:, span] += from_z[step, :, span].astype(F32)

            to_x[:, span] = total_kv[:, span].astype(BF16)
            relay_copy(head).start()

    def back(head):
        span = head_span(head)
        query_n[0] = low_half(qd[:, span].astype(F32)).astype(BF16)

        @pl.when(helps)
        def _():
            query_n[1] = low_half(qd_in[:, span].astype(F32)).astype(BF16)

        summed[...] = jnp.zeros_like(summed)

        @pl.loop(0, chunk_count)
        def _(turn_of):
            index = (turn_of + lent_count) % chunk_count
            which, at = chunk_place(index)
            chunk = head * 5 + index
            pl.when(both(helps, turn_of == chunk_count - lent_count))(stat_copy(head).wait_recv)
            change = dkv[at, :, span].astype(F32)
            for half in (0, 1):
                part = slice(half * 256, half * 256 + 256)
                factor = jnp.exp(tops[chunk, 0:1, part] - stat[which, head, 0:1, part]) * stat[which, head, 1:2, part]
                weight = weights[chunk, :, part]
                scaled = jnp.where(
                    row_is_low[:, 0:256], 0.0, qdt[which * 3 + head, :, part].astype(F32) * factor
                )
                d_weight = dot(kv[at, :, span], scaled.astype(BF16))
                d_score = (
                    weight.astype(F32) * (d_weight - stat[which, head, 2:3, part] * factor)
                ).astype(BF16)
                change = change + dot(d_score, query_n[which, part, :]) + dot(weight, scaled.T.astype(BF16))
                summed[which, :, part] += dot(kv_t[chunk], d_score)
            dkv[at, :, span] = change.astype(BF16)

        dq_t[head] = summed[0, 0:HD, :]

        @pl.when(helps)
        def _():
            dq_out[head] = summed[1, 0:HD, :].astype(BF16)
            dq_copy(head).start()

        for step in range(3):
            pl.when(receive[step])(give_back(head, step).start)

    @pl.loop(0, 4)
    def _(index):
        pl.when(index < 3)(lambda: ahead(index))
        pl.when(index == 0)(fc_sum.two)
        pl.when(index == 3)(fc_sum.three)
        pl.when(index > 0)(lambda: back(index - 1))
        pl.when(index < 3)(lambda: merge(index))
        pl.when(index > 1)(lambda: relay(index - 2))

    heads[:, 0:TILE] = jnp.concatenate([kept[0, 0:HD, :], kept[1, 0:HD, :]], axis=0).T.astype(BF16)
    heads[:, TILE : 2 * TILE] = jnp.concatenate(
        [kept[2, 0:HD, :], jnp.zeros((HD, ROWS), F32)], axis=0
    ).T.astype(BF16)


    for half in (0, 1):
        span = slice(half * 384, half * 384 + 384)
        out_send[span, :] = (mlp_t[span, :] + dot_nt(w2[span, DENSE], heads[...])).astype(BF16)
        gq[span, DENSE] = dot(cot_t[span, :], heads[...])

    def part_of(number):
        return pl.ds(pl.multiple_of(number * PART, 16), PART)

    out_copies = [
        net.copy(out_send.at[part_of((y + step) % 4), :], out_recv.at[step - 1], net.at_y(step))
        for step in (1, 2, 3)
    ]
    start(out_copies)


    relay(2)

    @pl.loop(0, 3)
    def _(head):
        pl.when(helped)(dq_copy(head).wait_recv)
        pl.when(lower)(relay_copy(head).wait_recv)

    total_kv[...] = dkv[block].astype(F32)
    for step in range(3):

        @pl.when(send_own[step])
        def _():
            total_kv[...] += from_z[step].astype(F32)

    @pl.when(lower)
    def _():
        total_kv[...] += from_x[...].astype(F32)

    rowsum[...] = jnp.zeros_like(rowsum)

    @pl.loop(0, 4)
    def _(index):
        rows = tile_at(index)
        turning = (cosine[rows, :], -sine_up[rows, :], -sine_down[rows, :])
        pieces = [turn(total_kv[rows, spans[head]], *turning) for head in range(3)]
        query = []
        for head in range(3):
            grad = (dq_t[head, :, rows] + dq_in[head, :, rows].astype(F32)) * 0.125
            grad = jnp.concatenate([grad, jnp.zeros((HD, TILE), F32)], axis=0).T
            query.append(turn(grad, *turning))
        pieces.append(low_half(query[0]) + swap_halves(low_half(query[1])))
        pieces.append(low_half(query[2]))
        stacked = jnp.concatenate(pieces, axis=1).astype(BF16)
        dqkv[rows, :] = stacked
        d_norm = dot_nt(stacked, w2[:, QKV])
        normed = xhat[rows, :]
        d_input = dx2[rows, :] + norm_back(small[0:1, :] * d_norm, normed, rstd[rows, 0:1])
        rowsum[0:8, :] += fold(d_norm * normed)
        rowsum[8:16, :] += fold(d_norm)
        rowsum[16:24, 0:640] += fold(stacked.astype(F32))
        dx_send[:, rows] = d_input.T.astype(BF16)

    dx_copies = [
        net.copy(dx_send.at[part_of((y + step) % 4), :], dx_recv.at[step - 1], net.at_y(step))
        for step in (1, 2, 3)
    ]

    def whole(ref, at):
        return column_sum(ref[at : at + 8, :])

    y_send[...] = jnp.concatenate(
        [whole(rowsum, 0), whole(srow, 0), whole(rowsum, 8), whole(srow, 8), jnp.zeros((4, WIDE), F32)], axis=0
    )
    y_copies = [net.copy(y_send, y_recv.at[step - 1], net.at_y(step)) for step in (1, 2, 3)]
    start(y_copies + dx_copies)
    for half in (0, 1):
        span = slice(half * 384, half * 384 + 384)
        gq[span, QKV] = dot_tn(n1[:, span], dqkv[...])
    fc1_sum, qkv_total = whole(srow, 16), whole(rowsum, 16)
    pieces = []
    for number in range(12):
        pieces.append(fc1_sum[:, number // 2 * TILE : number // 2 * TILE + TILE])
    for number in (3, 3, 4, 0, 1, 2, 0, 1, 2):
        pieces.append(qkv_total[:, number * TILE : number * TILE + TILE])
    pieces.append(jnp.zeros((3, TILE), F32))
    bias_grads = jnp.concatenate(pieces, axis=0)
    row = lax.broadcasted_iota(jnp.int32, (24, TILE), 0)
    swapped = ((row < 12) & (row % 2 == 1)) | (row == 13) | (row >= 18)
    bias_rows[...] = jnp.where(swapped, swap_halves(bias_grads), bias_grads)
    wait(y_copies)
    shared = y_send[...] + y_recv[0] + y_recv[1] + y_recv[2]
    columns = jnp.concatenate(
        [
            jnp.zeros((SMALL, WIDE), F32),
            shared[0:4],
            jnp.zeros((2, WIDE), F32),
            jnp.zeros((58, WIDE), F32),
        ],
        axis=0,
    ).T
    lane = lanes((WIDE, TILE))
    columns = jnp.where((lane == SMALL + 4) | (lane == SMALL + 5), out_sums, columns)
    gq[:, 512:640] = jnp.where(lane < HD, gq[:, 512:640], columns)

    @pl.loop(0, 32)
    def _(index):
        rows = pl.ds(pl.multiple_of(index * 24, 8), 24)
        first = jnp.concatenate([gq[rows, 0:384], gq[rows, 640:768]], axis=1)
        second = jnp.concatenate([gq[rows, 384:640], gq[rows, 768:896], bias_rows[...]], axis=1)
        slots[index, :, 0:EARLY] = jnp.concatenate([first, second], axis=0).astype(BF16)

    qkv_sum = Reduce(
        net, slots, 0, 256, EARLY, twin_in, halves, early_a, early_b, early_sa, early_sb, early_ea, early_eb
    )
    qkv_sum.one()
    qkv_sum.two()

    wait(out_copies + dx_copies)
    mine = part_of(y)
    total = out_send[mine, :].astype(F32) + tok_t[mine, :].astype(F32) + out_col[mine, 0:1]
    grad = dx_send[mine, :].astype(F32) + cot_own[...].astype(F32)
    for step in range(3):
        total = total + out_recv[step].astype(F32)
        grad = grad + dx_recv[step].astype(F32)
    out_t[...] = total.astype(BF16)
    grad_t[...] = grad
    qkv_sum.three()

    @pl.loop(0, 3)
    def _(head):
        pl.when(helps)(partial(head).wait_send)
        pl.when(helps)(partial_top(head).wait_send)
        pl.when(helped)(stat_copy(head).wait_send)
        pl.when(helps)(dq_copy(head).wait_send)
        pl.when(upper)(relay_copy(head).wait_send)
        for step in range(3):
            pl.when(either(send_own[step], send_prior[step]))(along(head, step).wait_send)
            pl.when(receive[step])(give_back(head, step).wait_send)

    pl.when(helped)(lend.wait_send)
    fc_sum.end(final)
    qkv_sum.end(final)


def finish_kernel(
    out_in, grad_in, final, out_t, grad_t, gain, shift, qkv, qkv_small, dense, fc1, fc1_small, fc2, outs
):
    out_t[...] = out_in[...]
    grad_t[...] = grad_in[...]
    fc1[...] = final[0:24, EARLY:HALF]
    fc2[...] = final[24:48, EARLY:HALF]
    left = lanes((24, TILE)) < HD
    one, two, three = (final[0:24, head * TILE : head * TILE + TILE] for head in range(3))
    qkv[1, :, 0:TILE] = jnp.where(left, one, swap_halves(two))
    qkv[1, :, TILE:PART] = three[:, 0:HD]
    qkv[2, :, 0:TILE] = jnp.where(left, swap_halves(one), two)
    qkv[2, :, TILE:PART] = swap_halves(three)[:, 0:HD]
    qkv[0, :, 0:TILE] = final[24:48, 0:TILE]
    mixed = final[24:48, TILE : 2 * TILE]
    qkv[0, :, TILE:PART] = mixed[:, 0:HD]
    dense[:, 0:TILE] = final[0:24, 384:512]
    dense[:, TILE:PART] = final[24:48, 256 : 256 + HD]
    rows = jnp.concatenate([mixed, jnp.zeros((TILE - 24, TILE), F32)], axis=0).T
    gain[...] = rows[SMALL : SMALL + 2, 0:24]
    shift[...] = rows[SMALL + 2 : SMALL + 4, 0:24]
    outs[...] = rows[SMALL + 4 : SMALL + 6, 0:24]
    own = lax.axis_index("dp") * 8 + lax.axis_index("ctx")
    moved = pltpu.roll(final[24:48, 384:512], TILE - 2 * own, axis=1)
    rows = jnp.concatenate([moved, jnp.zeros((TILE - 24, TILE), F32)], axis=0).T
    fc1_small[...] = rows[0:2, 0:12]
    for which in range(3):
        qkv_small[which] = pltpu.roll(rows[0:8], TILE - 12 - 3 * which, axis=1)[0:2, 0:3]


def angle_tables():
    frequency = 10000.0 ** (-2.0 * np.arange(ROT // 2) / ROT)
    result = []
    for positions in (np.arange(ROWS), ROWS * np.arange(8)):
        phases = np.zeros((len(positions), TILE))
        phases[:, 0:ROT] = positions[:, None] * np.concatenate([frequency, frequency])[None, :]
        result.append(np.stack([np.cos(phases), np.sin(phases)]).astype(np.float32))
    return result


def call(kernel, name, shapes, scratch, collective, inputs, outside=()):
    options = dict(vmem_limit_bytes=VMEM_LIMIT)
    if collective is not None:
        options.update(collective_id=collective, has_side_effects=True)
    return pl.pallas_call(
        kernel,
        name=name,
        out_shape=[jax.ShapeDtypeStruct(shape, kind) for shape, kind in shapes],
        in_specs=[
            pl.BlockSpec(memory_space=pl.ANY if number in outside else pltpu.VMEM)
            for number in range(len(inputs))
        ],
        out_specs=[pl.BlockSpec(memory_space=pltpu.VMEM)] * len(shapes),
        scratch_shapes=scratch,
        compiler_params=pltpu.CompilerParams(**options),
    )(*inputs)


def shards(
    tokens,
    norm_gain,
    norm_bias,
    qkv_weight,
    qkv_bias,
    dense_weight,
    fc1_weight,
    fc1_bias,
    fc2_weight,
    out_bias,
    cotangent,
):
    vm = pltpu.VMEM
    dma = pltpu.SemaphoreType.DMA
    wide = (ROWS, WIDE)
    row_angles, block_angles = angle_tables()
    out_t, grad_t, final = call(
        layer_kernel,
        "layer",
        [((PART, ROWS), BF16), ((PART, ROWS), F32), ((48, HALF), F32)],
        [
            vm(wide, BF16),
            vm((3, 24, PART), BF16),
            vm((24, PART), BF16),
            vm((24, WIDE), BF16),
            vm((24, WIDE), BF16),
            vm((PART, ROWS), BF16),
            vm((2, ROWS, TILE), F32),
            dma((7,)),
            vm((32, 48, HALF), BF16),
            vm((WIDE, 2432), BF16),
            vm((16, WIDE), F32),
            vm((8, WIDE), F32),
            vm((TILE, TILE), F32),
            vm((4, 24, TILE), F32),
            vm((24, TILE), F32),
            vm((WIDE, TILE), F32),
            vm((ROWS, TILE), F32),
            vm((ROWS, TILE), F32),
            vm((ROWS, TILE), F32),
            vm(wide, F32),
            vm((ROWS, TILE), F32),
            vm((WIDE, ROWS), BF16),
            vm(wide, BF16),
            vm(wide, BF16),
            vm(wide, BF16),
            vm(wide, BF16),
            vm((WIDE, ROWS), BF16),
            vm(wide, BF16),
            vm((WIDE, ROWS), F32),
            vm(wide, F32),
            vm((24, WIDE), F32),
            vm((ROWS, 384), BF16),
            vm((ROWS, 384), BF16),
            vm((6, TILE, ROWS), BF16),
            vm((8, ROWS, 384), BF16),
            vm((8, ROWS, 384), BF16),
            vm((15, TILE, ROWS), BF16),
            vm((15, ROWS, ROWS), BF16),
            vm((15, 8, ROWS), F32),
            vm((2, 8, ROWS), F32),
            vm((2, 8, ROWS), F32),
            vm((2, TILE, ROWS), F32),
            vm((2, TILE, ROWS), BF16),
            vm((2, ROWS, TILE), BF16),
            vm((3, HD, ROWS), BF16),
            vm((3, HD, ROWS), BF16),
            vm((3, 8, ROWS), F32),
            vm((3, 8, ROWS), F32),
            vm((2, 3, 8, ROWS), F32),
            vm((3, HD, ROWS), BF16),
            vm((3, HD, ROWS), BF16),
            vm((3, HD, ROWS), F32),
            vm((3, 80, ROWS), F32),
            vm((WIDE, 896), F32),
            vm((16, 48, HALF), BF16),
            vm((16, 48, HALF), BF16),
            vm((3, 4, 48, 256), BF16),
            vm((3, 4, 48, 256), BF16),
            vm((4, 48, 256), BF16),
            vm((4, 48, 256), BF16),
            vm((3, 48, 256), BF16),
            vm((3, 48, 256), BF16),
            vm((3, 4, 48, 384), BF16),
            vm((3, 4, 48, 384), BF16),
            vm((4, 48, 384), BF16),
            vm((4, 48, 384), BF16),
            vm((3, 48, 384), BF16),
            vm((3, 48, 384), BF16),
            vm((3, ROWS, 384), BF16),
            vm((ROWS, 384), BF16),
            vm((ROWS, 384), BF16),
            vm((ROWS, 256), BF16),
            vm((WIDE, ROWS), BF16),
            vm((3, PART, ROWS), BF16),
            vm((WIDE, ROWS), BF16),
            vm((3, PART, ROWS), BF16),
            vm((24, WIDE), F32),
            vm((8, WIDE), F32),
            vm((3, 8, WIDE), F32),
            dma((192,)),
            dma((192,)),
        ],
        0,
        [
            tokens[0],
            norm_gain,
            norm_bias,
            out_bias,
            jnp.transpose(qkv_weight, (1, 0, 2)),
            jnp.transpose(qkv_bias, (0, 2, 1)),
            dense_weight.T,
            fc1_weight,
            fc1_bias.T,
            fc2_weight.T,
            cotangent[0].T,
            jnp.asarray(row_angles),
            jnp.asarray(block_angles),
        ],
        (0, 4, 6, 7, 9, 10, 11),
    )
    out_t, grad_t, gain, shift, qkv, qkv_small, dense, fc1, fc1_small, fc2, outs = call(
        finish_kernel,
        "finish",
        [
            ((PART, ROWS), BF16),
            ((PART, ROWS), F32),
            ((2, 24), F32),
            ((2, 24), F32),
            ((3, 24, PART), F32),
            ((3, 2, 3), F32),
            ((24, PART), F32),
            ((24, WIDE), F32),
            ((2, 12), F32),
            ((24, WIDE), F32),
            ((2, 24), F32),
        ],
        [],
        None,
        [out_t, grad_t, final],
    )
    return (
        out_t.T[None],
        grad_t.T[None],
        gain,
        shift,
        jnp.transpose(qkv, (1, 0, 2)),
        jnp.transpose(qkv_small, (0, 2, 1)),
        dense.T,
        fc1,
        fc1_small.T,
        fc2.T,
        outs,
    )


def solution(mesh):
    return jax.shard_map(
        shards,
        mesh=mesh,
        in_specs=(
            P("dp", "ctx", None),
            P(None, ("dp", "ctx")),
            P(None, ("dp", "ctx")),
            P(("dp", "ctx"), None, "tensor"),
            P(None, "tensor", ("dp", "ctx")),
            P("tensor", ("dp", "ctx")),
            P(("dp", "ctx"), "tensor"),
            P("tensor", ("dp", "ctx")),
            P("tensor", ("dp", "ctx")),
            P(None, ("dp", "ctx")),
            P("dp", "ctx", "tensor"),
        ),
        out_specs=(
            P("dp", "ctx", "tensor"),
            P("dp", "ctx", "tensor"),
            P(None, ("dp", "ctx")),
            P(None, ("dp", "ctx")),
            P(("dp", "ctx"), None, "tensor"),
            P(None, "tensor", ("dp", "ctx")),
            P("tensor", ("dp", "ctx")),
            P(("dp", "ctx"), "tensor"),
            P("tensor", ("dp", "ctx")),
            P("tensor", ("dp", "ctx")),
            P(None, ("dp", "ctx")),
        ),
        check_vma=False,
    )
```
